32 devices in a mesh: node: 8 (over z, x), edge: 4 (over y, core).
Axes of the slice: x: 2, y: 2, z: 4, core: 2. Of those that a mesh axis runs over, the one named last changes fastest.
Arguments:
- teleport: float32 [16384, 128], P(('node', 'edge')), may hold values from -6 to 6
- cotangent: float32 [16384, 128], P(('node', 'edge')), may hold values from -6 to 6
- fetch_table: int32 [8, 16], replicated, may hold values from -1 to 7, as said below
- block_row: int32 [8, 192], P('node'), may hold values from 0 to 7
- block_slot: int32 [8, 192], P('node'), may hold values from 0 to 15, as said below
- values: bfloat16 [8, 192, 256, 256], P('node', None, 'edge'), may hold values from -0.078125 to 0.078125
Outputs:
- propagated: float32 [16384, 128], P(('node', 'edge'))
- teleport_grad: float32 [16384, 128], P(('node', 'edge'))
The draws below stay inside these ranges and needn't reach their ends.
Inputs may be any that keep to these rules, and one draw needn't show every extreme that they name: `fetch_table`: entry n, o * 2 + k names a node block index j of owner group o that group n reads in slot k, or is -1 for an empty slot. Within the 2 slots of one owner the live ones come first and name distinct blocks. One owner group has all 2 slots live in every row. `block_slot`: every entry names a live slot of the group's row of fetch_table, and every live slot of that row is named by at least one adjacency block of the group.
All inputs are finite; a program needn't handle non-finite values.
Results may differ from the reference program's by a relative error of at most 0.004.
Values may be sent and summed in bfloat16 or wider, within the bound.
No kernel may reach another device: no remote copies, remote signals or barrier semaphores. Data moves between devices by JAX's collectives and lax.ppermute only.
A program may use at most 128 MiB of HBM per device.

```python
import jax
import jax.numpy as jnp
from jax import lax

HID = 128
BS = 256
CAP = 2
STEPS = 2
NB_DEV = 8
EB = 192
QUARTER = 64
NODES = 16384
N_NODE = 8
N_EDGE = 4


def fetch_plan(key):
    busiest = jax.random.randint(jax.random.fold_in(key, 11), (), 0, N_NODE)
    appeal = jax.random.randint(jax.random.fold_in(key, 12), (N_NODE,), 0, 4)
    jitter = jax.random.randint(jax.random.fold_in(key, 13), (N_NODE, N_NODE), 0, 3)
    live_count = jnp.clip(jitter + appeal[None, :] - 1, 0, CAP)
    owners = jnp.arange(N_NODE, dtype=jnp.int32)
    live_count = jnp.where(owners[None, :] == busiest, CAP, live_count)
    scores = jax.random.randint(jax.random.fold_in(key, 14), (N_NODE, N_NODE, NB_DEV), 0, 2 ** 20)
    scores = scores * NB_DEV + jnp.arange(NB_DEV, dtype=jnp.int32)[None, None, :]
    picked = jnp.argsort(scores, axis=-1)[:, :, :CAP].astype(jnp.int32)
    in_use = jnp.arange(CAP, dtype=jnp.int32)[None, None, :] < live_count[:, :, None]
    return jnp.where(in_use, picked, -1).reshape(N_NODE, N_NODE * CAP).astype(jnp.int32)


def draw_fetch_table(key, part):
    return fetch_plan(key)


def draw_block_slot(key, part):
    table = fetch_plan(key)
    slot_total = N_NODE * CAP
    live_mask = table >= 0
    slot_range = jnp.arange(slot_total, dtype=jnp.int32)[None, :]
    order_key = jnp.where(live_mask, 0, slot_total) + slot_range
    live_order = jnp.argsort(order_key, axis=1).astype(jnp.int32)
    live_total = jnp.sum(live_mask.astype(jnp.int32), axis=1)
    positions = jnp.arange(EB, dtype=jnp.int32)[None, :]
    spread = jax.random.randint(jax.random.fold_in(key, 21), (N_NODE, EB), 0, live_total[:, None])
    chosen_pos = jnp.where(positions < live_total[:, None], positions, spread)
    chosen = jnp.take_along_axis(live_order, chosen_pos, axis=1)
    mixing = jax.random.randint(jax.random.fold_in(key, 22), (N_NODE, EB), 0, 2 ** 20) * EB + positions
    shuffle = jnp.argsort(mixing, axis=1)
    return jnp.take_along_axis(chosen, shuffle, axis=1).astype(jnp.int32)


def with_ends(values, key, low, high):
    place = [jax.random.randint(jax.random.fold_in(key, axis), (), 0, length) for axis, length in enumerate(values.shape)]
    main_axis = values.shape.index(max(values.shape))
    next_to = place[:main_axis] + [(place[main_axis] + 1) % values.shape[main_axis]] + place[main_axis + 1:]
    return values.at[tuple(place)].set(low).at[tuple(next_to)].set(high)


def steps_of(own_key, extent, cuts, smallest, largest):
    def one(dim, blocks):
        heights = jax.random.uniform(jax.random.fold_in(jax.random.fold_in(own_key, 6), dim), (blocks,), jnp.float32, smallest / len(cuts), largest / len(cuts))
        return jnp.repeat(jnp.exp(heights), extent[dim] // blocks).reshape((-1,) + (1,) * (len(extent) - dim - 1))

    gain = one(*cuts[0])
    for cut in cuts[1:]:
        gain = gain * one(*cut)
    return gain


def gaussian(rng, dims, scale, bound, cuts=(), held_as=jnp.bfloat16):
    level = steps_of(rng, dims, cuts, -0.22, 0.18) if cuts else 1.0
    drawn = jax.random.normal(rng, dims, jnp.float32) * scale * level
    return jnp.minimum(jnp.maximum(drawn, -bound), bound).astype(held_as)


def setup_inputs(seed: int = 0) -> dict:
    key_of = jax.random.split(jax.random.key(seed), 7)
    return {
        "teleport": gaussian(key_of[0], (NODES, HID), 1.0, 6.0, ((0, 32),), jnp.float32),
        "cotangent": gaussian(key_of[1], (NODES, HID), 1.0, 6.0, ((0, 32),), jnp.float32),
        "fetch_table": draw_fetch_table(jax.random.fold_in(key_of[6], 71), 0),
        "block_row": with_ends(jax.random.randint(key_of[3], (N_NODE, EB), 0, NB_DEV), jax.random.fold_in(key_of[3], 1), 0, NB_DEV - 1).astype(jnp.int32),
        "block_slot": draw_block_slot(jax.random.fold_in(key_of[6], 71), 0),
        "values": gaussian(key_of[5], (N_NODE, EB, BS, BS), (BS * EB // NB_DEV) ** -0.5, 0.078125, ((0, 8), (2, 4))),
    }


def node_blocks(array):
    arranged = array.reshape(N_NODE, N_EDGE, NB_DEV, QUARTER, HID).transpose(0, 2, 1, 3, 4)
    return arranged.reshape(N_NODE * NB_DEV, BS, HID)


def node_order(blocks):
    arranged = blocks.reshape(N_NODE, NB_DEV, N_EDGE, QUARTER, HID).transpose(0, 2, 1, 3, 4)
    return arranged.reshape(NODES, HID)


def forward_apply(rounded, values, block_row, column_ids):
    def one_group(inputs):
        weights, row_ids, targets = inputs
        gathered = jnp.take(rounded, targets, axis=0).astype(jnp.float32)
        product = jnp.einsum("bcr,bch->brh", weights.astype(jnp.float32), gathered, precision=lax.Precision.HIGHEST)
        return jnp.zeros((NB_DEV, BS, HID), jnp.float32).at[row_ids].add(product)

    result = lax.map(one_group, (values, block_row, column_ids))
    return result.reshape(N_NODE * NB_DEV, BS, HID)


def transpose_apply(rounded, values, block_row, column_ids):
    def one_group(running, inputs):
        group_id, weights, row_ids, targets = inputs
        sources = jnp.take(rounded, group_id * NB_DEV + row_ids, axis=0).astype(jnp.float32)
        product = jnp.einsum("bcr,brh->bch", weights.astype(jnp.float32), sources, precision=lax.Precision.HIGHEST)
        return running.at[targets].add(product), None

    start_sum = jnp.zeros((N_NODE * NB_DEV, BS, HID), jnp.float32)
    group_ids = jnp.arange(N_NODE, dtype=jnp.int32)
    result, _ = lax.scan(one_group, start_sum, (group_ids, values, block_row, column_ids))
    return result


def reference(teleport, cotangent, fetch_table, block_row, block_slot, values):
    owner_part = (block_slot // CAP).astype(jnp.int32)
    local_part = jnp.take_along_axis(fetch_table, block_slot, axis=1).astype(jnp.int32)
    column_ids = (owner_part * NB_DEV + local_part).astype(jnp.int32)
    base = node_blocks(teleport)
    current = base
    for step_index in range(STEPS):
        rounded = current.astype(jnp.bfloat16)
        current = 0.9 * forward_apply(rounded, values, block_row, column_ids) + 0.1 * base
    adjoint = node_blocks(cotangent)
    gradient = 0.1 * adjoint
    for step_index in range(STEPS):
        rounded = adjoint.astype(jnp.bfloat16)
        adjoint = 0.9 * transpose_apply(rounded, values, block_row, column_ids)
        factor = 0.1 if step_index + 1 < STEPS else 1.0
        gradient = gradient + factor * adjoint
    return node_order(current), node_order(gradient)
```

```python
import jax
import jax.numpy as jnp
from jax import lax
from jax.experimental import pallas as pl
from jax.experimental.pallas import tpu as pltpu
from jax.sharding import PartitionSpec as P

CAP = 2
STEPS = 2
DENSE_BYTES = 8 * 2**20
VMEM_LIMIT = 48 * 2**20
LOW = jnp.bfloat16
FULL = jnp.float32

VMEM = pl.BlockSpec(memory_space=pltpu.VMEM)
SMEM = pl.BlockSpec(memory_space=pltpu.SMEM)
PARAMS = pltpu.CompilerParams(vmem_limit_bytes=VMEM_LIMIT)


def requested(table, slot):
    column = lax.axis_index("node") * CAP + slot % CAP
    return jnp.maximum(table[slot // CAP, column], 0)


def start_kernel(table, teleport, cotangent, send, rounded):
    rounded[...] = cotangent[...].astype(LOW)
    for slot in range(send.shape[0]):
        send[slot] = teleport[requested(table, slot)].astype(LOW)


def build_kernel(rows, slots, weights, dense, total):
    step = pl.program_id(0)
    chunk, quarter, width = weights.shape[1:]

    @pl.when(step == 0)
    def _():
        total[...] = jnp.zeros_like(total)

    for index in range(chunk):
        block = step * chunk + index
        total[slots[0, block], rows[0, block]] += weights[0, index].astype(FULL)

    @pl.when(step == pl.num_programs(0) - 1)
    def _():
        for slot in range(total.shape[0]):
            for row in range(total.shape[1]):
                dense[pl.ds(slot * quarter, quarter), pl.ds(row * width, width)] = total[
                    slot, row
                ].astype(LOW)


def forward_kernel(columns, dense, partial):
    quarters, count, quarter, hidden = partial.shape
    width = quarters * quarter
    source = columns[...].reshape(-1, hidden)
    for row in range(count):
        product = lax.dot_general(
            source,
            dense[:, row * width : (row + 1) * width],
            (((0,), (0,)), ((), ())),
            preferred_element_type=FULL,
        ).T.astype(LOW)
        for part in range(quarters):
            partial[part, row] = product[part * quarter : (part + 1) * quarter]


def adjoint_kernel(dense, *refs):
    *arrived, send, source = refs
    count, quarters, quarter, hidden = source.shape
    edge = lax.axis_index("edge")
    for turn in range(quarters):
        source[:, lax.rem(edge + turn, quarters)] = arrived[turn][...]
    product = jnp.dot(
        dense[...],
        source[...].reshape(count * quarters * quarter, hidden),
        preferred_element_type=FULL,
    )
    send[...] = product.reshape(send.shape).astype(LOW)


def state_of(arrived, teleport):
    summed = arrived[0].astype(FULL)
    for part in range(1, arrived.shape[0]):
        summed += arrived[part].astype(FULL)
    return 0.9 * summed + 0.1 * teleport[...]


def next_state_kernel(table, arrived, teleport, send, state):
    state[...] = state_of(arrived, teleport).astype(LOW)
    for slot in range(send.shape[0]):
        send[slot] = state[requested(table, slot)]


def last_state_kernel(arrived, teleport, state):
    state[...] = state_of(arrived, teleport)


def gather_adjoint(table, arrived, summed):
    summed[...] = jnp.zeros_like(summed)
    for slot in range(arrived.shape[0]):
        summed[requested(table, slot)] += arrived[slot].astype(FULL)


def next_adjoint_kernel(table, arrived, gradient_in, gradient, rounded, summed):
    gather_adjoint(table, arrived, summed)
    adjoint = 0.9 * summed[...]
    gradient[...] = gradient_in[...] * 0.1 + 0.1 * adjoint
    rounded[...] = adjoint.astype(LOW)


def last_adjoint_kernel(table, arrived, gradient_in, gradient, summed):
    gather_adjoint(table, arrived, summed)
    gradient[...] = gradient_in[...] + 0.9 * summed[...]


def per_device_dense(teleport, cotangent, fetch_table, block_row, block_slot, values):
    row_count, hidden = teleport.shape
    _, block_count, quarter, width = values.shape
    count = row_count // quarter
    slot_total = fetch_table.shape[1]
    quarters = lax.axis_size("edge")
    shape = (count, quarter, hidden)
    slot_shape = (slot_total, quarter, hidden)
    teleport = teleport.reshape(shape)
    cotangent = cotangent.reshape(shape)

    def call(kernel, outs, memories, scratch=()):
        return pl.pallas_call(
            kernel,
            out_shape=[jax.ShapeDtypeStruct(*out) for out in outs],
            in_specs=memories,
            out_specs=[VMEM] * len(outs),
            scratch_shapes=list(scratch),
            compiler_params=PARAMS,
        )

    send, rounded = call(start_kernel, [(slot_shape, LOW), (shape, LOW)], [SMEM, VMEM, VMEM])(
        fetch_table, teleport, cotangent
    )
    chunk = next(size for size in (16, 8, 4, 2, 1) if block_count % size == 0)
    dense_shape = (slot_total * quarter, count * width)
    dense = pl.pallas_call(
        build_kernel,
        out_shape=jax.ShapeDtypeStruct(dense_shape, LOW),
        grid=(block_count // chunk,),
        in_specs=[SMEM, SMEM, pl.BlockSpec((1, chunk, quarter, width), lambda i: (0, i, 0, 0))],
        out_specs=pl.BlockSpec(dense_shape, lambda i: (0, 0)),
        scratch_shapes=[pltpu.VMEM((slot_total, count, quarter, width), FULL)],
        compiler_params=PARAMS,
        cost_estimate=pl.CostEstimate(
            flops=values.size, bytes_accessed=values.size * 4, transcendentals=0
        ),
    )(block_row, block_slot, values)

    cost = pl.CostEstimate(
        flops=2 * dense.size * hidden, bytes_accessed=dense.size * 2, transcendentals=0
    )
    forward = pl.pallas_call(
        forward_kernel,
        out_shape=jax.ShapeDtypeStruct((quarters,) + shape, LOW),
        in_specs=[VMEM, VMEM],
        out_specs=VMEM,
        compiler_params=PARAMS,
        cost_estimate=cost,
    )
    backward = pl.pallas_call(
        adjoint_kernel,
        out_shape=jax.ShapeDtypeStruct(slot_shape, LOW),
        in_specs=[VMEM] * (1 + quarters),
        out_specs=VMEM,
        scratch_shapes=[pltpu.VMEM((count, quarters, quarter, hidden), LOW)],
        compiler_params=PARAMS,
        cost_estimate=cost,
    )

    def from_edge(array, turn):
        pairs = [((target + turn) % quarters, target) for target in range(quarters)]
        return lax.ppermute(array, "edge", pairs)

    gradient = cotangent
    for step in range(STEPS):
        last = step + 1 == STEPS
        columns = lax.all_to_all(send, "node", 0, 0, tiled=True)
        arrived = [rounded] + [from_edge(rounded, turn) for turn in range(1, quarters)]
        partial = forward(columns, dense)
        transposed = backward(dense, *arrived)
        partial = lax.all_to_all(partial, "edge", 0, 0, tiled=True)
        transposed = lax.all_to_all(transposed, "node", 0, 0, tiled=True)
        total = pltpu.VMEM(shape, FULL)
        if not last:
            (send,) = call(
                next_state_kernel,
                [(slot_shape, LOW)],
                [SMEM, VMEM, VMEM],
                [pltpu.VMEM(shape, LOW)],
            )(fetch_table, partial, teleport)
            gradient, rounded = call(
                next_adjoint_kernel,
                [(shape, FULL), (shape, LOW)],
                [SMEM, VMEM, VMEM],
                [total],
            )(fetch_table, transposed, gradient)
        else:
            (state,) = call(last_state_kernel, [(shape, FULL)], [VMEM, VMEM])(partial, teleport)
            (gradient,) = call(
                last_adjoint_kernel, [(shape, FULL)], [SMEM, VMEM, VMEM], [total]
            )(fetch_table, transposed, gradient)
    return state.reshape(row_count, hidden), gradient.reshape(row_count, hidden)


def per_device_blocks(teleport, cotangent, fetch_table, block_row, block_slot, values):
    row_count, hidden = teleport.shape
    quarter = values.shape[2]
    block_count = values.shape[1]
    blocks_dev = row_count // quarter
    slot_total = fetch_table.shape[1]
    owner_count = lax.axis_size("node")
    group_size = 16
    turn_count = block_count // group_size
    owner_index = lax.axis_index("node")
    local_weights = values[0]
    row_ids = block_row[0]
    slot_ids = block_slot[0]
    own_plan = lax.dynamic_index_in_dim(fetch_table, owner_index, 0, keepdims=False)
    local_ids = jnp.take(own_plan, slot_ids, axis=0)
    global_ids = slot_ids // CAP * blocks_dev + local_ids
    requests = lax.dynamic_slice_in_dim(fetch_table, owner_index * CAP, CAP, 1).reshape(slot_total)
    block_range = jnp.arange(blocks_dev, dtype=jnp.int32)
    request_hot = requests[:, None] == block_range[None, :]
    request_float = request_hot.astype(jnp.float32)
    weight_groups = local_weights.reshape(turn_count, group_size, quarter, local_weights.shape[2])
    row_groups = row_ids.reshape(turn_count, group_size)
    slot_groups = slot_ids.reshape(turn_count, group_size)
    current = teleport
    for step_index in range(STEPS):
        propagate_rounded = current.astype(jnp.bfloat16)
        everything = lax.all_gather(propagate_rounded, "node", axis=0, tiled=True)
        feature_table = everything.reshape(owner_count * blocks_dev, quarter, hidden)
        columns = jnp.take(feature_table, global_ids, axis=0)
        column_groups = columns.reshape(turn_count, group_size, quarter, hidden)

        def partial_rows(amount):
            quarters_used = amount // row_count

            def partial_advance(running, inputs):
                weights, sources, targets = inputs
                product = jnp.einsum(
                    "bcr,bch->brh", weights, sources, preferred_element_type=jnp.float32
                )
                product = product.reshape(group_size, quarters_used, quarter, hidden)
                return (running.at[targets].add(product), None)

            start_sum = jnp.zeros((blocks_dev, quarters_used, quarter, hidden), jnp.float32)
            running, _ = lax.scan(
                partial_advance, start_sum, (weight_groups, column_groups, row_groups)
            )
            return running.transpose(1, 0, 2, 3).reshape(amount, hidden)

        current = (
            0.9
            * lax.psum_scatter(
                partial_rows(lax.axis_size("edge") * row_count),
                "edge",
                scatter_dimension=0,
                tiled=True,
            )
            + 0.1 * teleport
        )
    adjoint = cotangent
    gradient = 0.1 * cotangent
    for step_index in range(STEPS):
        rounded = adjoint.astype(jnp.bfloat16).reshape(blocks_dev, quarter, hidden)

        def fold_rows(running, arrived_rows):

            def fold_advance(carried, inputs):
                weights, targets, slot_targets = inputs
                sources = jnp.take(arrived_rows, targets, axis=0)
                product = jnp.einsum(
                    "bcr,brh->bch", weights, sources, preferred_element_type=jnp.float32
                )
                return (carried.at[slot_targets].add(product), None)

            carried, _ = lax.scan(fold_advance, running, (weight_groups, row_groups, slot_groups))
            return carried

        transpose_start_sum = jnp.zeros((slot_total, quarter, hidden), jnp.float32)
        partial_value = fold_rows(
            transpose_start_sum, lax.all_gather(rounded, "edge", axis=1, tiled=True)
        )
        summed = jnp.einsum(
            "sj,sch->jch",
            request_float,
            lax.all_to_all(partial_value, "node", split_axis=0, concat_axis=0, tiled=True),
            precision=lax.Precision.HIGHEST,
        )
        adjoint = 0.9 * summed.reshape(row_count, hidden)
        factor = 0.1 if step_index + 1 < STEPS else 1.0
        gradient = gradient + factor * adjoint
    return (current, gradient)


def per_device(teleport, cotangent, fetch_table, block_row, block_slot, values):
    arguments = (teleport, cotangent, fetch_table, block_row, block_slot, values)
    row_count = teleport.shape[0]
    dense_bytes = fetch_table.shape[1] * row_count * values.shape[3] * 2
    if dense_bytes <= DENSE_BYTES:
        return per_device_dense(*arguments)
    return per_device_blocks(*arguments)


def solution(mesh):
    placed = (
        P(("node", "edge"), None),
        P(("node", "edge"), None),
        P(),
        P("node", None),
        P("node", None),
        P("node", None, "edge", None),
    )
    return jax.shard_map(
        per_device,
        mesh=mesh,
        in_specs=placed,
        out_specs=(P(("node", "edge"), None), P(("node", "edge"), None)),
        check_vma=False,
    )
```

```python
import functools

import jax
import jax.numpy as jnp
from jax import lax
from jax.experimental import pallas as pl
from jax.experimental.pallas import tpu as pltpu
from jax.sharding import PartitionSpec as P

CAP = 2
STEPS = 2
DENSE_BYTES = 8 * 2**20
LOW = jnp.bfloat16
FULL = jnp.float32

VMEM = pl.BlockSpec(memory_space=pltpu.VMEM)
SMEM = pl.BlockSpec(memory_space=pltpu.SMEM)
HBM = pl.BlockSpec(memory_space=pltpu.HBM)


def params(mebibytes):
    return pltpu.CompilerParams(vmem_limit_bytes=mebibytes * 2**20)


def partner(axis, turn):
    return lax.axis_index(axis) ^ turn


def requested(table, reader, slot):
    return jnp.maximum(table[reader, lax.axis_index("node") * CAP + slot], 0)


def start_kernel(table, teleport, cotangent, *refs):
    *sends, rounded, plan, state, adjoint, sems = refs
    copies = [
        pltpu.make_async_copy(source, target, sems.at[index])
        for index, (source, target) in enumerate(
            ((table, plan), (teleport, state), (cotangent, adjoint))
        )
    ]
    for copy in copies:
        copy.start()
    copies[0].wait()
    copies[1].wait()
    for turn, send in enumerate(sends):
        for slot in range(CAP):
            send[slot] = state[requested(plan, partner("node", turn), slot)].astype(LOW)
    copies[2].wait()
    rounded[...] = adjoint[...].astype(LOW)


def build_kernel(rows, slots, weights, high, low, held, total, sems):
    parts = sems.shape[0]
    block_count, quarter, width = held.shape
    chunk = block_count // parts
    copies = [
        pltpu.make_async_copy(
            weights.at[0, pl.ds(part * chunk, chunk)],
            held.at[pl.ds(part * chunk, chunk)],
            sems.at[part],
        )
        for part in range(parts)
    ]
    for copy in copies:
        copy.start()
    total[...] = jnp.zeros_like(total)
    for part, copy in enumerate(copies):
        copy.wait()
        for block in range(part * chunk, (part + 1) * chunk):
            total[slots[0, block], rows[0, block]] += held[block].astype(FULL)
    for slot in range(total.shape[0]):
        for row in range(total.shape[1]):
            place = (pl.ds(slot * quarter, quarter), pl.ds(row * width, width))
            value = total[slot, row]
            rounded = value.astype(LOW)
            high[place] = rounded
            low[place] = (value - rounded.astype(FULL)).astype(LOW)


def forward_kernel(owners, operators, *refs):
    columns = refs[:owners]
    dense = refs[owners : owners + operators]
    *partials, source, product = refs[owners + operators :]
    quarters, quarter, hidden = product.shape
    width = quarters * quarter
    for turn in range(owners):
        source[partner("node", turn)] = columns[turn][...]
    vectors = source[...].reshape(-1, hidden)
    for row in range(partials[0].shape[0]):
        summed = sum(
            lax.dot_general(
                vectors,
                part[:, row * width : (row + 1) * width],
                (((0,), (0,)), ((), ())),
                preferred_element_type=FULL,
            )
            for part in dense
        )
        product[...] = summed.T.reshape(product.shape)
        for turn, partial in enumerate(partials):
            partial[row] = product[partner("edge", turn)].astype(partial.dtype)


def adjoint_kernel(owners, operators, *refs):
    quarters = len(refs) - operators - owners - 2
    arrived = refs[:quarters]
    dense = refs[quarters : quarters + operators]
    *sends, source, product = refs[quarters + operators :]
    for turn in range(quarters):
        source[:, partner("edge", turn)] = arrived[turn][...]
    vectors = source[...].reshape(-1, source.shape[-1])
    product[...] = sum(
        jnp.dot(part[...], vectors, preferred_element_type=FULL) for part in dense
    ).reshape(product.shape)
    for turn, send in enumerate(sends):
        send[...] = product[partner("node", turn)].astype(send.dtype)


def state_of(arrived, teleport):
    summed = arrived[0][...]
    for part in arrived[1:]:
        summed += part[...].astype(FULL)
    return 0.9 * summed + 0.1 * teleport[...]


def next_state_kernel(quarters, table, teleport, *refs):
    arrived = refs[:quarters]
    *sends, state = refs[quarters:]
    state[...] = state_of(arrived, teleport)
    for turn, send in enumerate(sends):
        for slot in range(CAP):
            send[slot] = state[requested(table, partner("node", turn), slot)].astype(LOW)


def last_state_kernel(teleport, *refs):
    *arrived, state = refs
    state[...] = state_of(arrived, teleport)


def gather_adjoint(table, arrived, summed):
    summed[...] = jnp.zeros_like(summed)
    for turn, part in enumerate(arrived):
        for slot in range(CAP):
            own = requested(table, partner("node", turn), slot)
            summed[own] += part[slot].astype(FULL)


def next_adjoint_kernel(table, cotangent, *refs):
    *arrived, gradient, rounded, summed = refs
    gather_adjoint(table, arrived, summed)
    adjoint = 0.9 * summed[...]
    gradient[...] = 0.1 * cotangent[...] + 0.1 * adjoint
    rounded[...] = adjoint.astype(LOW)


def last_adjoint_kernel(table, gradient_in, *refs):
    *arrived, gradient, summed = refs
    gather_adjoint(table, arrived, summed)
    gradient[...] = gradient_in[...] + 0.9 * summed[...]


def per_device_dense(teleport, cotangent, fetch_table, block_row, block_slot, values):
    row_count, hidden = teleport.shape
    _, block_count, quarter, width = values.shape
    count = row_count // quarter
    quarters = lax.axis_size("edge")
    owners = lax.axis_size("node")
    shape = (count, quarter, hidden)
    pair_shape = (CAP, quarter, hidden)
    slot_total = owners * CAP
    teleport = teleport.reshape(shape)
    cotangent = cotangent.reshape(shape)

    def call(kernel, operands, places, outs, scratch, mebibytes=8, cost=None):
        return pl.pallas_call(
            kernel,
            out_shape=[jax.ShapeDtypeStruct(*out) for out in outs],
            in_specs=places,
            out_specs=[VMEM] * len(outs),
            scratch_shapes=scratch,
            compiler_params=params(mebibytes),
            cost_estimate=cost,
        )(*operands)

    def exchange(arrays, axis):
        size = lax.axis_size(axis)
        return [arrays[0]] + [
            lax.ppermute(arrays[turn], axis, [(place, place ^ turn) for place in range(size)])
            for turn in range(1, size)
        ]

    *sends, rounded = call(
        start_kernel,
        (fetch_table, teleport, cotangent),
        [HBM] * 3,
        [(pair_shape, LOW)] * owners + [(shape, LOW)],
        [
            pltpu.SMEM(fetch_table.shape, fetch_table.dtype),
            pltpu.VMEM(shape, FULL),
            pltpu.VMEM(shape, FULL),
            pltpu.SemaphoreType.DMA((3,)),
        ],
    )
    dense_shape = (slot_total * quarter, count * width)
    parts = next(size for size in (12, 8, 4, 2, 1) if block_count % size == 0)
    high, low = call(
        build_kernel,
        (block_row, block_slot, values),
        [SMEM, SMEM, HBM],
        [(dense_shape, LOW)] * 2,
        [
            pltpu.VMEM((block_count, quarter, width), LOW),
            pltpu.VMEM((slot_total, count, quarter, width), FULL),
            pltpu.SemaphoreType.DMA((parts,)),
        ],
        28,
        pl.CostEstimate(flops=0, bytes_accessed=values.size * 2, transcendentals=0),
    )

    gradient = cotangent
    for step in range(STEPS):
        last = step + 1 == STEPS
        dense = (high,) if last else (high, low)
        cost = pl.CostEstimate(
            flops=2 * len(dense) * high.size * hidden,
            bytes_accessed=len(dense) * high.size * 2,
            transcendentals=0,
        )
        columns = exchange(sends, "node")
        arrived = exchange([rounded] * quarters, "edge")
        partials = call(
            functools.partial(forward_kernel, owners, len(dense)),
            (*columns, *dense),
            [VMEM] * (owners + len(dense)),
            [(shape, FULL)] + [(shape, LOW)] * (quarters - 1),
            [
                pltpu.VMEM((owners,) + pair_shape, LOW),
                pltpu.VMEM((quarters, quarter, hidden), FULL),
            ],
            cost=cost,
        )
        transposed = call(
            functools.partial(adjoint_kernel, owners, len(dense)),
            (*arrived, *dense),
            [VMEM] * (quarters + len(dense)),
            [(pair_shape, FULL)] + [(pair_shape, LOW)] * (owners - 1),
            [
                pltpu.VMEM((count, quarters, quarter, hidden), LOW),
                pltpu.VMEM((owners,) + pair_shape, FULL),
            ],
            cost=cost,
        )
        partials = exchange(partials, "edge")
        transposed = exchange(transposed, "node")
        total = [pltpu.VMEM(shape, FULL)]
        if not last:
            sends = call(
                functools.partial(next_state_kernel, quarters),
                (fetch_table, teleport, *partials),
                [SMEM] + [VMEM] * (1 + quarters),
                [(pair_shape, LOW)] * owners,
                total,
            )
            gradient, rounded = call(
                next_adjoint_kernel,
                (fetch_table, gradient, *transposed),
                [SMEM] + [VMEM] * (1 + owners),
                [(shape, FULL), (shape, LOW)],
                total,
            )
        else:
            (state,) = call(
                last_state_kernel,
                (teleport, *partials),
                [VMEM] * (1 + quarters),
                [(shape, FULL)],
                [],
            )
            (gradient,) = call(
                last_adjoint_kernel,
                (fetch_table, gradient, *transposed),
                [SMEM] + [VMEM] * (1 + owners),
                [(shape, FULL)],
                total,
            )
    return state.reshape(row_count, hidden), gradient.reshape(row_count, hidden)


def per_device_blocks(teleport, cotangent, fetch_table, block_row, block_slot, values):
    row_count, hidden = teleport.shape
    quarter = values.shape[2]
    block_count = values.shape[1]
    blocks_dev = row_count // quarter
    slot_total = fetch_table.shape[1]
    owner_count = lax.axis_size("node")
    group_size = 16
    turn_count = block_count // group_size
    owner_index = lax.axis_index("node")
    local_weights = values[0]
    row_ids = block_row[0]
    slot_ids = block_slot[0]
    own_plan = lax.dynamic_index_in_dim(fetch_table, owner_index, 0, keepdims=False)
    local_ids = jnp.take(own_plan, slot_ids, axis=0)
    global_ids = slot_ids // CAP * blocks_dev + local_ids
    requests = lax.dynamic_slice_in_dim(fetch_table, owner_index * CAP, CAP, 1).reshape(slot_total)
    block_range = jnp.arange(blocks_dev, dtype=jnp.int32)
    request_hot = requests[:, None] == block_range[None, :]
    request_float = request_hot.astype(jnp.float32)
    weight_groups = local_weights.reshape(turn_count, group_size, quarter, local_weights.shape[2])
    row_groups = row_ids.reshape(turn_count, group_size)
    slot_groups = slot_ids.reshape(turn_count, group_size)
    current = teleport
    for step_index in range(STEPS):
        propagate_rounded = current.astype(jnp.bfloat16)
        everything = lax.all_gather(propagate_rounded, "node", axis=0, tiled=True)
        feature_table = everything.reshape(owner_count * blocks_dev, quarter, hidden)
        columns = jnp.take(feature_table, global_ids, axis=0)
        column_groups = columns.reshape(turn_count, group_size, quarter, hidden)

        def partial_rows(amount):
            quarters_used = amount // row_count

            def partial_advance(running, inputs):
                weights, sources, targets = inputs
                product = jnp.einsum(
                    "bcr,bch->brh", weights, sources, preferred_element_type=jnp.float32
                )
                product = product.reshape(group_size, quarters_used, quarter, hidden)
                return (running.at[targets].add(product), None)

            start_sum = jnp.zeros((blocks_dev, quarters_used, quarter, hidden), jnp.float32)
            running, _ = lax.scan(
                partial_advance, start_sum, (weight_groups, column_groups, row_groups)
            )
            return running.transpose(1, 0, 2, 3).reshape(amount, hidden)

        current = (
            0.9
            * lax.psum_scatter(
                partial_rows(lax.axis_size("edge") * row_count),
                "edge",
                scatter_dimension=0,
                tiled=True,
            )
            + 0.1 * teleport
        )
    adjoint = cotangent
    gradient = 0.1 * cotangent
    for step_index in range(STEPS):
        rounded = adjoint.astype(jnp.bfloat16).reshape(blocks_dev, quarter, hidden)

        def fold_rows(running, arrived_rows):

            def fold_advance(carried, inputs):
                weights, targets, slot_targets = inputs
                sources = jnp.take(arrived_rows, targets, axis=0)
                product = jnp.einsum(
                    "bcr,brh->bch", weights, sources, preferred_element_type=jnp.float32
                )
                return (carried.at[slot_targets].add(product), None)

            carried, _ = lax.scan(fold_advance, running, (weight_groups, row_groups, slot_groups))
            return carried

        transpose_start_sum = jnp.zeros((slot_total, quarter, hidden), jnp.float32)
        partial_value = fold_rows(
            transpose_start_sum, lax.all_gather(rounded, "edge", axis=1, tiled=True)
        )
        summed = jnp.einsum(
            "sj,sch->jch",
            request_float,
            lax.all_to_all(partial_value, "node", split_axis=0, concat_axis=0, tiled=True),
            precision=lax.Precision.HIGHEST,
        )
        adjoint = 0.9 * summed.reshape(row_count, hidden)
        factor = 0.1 if step_index + 1 < STEPS else 1.0
        gradient = gradient + factor * adjoint
    return (current, gradient)


def per_device(teleport, cotangent, fetch_table, block_row, block_slot, values):
    arguments = (teleport, cotangent, fetch_table, block_row, block_slot, values)
    row_count = teleport.shape[0]
    dense_bytes = fetch_table.shape[1] * row_count * values.shape[3] * 2
    if dense_bytes <= DENSE_BYTES:
        return per_device_dense(*arguments)
    return per_device_blocks(*arguments)


def solution(mesh):
    placed = (
        P(("node", "edge"), None),
        P(("node", "edge"), None),
        P(),
        P("node", None),
        P("node", None),
        P("node", None, "edge", None),
    )
    return jax.shard_map(
        per_device,
        mesh=mesh,
        in_specs=placed,
        out_specs=(P(("node", "edge"), None), P(("node", "edge"), None)),
        check_vma=False,
    )
```

```python
import functools

import jax
import jax.numpy as jnp
from jax import lax
from jax.experimental import pallas as pl
from jax.experimental.pallas import tpu as pltpu
from jax.sharding import PartitionSpec as P

CAP = 2
STEPS = 2
DENSE_BYTES = 8 * 2**20
START_MEBIBYTES = 60
BUILD_MEBIBYTES = 40
LOW = jnp.bfloat16
FULL = jnp.float32

VMEM = pl.BlockSpec(memory_space=pltpu.VMEM)
SMEM = pl.BlockSpec(memory_space=pltpu.SMEM)
HBM = pl.BlockSpec(memory_space=pltpu.HBM)


def params(mebibytes):
    return pltpu.CompilerParams(vmem_limit_bytes=mebibytes * 2**20)


def partner(axis, turn):
    return lax.axis_index(axis) ^ turn


def requested(table, slot):
    column = lax.axis_index("node") * CAP + slot % CAP
    return jnp.maximum(table[slot // CAP, column], 0)


def start_kernel(table, teleport, cotangent, *refs):
    send, rounded, plan, state, adjoint, sems = refs
    copies = [
        pltpu.make_async_copy(source, target, sems.at[index])
        for index, (source, target) in enumerate(
            ((table, plan), (teleport, state), (cotangent, adjoint))
        )
    ]
    for copy in copies:
        copy.start()
    copies[0].wait()
    copies[1].wait()
    for slot in range(send.shape[0]):
        send[slot] = state[requested(plan, slot)].astype(LOW)
    copies[2].wait()
    rounded[...] = adjoint[...].astype(LOW)


def build_kernel(rows, slots, weights, high, low, held, total, sems):
    parts = sems.shape[0]
    block_count, quarter, width = held.shape
    chunk = block_count // parts
    copies = [
        pltpu.make_async_copy(
            weights.at[0, pl.ds(part * chunk, chunk)],
            held.at[pl.ds(part * chunk, chunk)],
            sems.at[part],
        )
        for part in range(parts)
    ]
    for copy in copies:
        copy.start()
    total[...] = jnp.zeros_like(total)
    for part, copy in enumerate(copies):
        copy.wait()
        for block in range(part * chunk, (part + 1) * chunk):
            total[slots[0, block], rows[0, block]] += held[block].astype(FULL)
    for slot in range(total.shape[0]):
        for row in range(total.shape[1]):
            place = (pl.ds(slot * quarter, quarter), pl.ds(row * width, width))
            value = total[slot, row]
            rounded = value.astype(LOW)
            high[place] = rounded
            low[place] = (value - rounded.astype(FULL)).astype(LOW)


def forward_kernel(operators, columns, *refs):
    dense = refs[:operators]
    *partials, product = refs[operators:]
    quarters, quarter, hidden = product.shape
    width = quarters * quarter
    vectors = columns[...].reshape(-1, hidden)
    for row in range(partials[0].shape[0]):
        summed = sum(
            lax.dot_general(
                vectors,
                part[:, row * width : (row + 1) * width],
                (((0,), (0,)), ((), ())),
                preferred_element_type=FULL,
            )
            for part in dense
        )
        product[...] = summed.T.reshape(product.shape)
        for turn, partial in enumerate(partials):
            partial[row] = product[partner("edge", turn)].astype(partial.dtype)


def adjoint_kernel(operators, *refs):
    *arrived, send, source = refs[operators:]
    for turn, part in enumerate(arrived):
        source[:, partner("edge", turn)] = part[...]
    vectors = source[...].reshape(-1, source.shape[-1])
    product = sum(jnp.dot(part[...], vectors, preferred_element_type=FULL) for part in refs[:operators])
    send[...] = product.reshape(send.shape).astype(LOW)


def state_of(arrived, teleport):
    summed = arrived[0][...]
    for part in arrived[1:]:
        summed += part[...].astype(FULL)
    return 0.9 * summed + 0.1 * teleport[...]


def next_state_kernel(table, teleport, *refs):
    *arrived, send, state = refs
    state[...] = state_of(arrived, teleport)
    for slot in range(send.shape[0]):
        send[slot] = state[requested(table, slot)].astype(LOW)


def last_state_kernel(teleport, *refs):
    *arrived, state = refs
    state[...] = state_of(arrived, teleport)


def gather_adjoint(table, arrived, summed):
    summed[...] = jnp.zeros_like(summed)
    for slot in range(arrived.shape[0]):
        summed[requested(table, slot)] += arrived[slot].astype(FULL)


def next_adjoint_kernel(table, cotangent, arrived, gradient, rounded, summed):
    gather_adjoint(table, arrived, summed)
    adjoint = 0.9 * summed[...]
    gradient[...] = 0.1 * cotangent[...] + 0.1 * adjoint
    rounded[...] = adjoint.astype(LOW)


def last_adjoint_kernel(table, gradient_in, arrived, gradient, summed):
    gather_adjoint(table, arrived, summed)
    gradient[...] = gradient_in[...] + 0.9 * summed[...]


def per_device_dense(teleport, cotangent, fetch_table, block_row, block_slot, values):
    row_count, hidden = teleport.shape
    _, block_count, quarter, width = values.shape
    count = row_count // quarter
    quarters = lax.axis_size("edge")
    slot_total = fetch_table.shape[1]
    shape = (count, quarter, hidden)
    slot_shape = (slot_total, quarter, hidden)
    teleport = teleport.reshape(shape)
    cotangent = cotangent.reshape(shape)

    def call(kernel, operands, places, outs, scratch, mebibytes=8, cost=None):
        return pl.pallas_call(
            kernel,
            out_shape=[jax.ShapeDtypeStruct(*out) for out in outs],
            in_specs=places,
            out_specs=[VMEM] * len(outs),
            scratch_shapes=scratch,
            compiler_params=params(mebibytes),
            cost_estimate=cost,
        )(*operands)

    def over_node(array):
        return lax.all_to_all(array, "node", 0, 0, tiled=True)

    def over_edge(arrays):
        return [arrays[0]] + [
            lax.ppermute(arrays[turn], "edge", [(place, place ^ turn) for place in range(quarters)])
            for turn in range(1, quarters)
        ]

    send, rounded = call(
        start_kernel,
        (fetch_table, teleport, cotangent),
        [HBM] * 3,
        [(slot_shape, LOW), (shape, LOW)],
        [
            pltpu.SMEM(fetch_table.shape, fetch_table.dtype),
            pltpu.VMEM(shape, FULL),
            pltpu.VMEM(shape, FULL),
            pltpu.SemaphoreType.DMA((3,)),
        ],
        START_MEBIBYTES,
    )
    dense_shape = (slot_total * quarter, count * width)
    parts = next(size for size in (12, 8, 4, 2, 1) if block_count % size == 0)
    high, low = call(
        build_kernel,
        (block_row, block_slot, values),
        [SMEM, SMEM, HBM],
        [(dense_shape, LOW)] * 2,
        [
            pltpu.VMEM((block_count, quarter, width), LOW),
            pltpu.VMEM((slot_total, count, quarter, width), FULL),
            pltpu.SemaphoreType.DMA((parts,)),
        ],
        BUILD_MEBIBYTES,
        pl.CostEstimate(flops=0, bytes_accessed=values.size * 2, transcendentals=0),
    )

    gradient = cotangent
    for step in range(STEPS):
        last = step + 1 == STEPS
        dense = (high,) if last else (high, low)
        cost = pl.CostEstimate(
            flops=2 * len(dense) * high.size * hidden,
            bytes_accessed=len(dense) * high.size * 2,
            transcendentals=0,
        )
        columns = over_node(send)
        arrived = over_edge([rounded] * quarters)
        (transposed,) = call(
            functools.partial(adjoint_kernel, len(dense)),
            (*dense, *arrived),
            [VMEM] * (quarters + len(dense)),
            [(slot_shape, LOW)],
            [pltpu.VMEM((count, quarters, quarter, hidden), LOW)],
            cost=cost,
        )
        transposed, columns = lax.optimization_barrier((transposed, columns))
        partials = call(
            functools.partial(forward_kernel, len(dense)),
            (columns, *dense),
            [VMEM] * (1 + len(dense)),
            [(shape, FULL)] + [(shape, LOW)] * (quarters - 1),
            [pltpu.VMEM((quarters, quarter, hidden), FULL)],
            cost=cost,
        )
        transposed = over_node(transposed)
        partials = over_edge(partials)
        total = [pltpu.VMEM(shape, FULL)]
        if not last:
            (send,) = call(
                next_state_kernel,
                (fetch_table, teleport, *partials),
                [SMEM] + [VMEM] * (1 + quarters),
                [(slot_shape, LOW)],
                total,
            )
            send, transposed = lax.optimization_barrier((send, transposed))
            gradient, rounded = call(
                next_adjoint_kernel,
                (fetch_table, gradient, transposed),
                [SMEM, VMEM, VMEM],
                [(shape, FULL), (shape, LOW)],
                total,
            )
        else:
            (state,) = call(
                last_state_kernel,
                (teleport, *partials),
                [VMEM] * (1 + quarters),
                [(shape, FULL)],
                [],
            )
            state, transposed = lax.optimization_barrier((state, transposed))
            (gradient,) = call(
                last_adjoint_kernel,
                (fetch_table, gradient, transposed),
                [SMEM, VMEM, VMEM],
                [(shape, FULL)],
                total,
            )
    return state.reshape(row_count, hidden), gradient.reshape(row_count, hidden)


def per_device_blocks(teleport, cotangent, fetch_table, block_row, block_slot, values):
    row_count, hidden = teleport.shape
    quarter = values.shape[2]
    block_count = values.shape[1]
    blocks_dev = row_count // quarter
    slot_total = fetch_table.shape[1]
    owner_count = lax.axis_size("node")
    group_size = 16
    turn_count = block_count // group_size
    owner_index = lax.axis_index("node")
    local_weights = values[0]
    row_ids = block_row[0]
    slot_ids = block_slot[0]
    own_plan = lax.dynamic_index_in_dim(fetch_table, owner_index, 0, keepdims=False)
    local_ids = jnp.take(own_plan, slot_ids, axis=0)
    global_ids = slot_ids // CAP * blocks_dev + local_ids
    requests = lax.dynamic_slice_in_dim(fetch_table, owner_index * CAP, CAP, 1).reshape(slot_total)
    block_range = jnp.arange(blocks_dev, dtype=jnp.int32)
    request_hot = requests[:, None] == block_range[None, :]
    request_float = request_hot.astype(jnp.float32)
    weight_groups = local_weights.reshape(turn_count, group_size, quarter, local_weights.shape[2])
    row_groups = row_ids.reshape(turn_count, group_size)
    slot_groups = slot_ids.reshape(turn_count, group_size)
    current = teleport
    for step_index in range(STEPS):
        propagate_rounded = current.astype(jnp.bfloat16)
        everything = lax.all_gather(propagate_rounded, "node", axis=0, tiled=True)
        feature_table = everything.reshape(owner_count * blocks_dev, quarter, hidden)
        columns = jnp.take(feature_table, global_ids, axis=0)
        column_groups = columns.reshape(turn_count, group_size, quarter, hidden)

        def partial_rows(amount):
            quarters_used = amount // row_count

            def partial_advance(running, inputs):
                weights, sources, targets = inputs
                product = jnp.einsum(
                    "bcr,bch->brh", weights, sources, preferred_element_type=jnp.float32
                )
                product = product.reshape(group_size, quarters_used, quarter, hidden)
                return (running.at[targets].add(product), None)

            start_sum = jnp.zeros((blocks_dev, quarters_used, quarter, hidden), jnp.float32)
            running, _ = lax.scan(
                partial_advance, start_sum, (weight_groups, column_groups, row_groups)
            )
            return running.transpose(1, 0, 2, 3).reshape(amount, hidden)

        current = (
            0.9
            * lax.psum_scatter(
                partial_rows(lax.axis_size("edge") * row_count),
                "edge",
                scatter_dimension=0,
                tiled=True,
            )
            + 0.1 * teleport
        )
    adjoint = cotangent
    gradient = 0.1 * cotangent
    for step_index in range(STEPS):
        rounded = adjoint.astype(jnp.bfloat16).reshape(blocks_dev, quarter, hidden)

        def fold_rows(running, arrived_rows):

            def fold_advance(carried, inputs):
                weights, targets, slot_targets = inputs
                sources = jnp.take(arrived_rows, targets, axis=0)
                product = jnp.einsum(
                    "bcr,brh->bch", weights, sources, preferred_element_type=jnp.float32
                )
                return (carried.at[slot_targets].add(product), None)

            carried, _ = lax.scan(fold_advance, running, (weight_groups, row_groups, slot_groups))
            return carried

        transpose_start_sum = jnp.zeros((slot_total, quarter, hidden), jnp.float32)
        partial_value = fold_rows(
            transpose_start_sum, lax.all_gather(rounded, "edge", axis=1, tiled=True)
        )
        summed = jnp.einsum(
            "sj,sch->jch",
            request_float,
            lax.all_to_all(partial_value, "node", split_axis=0, concat_axis=0, tiled=True),
            precision=lax.Precision.HIGHEST,
        )
        adjoint = 0.9 * summed.reshape(row_count, hidden)
        factor = 0.1 if step_index + 1 < STEPS else 1.0
        gradient = gradient + factor * adjoint
    return (current, gradient)


def per_device(teleport, cotangent, fetch_table, block_row, block_slot, values):
    arguments = (teleport, cotangent, fetch_table, block_row, block_slot, values)
    row_count = teleport.shape[0]
    dense_bytes = fetch_table.shape[1] * row_count * values.shape[3] * 2
    if dense_bytes <= DENSE_BYTES:
        return per_device_dense(*arguments)
    return per_device_blocks(*arguments)


def solution(mesh):
    placed = (
        P(("node", "edge"), None),
        P(("node", "edge"), None),
        P(),
        P("node", None),
        P("node", None),
        P("node", None, "edge", None),
    )
    return jax.shard_map(
        per_device,
        mesh=mesh,
        in_specs=placed,
        out_specs=(P(("node", "edge"), None), P(("node", "edge"), None)),
        check_vma=False,
    )
```

```python
import functools

import jax
import jax.numpy as jnp
from jax import lax
from jax.experimental import pallas as pl
from jax.experimental.pallas import tpu as pltpu
from jax.sharding import PartitionSpec as P

CAP = 2
STEPS = 2
DENSE_BYTES = 8 * 2**20
START_MEBIBYTES = 60
BUILD_MEBIBYTES = 32
LOW = jnp.bfloat16
FULL = jnp.float32

VMEM = pl.BlockSpec(memory_space=pltpu.VMEM)
SMEM = pl.BlockSpec(memory_space=pltpu.SMEM)
HBM = pl.BlockSpec(memory_space=pltpu.HBM)


def params(mebibytes):
    return pltpu.CompilerParams(vmem_limit_bytes=mebibytes * 2**20)


def partner(axis, turn):
    return lax.axis_index(axis) ^ turn


def requested(table, slot):
    column = lax.axis_index("node") * CAP + slot % CAP
    return jnp.maximum(table[slot // CAP, column], 0)


def start_kernel(table, teleport, cotangent, *refs):
    send, rounded, plan, state, adjoint, sems = refs
    copies = [
        pltpu.make_async_copy(source, target, sems.at[index])
        for index, (source, target) in enumerate(
            ((table, plan), (teleport, state), (cotangent, adjoint))
        )
    ]
    for copy in copies:
        copy.start()
    copies[0].wait()
    copies[1].wait()
    for slot in range(send.shape[0]):
        send[slot] = state[requested(plan, slot)].astype(LOW)
    copies[2].wait()
    rounded[...] = adjoint[...].astype(LOW)


def build_kernel(rows, slots, weights, high, low, held, total, sems):
    parts = sems.shape[0]
    block_count, quarter, width = held.shape
    chunk = block_count // parts
    copies = [
        pltpu.make_async_copy(
            weights.at[0, pl.ds(part * chunk, chunk)],
            held.at[pl.ds(part * chunk, chunk)],
            sems.at[part],
        )
        for part in range(parts)
    ]
    for copy in copies:
        copy.start()
    total[...] = jnp.zeros_like(total)
    for part, copy in enumerate(copies):
        copy.wait()
        for block in range(part * chunk, (part + 1) * chunk):
            total[slots[0, block], rows[0, block]] += held[block].astype(FULL)
    for slot in range(total.shape[0]):
        for row in range(total.shape[1]):
            place = (pl.ds(slot * quarter, quarter), pl.ds(row * width, width))
            value = total[slot, row]
            rounded = value.astype(LOW)
            high[place] = rounded
            low[place] = (value - rounded.astype(FULL)).astype(LOW)


def forward_kernel(operators, columns, *refs):
    dense = refs[:operators]
    *partials, product = refs[operators:]
    quarters, quarter, hidden = product.shape
    width = quarters * quarter
    vectors = columns[...].reshape(-1, hidden)
    for row in range(partials[0].shape[0]):
        summed = sum(
            lax.dot_general(
                vectors,
                part[:, row * width : (row + 1) * width],
                (((0,), (0,)), ((), ())),
                preferred_element_type=FULL,
            )
            for part in dense
        )
        product[...] = summed.T.reshape(product.shape)
        for turn, partial in zip((0, *range(quarters - 1, 0, -1)), partials):
            partial[row] = product[partner("edge", turn)].astype(partial.dtype)


def apply_adjoint(dense, vectors, send):
    product = sum(jnp.dot(part[...], vectors, preferred_element_type=FULL) for part in dense)
    send[...] = product.reshape(send.shape).astype(LOW)


def adjoint_kernel(operators, *refs):
    *arrived, send, source = refs[operators:]
    for turn, part in enumerate(arrived):
        source[:, partner("edge", turn)] = part[...]
    apply_adjoint(refs[:operators], source[...].reshape(-1, source.shape[-1]), send)


def gathered_adjoint_kernel(dense, arrived, send):
    apply_adjoint((dense,), arrived[...].reshape(-1, arrived.shape[-1]), send)


def state_of(arrived, teleport):
    summed = arrived[0][...]
    for part in arrived[1:]:
        summed += part[...].astype(FULL)
    return 0.9 * summed + 0.1 * teleport[...]


def next_state_kernel(table, teleport, *refs):
    *arrived, send, state = refs
    state[...] = state_of(arrived, teleport)
    for slot in range(send.shape[0]):
        send[slot] = state[requested(table, slot)].astype(LOW)


def last_state_kernel(teleport, *refs):
    *arrived, state = refs
    state[...] = state_of(arrived, teleport)


def gather_adjoint(table, arrived, summed):
    summed[...] = jnp.zeros_like(summed)
    for slot in range(arrived.shape[0]):
        summed[requested(table, slot)] += arrived[slot].astype(FULL)


def next_adjoint_kernel(table, cotangent, arrived, gradient, rounded, summed):
    gather_adjoint(table, arrived, summed)
    adjoint = 0.9 * summed[...]
    gradient[...] = 0.1 * cotangent[...] + 0.1 * adjoint
    rounded[...] = adjoint.astype(LOW)


def last_adjoint_kernel(table, gradient_in, arrived, gradient, summed):
    gather_adjoint(table, arrived, summed)
    gradient[...] = gradient_in[...] + 0.9 * summed[...]


def per_device_dense(teleport, cotangent, fetch_table, block_row, block_slot, values):
    row_count, hidden = teleport.shape
    _, block_count, quarter, width = values.shape
    count = row_count // quarter
    quarters = lax.axis_size("edge")
    slot_total = fetch_table.shape[1]
    shape = (count, quarter, hidden)
    slot_shape = (slot_total, quarter, hidden)
    teleport = teleport.reshape(shape)
    cotangent = cotangent.reshape(shape)

    def call(kernel, operands, places, outs, scratch, mebibytes=8, cost=None):
        return pl.pallas_call(
            kernel,
            out_shape=[jax.ShapeDtypeStruct(*out) for out in outs],
            in_specs=places,
            out_specs=[VMEM] * len(outs),
            scratch_shapes=scratch,
            compiler_params=params(mebibytes),
            cost_estimate=cost,
        )(*operands)

    def over_node(array):
        merged = array.reshape(lax.axis_size("node"), CAP * quarter, hidden)
        return lax.all_to_all(merged, "node", 0, 0, tiled=True).reshape(slot_shape)

    def over_edge(arrays, turns):
        return [arrays[0]] + [
            lax.ppermute(array, "edge", [(place, place ^ turn) for place in range(quarters)])
            for turn, array in zip(turns, arrays[1:])
        ]

    send, rounded = call(
        start_kernel,
        (fetch_table, teleport, cotangent),
        [HBM] * 3,
        [(slot_shape, LOW), (shape, LOW)],
        [
            pltpu.SMEM(fetch_table.shape, fetch_table.dtype),
            pltpu.VMEM(shape, FULL),
            pltpu.VMEM(shape, FULL),
            pltpu.SemaphoreType.DMA((3,)),
        ],
        START_MEBIBYTES,
    )
    dense_shape = (slot_total * quarter, count * width)
    parts = next(size for size in (12, 8, 4, 2, 1) if block_count % size == 0)
    high, low = call(
        build_kernel,
        (block_row, block_slot, values),
        [SMEM, SMEM, HBM],
        [(dense_shape, LOW)] * 2,
        [
            pltpu.VMEM((block_count, quarter, width), LOW),
            pltpu.VMEM((slot_total, count, quarter, width), FULL),
            pltpu.SemaphoreType.DMA((parts,)),
        ],
        BUILD_MEBIBYTES,
        pl.CostEstimate(flops=0, bytes_accessed=values.size * 2, transcendentals=0),
    )

    gradient = cotangent
    for step in range(STEPS):
        last = step + 1 == STEPS
        dense = (high,) if last else (high, low)
        cost = pl.CostEstimate(
            flops=2 * len(dense) * high.size * hidden,
            bytes_accessed=len(dense) * high.size * 2,
            transcendentals=0,
        )
        columns = over_node(send)
        if not last:
            arrived = over_edge([rounded] * quarters, range(1, quarters))
            (transposed,) = call(
                functools.partial(adjoint_kernel, len(dense)),
                (*dense, *arrived),
                [VMEM] * (quarters + len(dense)),
                [(slot_shape, LOW)],
                [pltpu.VMEM((count, quarters, quarter, hidden), LOW)],
                cost=cost,
            )
        else:
            (transposed,) = call(
                gathered_adjoint_kernel,
                (high, lax.all_gather(rounded, "edge", axis=1, tiled=True)),
                [VMEM] * 2,
                [(slot_shape, LOW)],
                [],
                cost=cost,
            )
        transposed, columns = lax.optimization_barrier((transposed, columns))
        partials = call(
            functools.partial(forward_kernel, len(dense)),
            (columns, *dense),
            [VMEM] * (1 + len(dense)),
            [(shape, FULL)] + [(shape, LOW)] * (quarters - 1),
            [pltpu.VMEM((quarters, quarter, hidden), FULL)],
            cost=cost,
        )
        transposed = over_node(transposed)
        partials = over_edge(partials, range(quarters - 1, 0, -1))
        total = [pltpu.VMEM(shape, FULL)]
        if not last:
            (send,) = call(
                next_state_kernel,
                (fetch_table, teleport, *partials),
                [SMEM] + [VMEM] * (1 + quarters),
                [(slot_shape, LOW)],
                total,
            )
            send, transposed = lax.optimization_barrier((send, transposed))
            gradient, rounded = call(
                next_adjoint_kernel,
                (fetch_table, gradient, transposed),
                [SMEM, VMEM, VMEM],
                [(shape, FULL), (shape, LOW)],
                total,
            )
        else:
            (state,) = call(
                last_state_kernel,
                (teleport, *partials),
                [VMEM] * (1 + quarters),
                [(shape, FULL)],
                [],
            )
            state, transposed = lax.optimization_barrier((state, transposed))
            (gradient,) = call(
                last_adjoint_kernel,
                (fetch_table, gradient, transposed),
                [SMEM, VMEM, VMEM],
                [(shape, FULL)],
                total,
            )
    return state.reshape(row_count, hidden), gradient.reshape(row_count, hidden)


def per_device_blocks(teleport, cotangent, fetch_table, block_row, block_slot, values):
    row_count, hidden = teleport.shape
    quarter = values.shape[2]
    block_count = values.shape[1]
    blocks_dev = row_count // quarter
    slot_total = fetch_table.shape[1]
    owner_count = lax.axis_size("node")
    group_size = 16
    turn_count = block_count // group_size
    owner_index = lax.axis_index("node")
    local_weights = values[0]
    row_ids = block_row[0]
    slot_ids = block_slot[0]
    own_plan = lax.dynamic_index_in_dim(fetch_table, owner_index, 0, keepdims=False)
    local_ids = jnp.take(own_plan, slot_ids, axis=0)
    global_ids = slot_ids // CAP * blocks_dev + local_ids
    requests = lax.dynamic_slice_in_dim(fetch_table, owner_index * CAP, CAP, 1).reshape(slot_total)
    block_range = jnp.arange(blocks_dev, dtype=jnp.int32)
    request_hot = requests[:, None] == block_range[None, :]
    request_float = request_hot.astype(jnp.float32)
    weight_groups = local_weights.reshape(turn_count, group_size, quarter, local_weights.shape[2])
    row_groups = row_ids.reshape(turn_count, group_size)
    slot_groups = slot_ids.reshape(turn_count, group_size)
    current = teleport
    for step_index in range(STEPS):
        propagate_rounded = current.astype(jnp.bfloat16)
        everything = lax.all_gather(propagate_rounded, "node", axis=0, tiled=True)
        feature_table = everything.reshape(owner_count * blocks_dev, quarter, hidden)
        columns = jnp.take(feature_table, global_ids, axis=0)
        column_groups = columns.reshape(turn_count, group_size, quarter, hidden)

        def partial_rows(amount):
            quarters_used = amount // row_count

            def partial_advance(running, inputs):
                weights, sources, targets = inputs
                product = jnp.einsum(
                    "bcr,bch->brh", weights, sources, preferred_element_type=jnp.float32
                )
                product = product.reshape(group_size, quarters_used, quarter, hidden)
                return (running.at[targets].add(product), None)

            start_sum = jnp.zeros((blocks_dev, quarters_used, quarter, hidden), jnp.float32)
            running, _ = lax.scan(
                partial_advance, start_sum, (weight_groups, column_groups, row_groups)
            )
            return running.transpose(1, 0, 2, 3).reshape(amount, hidden)

        current = (
            0.9
            * lax.psum_scatter(
                partial_rows(lax.axis_size("edge") * row_count),
                "edge",
                scatter_dimension=0,
                tiled=True,
            )
            + 0.1 * teleport
        )
    adjoint = cotangent
    gradient = 0.1 * cotangent
    for step_index in range(STEPS):
        rounded = adjoint.astype(jnp.bfloat16).reshape(blocks_dev, quarter, hidden)

        def fold_rows(running, arrived_rows):

            def fold_advance(carried, inputs):
                weights, targets, slot_targets = inputs
                sources = jnp.take(arrived_rows, targets, axis=0)
                product = jnp.einsum(
                    "bcr,brh->bch", weights, sources, preferred_element_type=jnp.float32
                )
                return (carried.at[slot_targets].add(product), None)

            carried, _ = lax.scan(fold_advance, running, (weight_groups, row_groups, slot_groups))
            return carried

        transpose_start_sum = jnp.zeros((slot_total, quarter, hidden), jnp.float32)
        partial_value = fold_rows(
            transpose_start_sum, lax.all_gather(rounded, "edge", axis=1, tiled=True)
        )
        summed = jnp.einsum(
            "sj,sch->jch",
            request_float,
            lax.all_to_all(partial_value, "node", split_axis=0, concat_axis=0, tiled=True),
            precision=lax.Precision.HIGHEST,
        )
        adjoint = 0.9 * summed.reshape(row_count, hidden)
        factor = 0.1 if step_index + 1 < STEPS else 1.0
        gradient = gradient + factor * adjoint
    return (current, gradient)


def per_device(teleport, cotangent, fetch_table, block_row, block_slot, values):
    arguments = (teleport, cotangent, fetch_table, block_row, block_slot, values)
    row_count = teleport.shape[0]
    dense_bytes = fetch_table.shape[1] * row_count * values.shape[3] * 2
    if dense_bytes <= DENSE_BYTES:
        return per_device_dense(*arguments)
    return per_device_blocks(*arguments)


def solution(mesh):
    placed = (
        P(("node", "edge"), None),
        P(("node", "edge"), None),
        P(),
        P("node", None),
        P("node", None),
        P("node", None, "edge", None),
    )
    return jax.shard_map(
        per_device,
        mesh=mesh,
        in_specs=placed,
        out_specs=(P(("node", "edge"), None), P(("node", "edge"), None)),
        check_vma=False,
    )
```

```python
import functools

import jax
import jax.numpy as jnp
from jax import lax
from jax.experimental import pallas as pl
from jax.experimental.pallas import tpu as pltpu
from jax.sharding import PartitionSpec as P

CAP = 2
STEPS = 2
DENSE_BYTES = 8 * 2**20
START_MEBIBYTES = 60
BUILD_MEBIBYTES = 60
APPLY_MEBIBYTES = 57
LOW = jnp.bfloat16
FULL = jnp.float32

VMEM = pl.BlockSpec(memory_space=pltpu.VMEM)
SMEM = pl.BlockSpec(memory_space=pltpu.SMEM)
HBM = pl.BlockSpec(memory_space=pltpu.HBM)


def params(mebibytes):
    return pltpu.CompilerParams(vmem_limit_bytes=mebibytes * 2**20)


def partner(axis, turn):
    return lax.axis_index(axis) ^ turn


def requested(table, slot):
    column = lax.axis_index("node") * CAP + slot % CAP
    return jnp.maximum(table[slot // CAP, column], 0)


def start_kernel(table, teleport, cotangent, *refs):
    send, rounded, plan, state, adjoint, sems = refs
    copies = [
        pltpu.make_async_copy(source, target, sems.at[index])
        for index, (source, target) in enumerate(
            ((table, plan), (teleport, state), (cotangent, adjoint))
        )
    ]
    for copy in copies:
        copy.start()
    copies[0].wait()
    copies[1].wait()
    for slot in range(send.shape[0]):
        send[slot] = state[requested(plan, slot)].astype(LOW)
    copies[2].wait()
    rounded[...] = adjoint[...].astype(LOW)


def build_kernel(rows, slots, weights, *refs):
    outs = refs[:2]
    row_of, slot_of, held, total, high, low, sems, out_sems = refs[2:]
    parts = sems.shape[0] - 2
    block_count, quarter, width = held.shape
    chunk = block_count // parts
    indices = [
        pltpu.make_async_copy(source, target, sems.at[parts + index])
        for index, (source, target) in enumerate(((rows, row_of), (slots, slot_of)))
    ]
    copies = [
        pltpu.make_async_copy(
            weights.at[0, pl.ds(part * chunk, chunk)],
            held.at[pl.ds(part * chunk, chunk)],
            sems.at[part],
        )
        for part in range(parts)
    ]
    for copy in indices + copies:
        copy.start()
    total[...] = jnp.zeros_like(total)
    for copy in indices:
        copy.wait()
    for part, copy in enumerate(copies):
        copy.wait()
        for block in range(part * chunk, (part + 1) * chunk):
            total[row_of[0, block], slot_of[0, block]] += held[block].astype(FULL)
    stores = []
    for row in range(total.shape[0]):
        value = total[row].reshape(-1, width)
        rounded = value.astype(LOW)
        high[row] = rounded
        low[row] = (value - rounded.astype(FULL)).astype(LOW)
        for index, part in enumerate((high, low)):
            store = pltpu.make_async_copy(
                part.at[row], outs[index].at[row], out_sems.at[index, row]
            )
            store.start()
            stores.append(store)
    for store in stores:
        store.wait()


def fetch(dense, held, sems):
    copies = [
        [
            pltpu.make_async_copy(part.at[row], held.at[index, row], sems.at[index, row])
            for index, part in enumerate(dense)
        ]
        for row in range(held.shape[1])
    ]
    for row_copies in copies:
        for copy in row_copies:
            copy.start()
    return copies


def forward_kernel(operators, *refs):
    columns, *partials, product, held, sems = refs[operators:]
    copies = fetch(refs[:operators], held, sems)
    quarters, quarter, hidden = product.shape
    vectors = columns[...].reshape(-1, hidden)
    for row, row_copies in enumerate(copies):
        for copy in row_copies:
            copy.wait()
        summed = sum(
            lax.dot_general(
                vectors,
                held[index, row],
                (((0,), (0,)), ((), ())),
                preferred_element_type=FULL,
            )
            for index in range(operators)
        )
        product[...] = summed.T.reshape(product.shape)
        for turn, partial in zip((0, *range(quarters - 1, 0, -1)), partials):
            partial[row] = product[partner("edge", turn)].astype(partial.dtype)


def adjoint_kernel(operators, *refs):
    *arrived, send, source, held, sems = refs[operators:]
    copies = fetch(refs[:operators], held, sems)
    if len(arrived) == 1:
        source = arrived[0]
    else:
        for turn, part in enumerate(arrived):
            source[:, partner("edge", turn)] = part[...]
    total = 0
    for row, row_copies in enumerate(copies):
        for copy in row_copies:
            copy.wait()
        vectors = source[row].reshape(-1, source.shape[-1])
        for index in range(operators):
            total += jnp.dot(held[index, row], vectors, preferred_element_type=FULL)
    send[...] = total.reshape(send.shape).astype(LOW)


def state_of(arrived, teleport):
    summed = arrived[0][...]
    for part in arrived[1:]:
        summed += part[...].astype(FULL)
    return 0.9 * summed + 0.1 * teleport[...]


def next_state_kernel(table, teleport, *refs):
    *arrived, send, state = refs
    state[...] = state_of(arrived, teleport)
    for slot in range(send.shape[0]):
        send[slot] = state[requested(table, slot)].astype(LOW)


def last_state_kernel(teleport, *refs):
    *arrived, state = refs
    state[...] = state_of(arrived, teleport)


def gather_adjoint(table, arrived, summed):
    summed[...] = jnp.zeros_like(summed)
    for slot in range(arrived.shape[0]):
        summed[requested(table, slot)] += arrived[slot].astype(FULL)


def next_adjoint_kernel(table, cotangent, arrived, gradient, rounded, summed):
    gather_adjoint(table, arrived, summed)
    adjoint = 0.9 * summed[...]
    gradient[...] = 0.1 * cotangent[...] + 0.1 * adjoint
    rounded[...] = adjoint.astype(LOW)


def last_adjoint_kernel(table, gradient_in, arrived, gradient, summed):
    gather_adjoint(table, arrived, summed)
    gradient[...] = gradient_in[...] + 0.9 * summed[...]


def per_device_dense(teleport, cotangent, fetch_table, block_row, block_slot, values):
    row_count, hidden = teleport.shape
    _, block_count, quarter, width = values.shape
    count = row_count // quarter
    quarters = lax.axis_size("edge")
    slot_total = fetch_table.shape[1]
    shape = (count, quarter, hidden)
    slot_shape = (slot_total, quarter, hidden)
    teleport = teleport.reshape(shape)
    cotangent = cotangent.reshape(shape)

    def call(kernel, operands, places, outs, scratch, mebibytes=8, cost=None, place=VMEM):
        return pl.pallas_call(
            kernel,
            out_shape=[jax.ShapeDtypeStruct(*out) for out in outs],
            in_specs=places,
            out_specs=[place] * len(outs),
            scratch_shapes=scratch,
            compiler_params=params(mebibytes),
            cost_estimate=cost,
        )(*operands)

    def over_node(array):
        merged = array.reshape(lax.axis_size("node"), CAP * quarter, hidden)
        return lax.all_to_all(merged, "node", 0, 0, tiled=True).reshape(slot_shape)

    def over_edge(arrays, turns):
        return [arrays[0]] + [
            lax.ppermute(array, "edge", [(place, place ^ turn) for place in range(quarters)])
            for turn, array in zip(turns, arrays[1:])
        ]

    send, rounded = call(
        start_kernel,
        (fetch_table, teleport, cotangent),
        [HBM] * 3,
        [(slot_shape, LOW), (shape, LOW)],
        [
            pltpu.SMEM(fetch_table.shape, fetch_table.dtype),
            pltpu.VMEM(shape, FULL),
            pltpu.VMEM(shape, FULL),
            pltpu.SemaphoreType.DMA((3,)),
        ],
        START_MEBIBYTES,
    )
    dense_shape = (count, slot_total * quarter, width)
    parts = next(size for size in (12, 8, 4, 2, 1) if block_count % size == 0)
    high, low = call(
        build_kernel,
        (block_row, block_slot, values),
        [HBM] * 3,
        [(dense_shape, LOW)] * 2,
        [
            pltpu.SMEM(block_row.shape, block_row.dtype),
            pltpu.SMEM(block_slot.shape, block_slot.dtype),
            pltpu.VMEM((block_count, quarter, width), LOW),
            pltpu.VMEM((count, slot_total, quarter, width), FULL),
            pltpu.VMEM(dense_shape, LOW),
            pltpu.VMEM(dense_shape, LOW),
            pltpu.SemaphoreType.DMA((parts + 2,)),
            pltpu.SemaphoreType.DMA((2, count)),
        ],
        BUILD_MEBIBYTES,
        pl.CostEstimate(flops=0, bytes_accessed=values.size * 2, transcendentals=0),
        HBM,
    )

    gradient = cotangent
    for step in range(STEPS):
        last = step + 1 == STEPS
        dense = (high,) if last else (high, low)
        cost = pl.CostEstimate(
            flops=2 * len(dense) * high.size * hidden,
            bytes_accessed=len(dense) * high.size * 2,
            transcendentals=0,
        )
        fetched = [
            pltpu.VMEM((len(dense),) + dense_shape, LOW),
            pltpu.SemaphoreType.DMA((len(dense), count)),
        ]
        columns = over_node(send)
        if not last:
            arrived = over_edge([rounded] * quarters, range(1, quarters))
        else:
            arrived = [lax.all_gather(rounded, "edge", axis=1, tiled=True)]
        (transposed,) = call(
            functools.partial(adjoint_kernel, len(dense)),
            (*dense, *arrived),
            [HBM] * len(dense) + [VMEM] * len(arrived),
            [(slot_shape, LOW)],
            [pltpu.VMEM((count, quarters, quarter, hidden), LOW), *fetched],
            APPLY_MEBIBYTES,
            cost,
        )
        transposed, columns = lax.optimization_barrier((transposed, columns))
        partials = call(
            functools.partial(forward_kernel, len(dense)),
            (*dense, columns),
            [HBM] * len(dense) + [VMEM],
            [(shape, FULL)] + [(shape, LOW)] * (quarters - 1),
            [pltpu.VMEM((quarters, quarter, hidden), FULL), *fetched],
            APPLY_MEBIBYTES,
            cost,
        )
        transposed = over_node(transposed)
        partials = over_edge(partials, range(quarters - 1, 0, -1))
        total = [pltpu.VMEM(shape, FULL)]
        if not last:
            (send,) = call(
                next_state_kernel,
                (fetch_table, teleport, *partials),
                [SMEM] + [VMEM] * (1 + quarters),
                [(slot_shape, LOW)],
                total,
            )
            send, transposed = lax.optimization_barrier((send, transposed))
            gradient, rounded = call(
                next_adjoint_kernel,
                (fetch_table, gradient, transposed),
                [SMEM, VMEM, VMEM],
                [(shape, FULL), (shape, LOW)],
                total,
            )
        else:
            (state,) = call(
                last_state_kernel,
                (teleport, *partials),
                [VMEM] * (1 + quarters),
                [(shape, FULL)],
                [],
            )
            state, transposed = lax.optimization_barrier((state, transposed))
            (gradient,) = call(
                last_adjoint_kernel,
                (fetch_table, gradient, transposed),
                [SMEM, VMEM, VMEM],
                [(shape, FULL)],
                total,
            )
    return state.reshape(row_count, hidden), gradient.reshape(row_count, hidden)


def per_device_blocks(teleport, cotangent, fetch_table, block_row, block_slot, values):
    row_count, hidden = teleport.shape
    quarter = values.shape[2]
    block_count = values.shape[1]
    blocks_dev = row_count // quarter
    slot_total = fetch_table.shape[1]
    owner_count = lax.axis_size("node")
    group_size = 16
    turn_count = block_count // group_size
    owner_index = lax.axis_index("node")
    local_weights = values[0]
    row_ids = block_row[0]
    slot_ids = block_slot[0]
    own_plan = lax.dynamic_index_in_dim(fetch_table, owner_index, 0, keepdims=False)
    local_ids = jnp.take(own_plan, slot_ids, axis=0)
    global_ids = slot_ids // CAP * blocks_dev + local_ids
    requests = lax.dynamic_slice_in_dim(fetch_table, owner_index * CAP, CAP, 1).reshape(slot_total)
    block_range = jnp.arange(blocks_dev, dtype=jnp.int32)
    request_hot = requests[:, None] == block_range[None, :]
    request_float = request_hot.astype(jnp.float32)
    weight_groups = local_weights.reshape(turn_count, group_size, quarter, local_weights.shape[2])
    row_groups = row_ids.reshape(turn_count, group_size)
    slot_groups = slot_ids.reshape(turn_count, group_size)
    current = teleport
    for step_index in range(STEPS):
        propagate_rounded = current.astype(jnp.bfloat16)
        everything = lax.all_gather(propagate_rounded, "node", axis=0, tiled=True)
        feature_table = everything.reshape(owner_count * blocks_dev, quarter, hidden)
        columns = jnp.take(feature_table, global_ids, axis=0)
        column_groups = columns.reshape(turn_count, group_size, quarter, hidden)

        def partial_rows(amount):
            quarters_used = amount // row_count

            def partial_advance(running, inputs):
                weights, sources, targets = inputs
                product = jnp.einsum(
                    "bcr,bch->brh", weights, sources, preferred_element_type=jnp.float32
                )
                product = product.reshape(group_size, quarters_used, quarter, hidden)
                return (running.at[targets].add(product), None)

            start_sum = jnp.zeros((blocks_dev, quarters_used, quarter, hidden), jnp.float32)
            running, _ = lax.scan(
                partial_advance, start_sum, (weight_groups, column_groups, row_groups)
            )
            return running.transpose(1, 0, 2, 3).reshape(amount, hidden)

        current = (
            0.9
            * lax.psum_scatter(
                partial_rows(lax.axis_size("edge") * row_count),
                "edge",
                scatter_dimension=0,
                tiled=True,
            )
            + 0.1 * teleport
        )
    adjoint = cotangent
    gradient = 0.1 * cotangent
    for step_index in range(STEPS):
        rounded = adjoint.astype(jnp.bfloat16).reshape(blocks_dev, quarter, hidden)

        def fold_rows(running, arrived_rows):

            def fold_advance(carried, inputs):
                weights, targets, slot_targets = inputs
                sources = jnp.take(arrived_rows, targets, axis=0)
                product = jnp.einsum(
                    "bcr,brh->bch", weights, sources, preferred_element_type=jnp.float32
                )
                return (carried.at[slot_targets].add(product), None)

            carried, _ = lax.scan(fold_advance, running, (weight_groups, row_groups, slot_groups))
            return carried

        transpose_start_sum = jnp.zeros((slot_total, quarter, hidden), jnp.float32)
        partial_value = fold_rows(
            transpose_start_sum, lax.all_gather(rounded, "edge", axis=1, tiled=True)
        )
        summed = jnp.einsum(
            "sj,sch->jch",
            request_float,
            lax.all_to_all(partial_value, "node", split_axis=0, concat_axis=0, tiled=True),
            precision=lax.Precision.HIGHEST,
        )
        adjoint = 0.9 * summed.reshape(row_count, hidden)
        factor = 0.1 if step_index + 1 < STEPS else 1.0
        gradient = gradient + factor * adjoint
    return (current, gradient)


def per_device(teleport, cotangent, fetch_table, block_row, block_slot, values):
    arguments = (teleport, cotangent, fetch_table, block_row, block_slot, values)
    row_count = teleport.shape[0]
    dense_bytes = fetch_table.shape[1] * row_count * values.shape[3] * 2
    if dense_bytes <= DENSE_BYTES:
        return per_device_dense(*arguments)
    return per_device_blocks(*arguments)


def solution(mesh):
    placed = (
        P(("node", "edge"), None),
        P(("node", "edge"), None),
        P(),
        P("node", None),
        P("node", None),
        P("node", None, "edge", None),
    )
    return jax.shard_map(
        per_device,
        mesh=mesh,
        in_specs=placed,
        out_specs=(P(("node", "edge"), None), P(("node", "edge"), None)),
        check_vma=False,
    )
```

```python
import functools

import jax
import jax.numpy as jnp
from jax import lax
from jax.experimental import pallas as pl
from jax.experimental.pallas import tpu as pltpu
from jax.sharding import PartitionSpec as P

CAP = 2
STEPS = 2
DENSE_BYTES = 8 * 2**20
START_MEBIBYTES = 60
BUILD_MEBIBYTES = 40
LOW = jnp.bfloat16
FULL = jnp.float32

VMEM = pl.BlockSpec(memory_space=pltpu.VMEM)
SMEM = pl.BlockSpec(memory_space=pltpu.SMEM)
HBM = pl.BlockSpec(memory_space=pltpu.HBM)


def params(mebibytes):
    return pltpu.CompilerParams(vmem_limit_bytes=mebibytes * 2**20)


def partner(axis, turn):
    return lax.axis_index(axis) ^ turn


def requested(table, turn, slot):
    column = lax.axis_index("node") * CAP + slot
    return jnp.maximum(table[partner("node", turn), column], 0)


def fill(sends, block):
    for low, send in enumerate(sends):
        for turn in range(send.shape[0]):
            for slot in range(CAP):
                send[turn, slot] = block(2 * turn + low, slot).astype(send.dtype)


def start_kernel(table, teleport, cotangent, *refs):
    *sends, rounded, plan, state, adjoint, sems = refs
    copies = [
        pltpu.make_async_copy(source, target, sems.at[index])
        for index, (source, target) in enumerate(
            ((table, plan), (teleport, state), (cotangent, adjoint))
        )
    ]
    for copy in copies:
        copy.start()
    copies[0].wait()
    copies[1].wait()
    fill(sends, lambda turn, slot: state[requested(plan, turn, slot)])
    copies[2].wait()
    rounded[...] = adjoint[...].astype(LOW)


def build_kernel(rows, slots, weights, high, low, held, total, sems):
    parts = sems.shape[0]
    block_count, quarter, width = held.shape
    chunk = block_count // parts
    copies = [
        pltpu.make_async_copy(
            weights.at[0, pl.ds(part * chunk, chunk)],
            held.at[pl.ds(part * chunk, chunk)],
            sems.at[part],
        )
        for part in range(parts)
    ]
    for copy in copies:
        copy.start()
    total[...] = jnp.zeros_like(total)
    for part, copy in enumerate(copies):
        copy.wait()
        for block in range(part * chunk, (part + 1) * chunk):
            total[slots[0, block], rows[0, block]] += held[block].astype(FULL)
    for slot in range(total.shape[0]):
        for row in range(total.shape[1]):
            place = (pl.ds(slot * quarter, quarter), pl.ds(row * width, width))
            value = total[slot, row]
            rounded = value.astype(LOW)
            high[place] = rounded
            low[place] = (value - rounded.astype(FULL)).astype(LOW)


def pair_kernel(kept, got, *pairs):
    for turn, pair in enumerate(pairs, 1):
        pair[0] = kept[turn]
        pair[1] = got[turn]


def by_turn(parts):
    kept, got, *pairs = parts
    yield 0, kept.at[0]
    yield 1, got.at[0]
    for turn, pair in enumerate(pairs, 1):
        yield 2 * turn, pair.at[0]
        yield 2 * turn + 1, pair.at[1]


def forward_kernel(operators, *refs):
    dense = refs[:operators]
    parts = refs[operators : operators + 1 + refs[operators].shape[0]]
    *partials, source, product = refs[operators + len(parts) :]
    quarters, quarter, hidden = product.shape
    width = quarters * quarter
    for turn, part in by_turn(parts):
        source[partner("node", turn)] = part[...]
    vectors = source[...].reshape(-1, hidden)
    for row in range(partials[0].shape[0]):
        summed = sum(
            lax.dot_general(
                vectors,
                part[:, row * width : (row + 1) * width],
                (((0,), (0,)), ((), ())),
                preferred_element_type=FULL,
            )
            for part in dense
        )
        product[...] = summed.T.reshape(product.shape)
        for turn, partial in zip((0, *range(quarters - 1, 0, -1)), partials):
            partial[row] = product[partner("edge", turn)].astype(partial.dtype)


def adjoint_kernel(operators, *refs):
    *arrived, kept, away, source, product = refs[operators:]
    for turn, part in enumerate(arrived):
        source[:, partner("edge", turn)] = part[...]
    vectors = source[...].reshape(-1, source.shape[-1])
    product[...] = sum(
        jnp.dot(part[...], vectors, preferred_element_type=FULL) for part in refs[:operators]
    ).reshape(product.shape)
    fill((kept, away), lambda turn, slot: product[partner("node", turn), slot])


def state_of(arrived, teleport):
    summed = arrived[0][...]
    for part in arrived[1:]:
        summed += part[...].astype(FULL)
    return 0.9 * summed + 0.1 * teleport[...]


def next_state_kernel(table, teleport, *refs):
    *arrived, kept, away, state = refs
    state[...] = state_of(arrived, teleport)
    fill((kept, away), lambda turn, slot: state[requested(table, turn, slot)])


def last_state_kernel(teleport, *refs):
    *arrived, state = refs
    state[...] = state_of(arrived, teleport)


def gather_adjoint(table, parts, summed):
    summed[...] = jnp.zeros_like(summed)
    for turn, part in by_turn(parts):
        for slot in range(CAP):
            summed[requested(table, turn, slot)] += part[slot].astype(FULL)


def next_adjoint_kernel(table, cotangent, *refs):
    *parts, gradient, rounded, summed = refs
    gather_adjoint(table, parts, summed)
    adjoint = 0.9 * summed[...]
    gradient[...] = 0.1 * cotangent[...] + 0.1 * adjoint
    rounded[...] = adjoint.astype(LOW)


def last_adjoint_kernel(table, gradient_in, *refs):
    *parts, gradient, summed = refs
    gather_adjoint(table, parts, summed)
    gradient[...] = gradient_in[...] + 0.9 * summed[...]


def per_device_dense(teleport, cotangent, fetch_table, block_row, block_slot, values):
    row_count, hidden = teleport.shape
    _, block_count, quarter, width = values.shape
    count = row_count // quarter
    quarters = lax.axis_size("edge")
    slot_total = fetch_table.shape[1]
    owners = lax.axis_size("node")
    shape = (count, quarter, hidden)
    half_shape = (owners // 2, CAP, quarter, hidden)
    pair_shape = (2, CAP, quarter, hidden)
    teleport = teleport.reshape(shape)
    cotangent = cotangent.reshape(shape)

    def call(kernel, operands, places, outs, scratch, mebibytes=8, cost=None):
        return pl.pallas_call(
            kernel,
            out_shape=[jax.ShapeDtypeStruct(*out) for out in outs],
            in_specs=places,
            out_specs=[VMEM] * len(outs),
            scratch_shapes=scratch,
            compiler_params=params(mebibytes),
            cost_estimate=cost,
        )(*operands)

    def after(arrays, others):
        return lax.optimization_barrier((tuple(arrays), tuple(others)))[0]

    def to_node(array, turn):
        return lax.ppermute(array, "node", [(place, place ^ turn) for place in range(owners)])

    def over_node(kept, got):
        pairs = call(
            pair_kernel,
            (kept, got),
            [VMEM] * 2,
            [(pair_shape, LOW)] * (owners // 2 - 1),
            [],
        )
        moved = [to_node(pair, 2 * turn) for turn, pair in enumerate(pairs, 1)]
        return (kept, got, *moved), pairs

    def over_edge(arrays, turns):
        return [arrays[0]] + [
            lax.ppermute(array, "edge", [(place, place ^ turn) for place in range(quarters)])
            for turn, array in zip(turns, arrays[1:])
        ]

    kept, away, rounded = call(
        start_kernel,
        (fetch_table, teleport, cotangent),
        [HBM] * 3,
        [(half_shape, LOW)] * 2 + [(shape, LOW)],
        [
            pltpu.SMEM(fetch_table.shape, fetch_table.dtype),
            pltpu.VMEM(shape, FULL),
            pltpu.VMEM(shape, FULL),
            pltpu.SemaphoreType.DMA((3,)),
        ],
        START_MEBIBYTES,
    )
    got = to_node(away, 1)
    columns, pairs = over_node(kept, got)
    block_row, block_slot = after((block_row, block_slot), pairs)
    dense_shape = (slot_total * quarter, count * width)
    parts = next(size for size in (12, 8, 4, 2, 1) if block_count % size == 0)
    high, low = call(
        build_kernel,
        (block_row, block_slot, values),
        [SMEM, SMEM, HBM],
        [(dense_shape, LOW)] * 2,
        [
            pltpu.VMEM((block_count, quarter, width), LOW),
            pltpu.VMEM((slot_total, count, quarter, width), FULL),
            pltpu.SemaphoreType.DMA((parts,)),
        ],
        BUILD_MEBIBYTES,
        pl.CostEstimate(flops=0, bytes_accessed=values.size * 2, transcendentals=0),
    )

    gradient = cotangent
    for step in range(STEPS):
        last = step + 1 == STEPS
        dense = (high,) if last else (high, low)
        cost = pl.CostEstimate(
            flops=2 * len(dense) * high.size * hidden,
            bytes_accessed=len(dense) * high.size * 2,
            transcendentals=0,
        )
        arrived = over_edge([rounded] * quarters, range(1, quarters))
        if step > 0:
            got = to_node(away, 1)
            (got,) = after((got,), (rounded,))
            columns, _ = over_node(kept, got)
        kept_sums, away_sums = call(
            functools.partial(adjoint_kernel, len(dense)),
            (*dense, *arrived),
            [VMEM] * (quarters + len(dense)),
            [(half_shape, LOW)] * 2,
            [
                pltpu.VMEM((count, quarters, quarter, hidden), LOW),
                pltpu.VMEM((owners, CAP, quarter, hidden), FULL),
            ],
            cost=cost,
        )
        got_sums = to_node(away_sums, 1)
        columns = after(columns, (away_sums,))
        partials = call(
            functools.partial(forward_kernel, len(dense)),
            (*dense, *columns),
            [VMEM] * (len(columns) + len(dense)),
            [(shape, FULL)] + [(shape, LOW)] * (quarters - 1),
            [
                pltpu.VMEM((owners, CAP, quarter, hidden), LOW),
                pltpu.VMEM((quarters, quarter, hidden), FULL),
            ],
            cost=cost,
        )
        (got_sums,) = after((got_sums,), partials[1:])
        transposed, _ = over_node(kept_sums, got_sums)
        partials = over_edge(partials, range(quarters - 1, 0, -1))
        total = [pltpu.VMEM(shape, FULL)]
        if not last:
            kept, away = call(
                next_state_kernel,
                (fetch_table, teleport, *partials),
                [SMEM] + [VMEM] * (1 + quarters),
                [(half_shape, LOW)] * 2,
                total,
            )
            transposed = after(transposed, (away,))
            gradient, rounded = call(
                next_adjoint_kernel,
                (fetch_table, gradient, *transposed),
                [SMEM] + [VMEM] * (1 + len(transposed)),
                [(shape, FULL), (shape, LOW)],
                total,
            )
        else:
            (state,) = call(
                last_state_kernel,
                (teleport, *partials),
                [VMEM] * (1 + quarters),
                [(shape, FULL)],
                [],
            )
            transposed = after(transposed, (state,))
            (gradient,) = call(
                last_adjoint_kernel,
                (fetch_table, gradient, *transposed),
                [SMEM] + [VMEM] * (1 + len(transposed)),
                [(shape, FULL)],
                total,
            )
    return state.reshape(row_count, hidden), gradient.reshape(row_count, hidden)


def per_device_blocks(teleport, cotangent, fetch_table, block_row, block_slot, values):
    row_count, hidden = teleport.shape
    quarter = values.shape[2]
    block_count = values.shape[1]
    blocks_dev = row_count // quarter
    slot_total = fetch_table.shape[1]
    owner_count = lax.axis_size("node")
    group_size = 16
    turn_count = block_count // group_size
    owner_index = lax.axis_index("node")
    local_weights = values[0]
    row_ids = block_row[0]
    slot_ids = block_slot[0]
    own_plan = lax.dynamic_index_in_dim(fetch_table, owner_index, 0, keepdims=False)
    local_ids = jnp.take(own_plan, slot_ids, axis=0)
    global_ids = slot_ids // CAP * blocks_dev + local_ids
    requests = lax.dynamic_slice_in_dim(fetch_table, owner_index * CAP, CAP, 1).reshape(slot_total)
    block_range = jnp.arange(blocks_dev, dtype=jnp.int32)
    request_hot = requests[:, None] == block_range[None, :]
    request_float = request_hot.astype(jnp.float32)
    weight_groups = local_weights.reshape(turn_count, group_size, quarter, local_weights.shape[2])
    row_groups = row_ids.reshape(turn_count, group_size)
    slot_groups = slot_ids.reshape(turn_count, group_size)
    current = teleport
    for step_index in range(STEPS):
        propagate_rounded = current.astype(jnp.bfloat16)
        everything = lax.all_gather(propagate_rounded, "node", axis=0, tiled=True)
        feature_table = everything.reshape(owner_count * blocks_dev, quarter, hidden)
        columns = jnp.take(feature_table, global_ids, axis=0)
        column_groups = columns.reshape(turn_count, group_size, quarter, hidden)

        def partial_rows(amount):
            quarters_used = amount // row_count

            def partial_advance(running, inputs):
                weights, sources, targets = inputs
                product = jnp.einsum(
                    "bcr,bch->brh", weights, sources, preferred_element_type=jnp.float32
                )
                product = product.reshape(group_size, quarters_used, quarter, hidden)
                return (running.at[targets].add(product), None)

            start_sum = jnp.zeros((blocks_dev, quarters_used, quarter, hidden), jnp.float32)
            running, _ = lax.scan(
                partial_advance, start_sum, (weight_groups, column_groups, row_groups)
            )
            return running.transpose(1, 0, 2, 3).reshape(amount, hidden)

        current = (
            0.9
            * lax.psum_scatter(
                partial_rows(lax.axis_size("edge") * row_count),
                "edge",
                scatter_dimension=0,
                tiled=True,
            )
            + 0.1 * teleport
        )
    adjoint = cotangent
    gradient = 0.1 * cotangent
    for step_index in range(STEPS):
        rounded = adjoint.astype(jnp.bfloat16).reshape(blocks_dev, quarter, hidden)

        def fold_rows(running, arrived_rows):

            def fold_advance(carried, inputs):
                weights, targets, slot_targets = inputs
                sources = jnp.take(arrived_rows, targets, axis=0)
                product = jnp.einsum(
                    "bcr,brh->bch", weights, sources, preferred_element_type=jnp.float32
                )
                return (carried.at[slot_targets].add(product), None)

            carried, _ = lax.scan(fold_advance, running, (weight_groups, row_groups, slot_groups))
            return carried

        transpose_start_sum = jnp.zeros((slot_total, quarter, hidden), jnp.float32)
        partial_value = fold_rows(
            transpose_start_sum, lax.all_gather(rounded, "edge", axis=1, tiled=True)
        )
        summed = jnp.einsum(
            "sj,sch->jch",
            request_float,
            lax.all_to_all(partial_value, "node", split_axis=0, concat_axis=0, tiled=True),
            precision=lax.Precision.HIGHEST,
        )
        adjoint = 0.9 * summed.reshape(row_count, hidden)
        factor = 0.1 if step_index + 1 < STEPS else 1.0
        gradient = gradient + factor * adjoint
    return (current, gradient)


def per_device(teleport, cotangent, fetch_table, block_row, block_slot, values):
    arguments = (teleport, cotangent, fetch_table, block_row, block_slot, values)
    row_count = teleport.shape[0]
    dense_bytes = fetch_table.shape[1] * row_count * values.shape[3] * 2
    if dense_bytes <= DENSE_BYTES:
        return per_device_dense(*arguments)
    return per_device_blocks(*arguments)


def solution(mesh):
    placed = (
        P(("node", "edge"), None),
        P(("node", "edge"), None),
        P(),
        P("node", None),
        P("node", None),
        P("node", None, "edge", None),
    )
    return jax.shard_map(
        per_device,
        mesh=mesh,
        in_specs=placed,
        out_specs=(P(("node", "edge"), None), P(("node", "edge"), None)),
        check_vma=False,
    )
```

```python
import functools

import jax
import jax.numpy as jnp
from jax import lax
from jax.experimental import pallas as pl
from jax.experimental.pallas import tpu as pltpu
from jax.sharding import PartitionSpec as P

CAP = 2
STEPS = 2
DENSE_BYTES = 8 * 2**20
START_MEBIBYTES = 60
BUILD_MEBIBYTES = 40
LOW = jnp.bfloat16
FULL = jnp.float32

VMEM = pl.BlockSpec(memory_space=pltpu.VMEM)
SMEM = pl.BlockSpec(memory_space=pltpu.SMEM)
HBM = pl.BlockSpec(memory_space=pltpu.HBM)


def params(mebibytes):
    return pltpu.CompilerParams(vmem_limit_bytes=mebibytes * 2**20)


def partner(axis, turn):
    return lax.axis_index(axis) ^ turn


def requested(table, turn, slot):
    column = lax.axis_index("node") * CAP + slot
    return jnp.maximum(table[partner("node", turn), column], 0)


def fill(sends, block):
    for low, send in enumerate(sends):
        for turn in range(send.shape[0]):
            for slot in range(CAP):
                send[turn, slot] = block(2 * turn + low, slot).astype(send.dtype)


def start_kernel(table, teleport, cotangent, *refs):
    *sends, rounded, plan, state, adjoint, sems = refs
    copies = [
        pltpu.make_async_copy(source, target, sems.at[index])
        for index, (source, target) in enumerate(
            ((table, plan), (teleport, state), (cotangent, adjoint))
        )
    ]
    for copy in copies:
        copy.start()
    copies[0].wait()
    copies[1].wait()
    fill(sends, lambda turn, slot: state[requested(plan, turn, slot)])
    copies[2].wait()
    rounded[...] = adjoint[...].astype(LOW)


def build_kernel(rows, slots, weights, high, low, held, total, sems):
    parts = sems.shape[0]
    block_count, quarter, width = held.shape
    chunk = block_count // parts
    copies = [
        pltpu.make_async_copy(
            weights.at[0, pl.ds(part * chunk, chunk)],
            held.at[pl.ds(part * chunk, chunk)],
            sems.at[part],
        )
        for part in range(parts)
    ]
    for copy in copies:
        copy.start()
    total[...] = jnp.zeros_like(total)
    for part, copy in enumerate(copies):
        copy.wait()
        for block in range(part * chunk, (part + 1) * chunk):
            total[slots[0, block], rows[0, block]] += held[block].astype(FULL)
    for slot in range(total.shape[0]):
        for row in range(total.shape[1]):
            place = (pl.ds(slot * quarter, quarter), pl.ds(row * width, width))
            value = total[slot, row]
            rounded = value.astype(LOW)
            high[place] = rounded
            low[place] = (value - rounded.astype(FULL)).astype(LOW)


def far_first(pairs):
    return zip(range(len(pairs), 0, -1), pairs)


def pair_kernel(kept, got, *pairs):
    for turn, pair in far_first(pairs):
        pair[0] = kept[turn]
        pair[1] = got[turn]


def by_turn(parts):
    kept, got, *pairs = parts
    yield 0, kept.at[0]
    yield 1, got.at[0]
    for turn, pair in far_first(pairs):
        yield 2 * turn, pair.at[0]
        yield 2 * turn + 1, pair.at[1]


def forward_kernel(operators, *refs):
    dense = refs[:operators]
    parts = refs[operators : operators + 1 + refs[operators].shape[0]]
    *partials, source, product = refs[operators + len(parts) :]
    quarters, quarter, hidden = product.shape
    width = quarters * quarter
    for turn, part in by_turn(parts):
        source[partner("node", turn)] = part[...]
    vectors = source[...].reshape(-1, hidden)
    for row in range(partials[0].shape[0]):
        summed = sum(
            lax.dot_general(
                vectors,
                part[:, row * width : (row + 1) * width],
                (((0,), (0,)), ((), ())),
                preferred_element_type=FULL,
            )
            for part in dense
        )
        product[...] = summed.T.reshape(product.shape)
        for turn, partial in zip((0, *range(quarters - 1, 0, -1)), partials):
            partial[row] = product[partner("edge", turn)].astype(partial.dtype)


def adjoint_kernel(operators, *refs):
    *arrived, kept, away, source, product = refs[operators:]
    for turn, part in enumerate(arrived):
        source[:, partner("edge", turn)] = part[...]
    vectors = source[...].reshape(-1, source.shape[-1])
    product[...] = sum(
        jnp.dot(part[...], vectors, preferred_element_type=FULL) for part in refs[:operators]
    ).reshape(product.shape)
    fill((kept, away), lambda turn, slot: product[partner("node", turn), slot])


def state_of(arrived, teleport):
    summed = arrived[0][...]
    for part in arrived[1:]:
        summed += part[...].astype(FULL)
    return 0.9 * summed + 0.1 * teleport[...]


def next_state_kernel(table, teleport, *refs):
    *arrived, kept, away, state = refs
    state[...] = state_of(arrived, teleport)
    fill((kept, away), lambda turn, slot: state[requested(table, turn, slot)])


def last_state_kernel(teleport, *refs):
    *arrived, state = refs
    state[...] = state_of(arrived, teleport)


def gather_adjoint(table, parts, summed):
    summed[...] = jnp.zeros_like(summed)
    for turn, part in by_turn(parts):
        for slot in range(CAP):
            summed[requested(table, turn, slot)] += part[slot].astype(FULL)


def next_adjoint_kernel(table, cotangent, *refs):
    *parts, gradient, rounded, summed = refs
    gather_adjoint(table, parts, summed)
    adjoint = 0.9 * summed[...]
    gradient[...] = 0.1 * cotangent[...] + 0.1 * adjoint
    rounded[...] = adjoint.astype(LOW)


def last_adjoint_kernel(table, gradient_in, *refs):
    *parts, gradient, summed = refs
    gather_adjoint(table, parts, summed)
    gradient[...] = gradient_in[...] + 0.9 * summed[...]


def per_device_dense(teleport, cotangent, fetch_table, block_row, block_slot, values):
    row_count, hidden = teleport.shape
    _, block_count, quarter, width = values.shape
    count = row_count // quarter
    quarters = lax.axis_size("edge")
    slot_total = fetch_table.shape[1]
    owners = lax.axis_size("node")
    shape = (count, quarter, hidden)
    half_shape = (owners // 2, CAP, quarter, hidden)
    pair_shape = (2, CAP, quarter, hidden)
    teleport = teleport.reshape(shape)
    cotangent = cotangent.reshape(shape)

    def call(kernel, operands, places, outs, scratch, mebibytes=8, cost=None):
        return pl.pallas_call(
            kernel,
            out_shape=[jax.ShapeDtypeStruct(*out) for out in outs],
            in_specs=places,
            out_specs=[VMEM] * len(outs),
            scratch_shapes=scratch,
            compiler_params=params(mebibytes),
            cost_estimate=cost,
        )(*operands)

    def after(arrays, others):
        return lax.optimization_barrier((tuple(arrays), tuple(others)))[0]

    def to_node(array, turn):
        return lax.ppermute(array, "node", [(place, place ^ turn) for place in range(owners)])

    def over_node(kept, got):
        pairs = call(
            pair_kernel,
            (kept, got),
            [VMEM] * 2,
            [(pair_shape, LOW)] * (owners // 2 - 1),
            [],
        )
        return (kept, got, *(to_node(pair, 2 * turn) for turn, pair in far_first(pairs)))

    def over_edge(arrays, turns):
        return [arrays[0]] + [
            lax.ppermute(array, "edge", [(place, place ^ turn) for place in range(quarters)])
            for turn, array in zip(turns, arrays[1:])
        ]

    kept, away, rounded = call(
        start_kernel,
        (fetch_table, teleport, cotangent),
        [HBM] * 3,
        [(half_shape, LOW)] * 2 + [(shape, LOW)],
        [
            pltpu.SMEM(fetch_table.shape, fetch_table.dtype),
            pltpu.VMEM(shape, FULL),
            pltpu.VMEM(shape, FULL),
            pltpu.SemaphoreType.DMA((3,)),
        ],
        START_MEBIBYTES,
    )
    dense_shape = (slot_total * quarter, count * width)
    parts = next(size for size in (12, 8, 4, 2, 1) if block_count % size == 0)
    high, low = call(
        build_kernel,
        (block_row, block_slot, values),
        [SMEM, SMEM, HBM],
        [(dense_shape, LOW)] * 2,
        [
            pltpu.VMEM((block_count, quarter, width), LOW),
            pltpu.VMEM((slot_total, count, quarter, width), FULL),
            pltpu.SemaphoreType.DMA((parts,)),
        ],
        BUILD_MEBIBYTES,
        pl.CostEstimate(flops=0, bytes_accessed=values.size * 2, transcendentals=0),
    )

    gradient = cotangent
    for step in range(STEPS):
        last = step + 1 == STEPS
        dense = (high,) if last else (high, low)
        cost = pl.CostEstimate(
            flops=2 * len(dense) * high.size * hidden,
            bytes_accessed=len(dense) * high.size * 2,
            transcendentals=0,
        )
        arrived = over_edge([rounded] * quarters, range(1, quarters))
        got = to_node(away, 1)
        (got,) = after((got,), (rounded, high) if step else (high,))
        columns = over_node(kept, got)
        kept_sums, away_sums = call(
            functools.partial(adjoint_kernel, len(dense)),
            (*dense, *arrived),
            [VMEM] * (quarters + len(dense)),
            [(half_shape, LOW)] * 2,
            [
                pltpu.VMEM((count, quarters, quarter, hidden), LOW),
                pltpu.VMEM((owners, CAP, quarter, hidden), FULL),
            ],
            cost=cost,
        )
        got_sums = to_node(away_sums, 1)
        columns = after(columns, (away_sums,))
        partials = call(
            functools.partial(forward_kernel, len(dense)),
            (*dense, *columns),
            [VMEM] * (len(columns) + len(dense)),
            [(shape, FULL)] + [(shape, LOW)] * (quarters - 1),
            [
                pltpu.VMEM((owners, CAP, quarter, hidden), LOW),
                pltpu.VMEM((quarters, quarter, hidden), FULL),
            ],
            cost=cost,
        )
        (got_sums,) = after((got_sums,), partials[1:])
        transposed = over_node(kept_sums, got_sums)
        partials = over_edge(partials, range(quarters - 1, 0, -1))
        total = [pltpu.VMEM(shape, FULL)]
        if not last:
            kept, away = call(
                next_state_kernel,
                (fetch_table, teleport, *partials),
                [SMEM] + [VMEM] * (1 + quarters),
                [(half_shape, LOW)] * 2,
                total,
            )
            transposed = after(transposed, (away,))
            gradient, rounded = call(
                next_adjoint_kernel,
                (fetch_table, gradient, *transposed),
                [SMEM] + [VMEM] * (1 + len(transposed)),
                [(shape, FULL), (shape, LOW)],
                total,
            )
        else:
            (state,) = call(
                last_state_kernel,
                (teleport, *partials),
                [VMEM] * (1 + quarters),
                [(shape, FULL)],
                [],
            )
            transposed = after(transposed, (state,))
            (gradient,) = call(
                last_adjoint_kernel,
                (fetch_table, gradient, *transposed),
                [SMEM] + [VMEM] * (1 + len(transposed)),
                [(shape, FULL)],
                total,
            )
    return state.reshape(row_count, hidden), gradient.reshape(row_count, hidden)


def per_device_blocks(teleport, cotangent, fetch_table, block_row, block_slot, values):
    row_count, hidden = teleport.shape
    quarter = values.shape[2]
    block_count = values.shape[1]
    blocks_dev = row_count // quarter
    slot_total = fetch_table.shape[1]
    owner_count = lax.axis_size("node")
    group_size = 16
    turn_count = block_count // group_size
    owner_index = lax.axis_index("node")
    local_weights = values[0]
    row_ids = block_row[0]
    slot_ids = block_slot[0]
    own_plan = lax.dynamic_index_in_dim(fetch_table, owner_index, 0, keepdims=False)
    local_ids = jnp.take(own_plan, slot_ids, axis=0)
    global_ids = slot_ids // CAP * blocks_dev + local_ids
    requests = lax.dynamic_slice_in_dim(fetch_table, owner_index * CAP, CAP, 1).reshape(slot_total)
    block_range = jnp.arange(blocks_dev, dtype=jnp.int32)
    request_hot = requests[:, None] == block_range[None, :]
    request_float = request_hot.astype(jnp.float32)
    weight_groups = local_weights.reshape(turn_count, group_size, quarter, local_weights.shape[2])
    row_groups = row_ids.reshape(turn_count, group_size)
    slot_groups = slot_ids.reshape(turn_count, group_size)
    current = teleport
    for step_index in range(STEPS):
        propagate_rounded = current.astype(jnp.bfloat16)
        everything = lax.all_gather(propagate_rounded, "node", axis=0, tiled=True)
        feature_table = everything.reshape(owner_count * blocks_dev, quarter, hidden)
        columns = jnp.take(feature_table, global_ids, axis=0)
        column_groups = columns.reshape(turn_count, group_size, quarter, hidden)

        def partial_rows(amount):
            quarters_used = amount // row_count

            def partial_advance(running, inputs):
                weights, sources, targets = inputs
                product = jnp.einsum(
                    "bcr,bch->brh", weights, sources, preferred_element_type=jnp.float32
                )
                product = product.reshape(group_size, quarters_used, quarter, hidden)
                return (running.at[targets].add(product), None)

            start_sum = jnp.zeros((blocks_dev, quarters_used, quarter, hidden), jnp.float32)
            running, _ = lax.scan(
                partial_advance, start_sum, (weight_groups, column_groups, row_groups)
            )
            return running.transpose(1, 0, 2, 3).reshape(amount, hidden)

        current = (
            0.9
            * lax.psum_scatter(
                partial_rows(lax.axis_size("edge") * row_count),
                "edge",
                scatter_dimension=0,
                tiled=True,
            )
            + 0.1 * teleport
        )
    adjoint = cotangent
    gradient = 0.1 * cotangent
    for step_index in range(STEPS):
        rounded = adjoint.astype(jnp.bfloat16).reshape(blocks_dev, quarter, hidden)

        def fold_rows(running, arrived_rows):

            def fold_advance(carried, inputs):
                weights, targets, slot_targets = inputs
                sources = jnp.take(arrived_rows, targets, axis=0)
                product = jnp.einsum(
                    "bcr,brh->bch", weights, sources, preferred_element_type=jnp.float32
                )
                return (carried.at[slot_targets].add(product), None)

            carried, _ = lax.scan(fold_advance, running, (weight_groups, row_groups, slot_groups))
            return carried

        transpose_start_sum = jnp.zeros((slot_total, quarter, hidden), jnp.float32)
        partial_value = fold_rows(
            transpose_start_sum, lax.all_gather(rounded, "edge", axis=1, tiled=True)
        )
        summed = jnp.einsum(
            "sj,sch->jch",
            request_float,
            lax.all_to_all(partial_value, "node", split_axis=0, concat_axis=0, tiled=True),
            precision=lax.Precision.HIGHEST,
        )
        adjoint = 0.9 * summed.reshape(row_count, hidden)
        factor = 0.1 if step_index + 1 < STEPS else 1.0
        gradient = gradient + factor * adjoint
    return (current, gradient)


def per_device(teleport, cotangent, fetch_table, block_row, block_slot, values):
    arguments = (teleport, cotangent, fetch_table, block_row, block_slot, values)
    row_count = teleport.shape[0]
    dense_bytes = fetch_table.shape[1] * row_count * values.shape[3] * 2
    if dense_bytes <= DENSE_BYTES:
        return per_device_dense(*arguments)
    return per_device_blocks(*arguments)


def solution(mesh):
    placed = (
        P(("node", "edge"), None),
        P(("node", "edge"), None),
        P(),
        P("node", None),
        P("node", None),
        P("node", None, "edge", None),
    )
    return jax.shard_map(
        per_device,
        mesh=mesh,
        in_specs=placed,
        out_specs=(P(("node", "edge"), None), P(("node", "edge"), None)),
        check_vma=False,
    )
```

```python
import functools

import jax
import jax.numpy as jnp
from jax import lax
from jax.experimental import pallas as pl
from jax.experimental.pallas import tpu as pltpu
from jax.sharding import PartitionSpec as P

CAP = 2
STEPS = 2
DENSE_BYTES = 8 * 2**20
START_MEBIBYTES = 60
BUILD_MEBIBYTES = 40
LOW = jnp.bfloat16
FULL = jnp.float32

VMEM = pl.BlockSpec(memory_space=pltpu.VMEM)
SMEM = pl.BlockSpec(memory_space=pltpu.SMEM)
HBM = pl.BlockSpec(memory_space=pltpu.HBM)


def params(mebibytes):
    return pltpu.CompilerParams(vmem_limit_bytes=mebibytes * 2**20)


def partner(axis, turn):
    return lax.axis_index(axis) ^ turn


def requested(table, turn, slot):
    column = lax.axis_index("node") * CAP + slot
    return jnp.maximum(table[partner("node", turn), column], 0)


def fill(sends, block):
    for low, send in enumerate(sends):
        for turn in range(send.shape[0]):
            for slot in range(CAP):
                send[turn, slot] = block(2 * turn + low, slot).astype(send.dtype)


def start_kernel(table, teleport, cotangent, *refs):
    *sends, rounded, plan, state, adjoint, sems = refs
    copies = [
        pltpu.make_async_copy(source, target, sems.at[index])
        for index, (source, target) in enumerate(
            ((table, plan), (teleport, state), (cotangent, adjoint))
        )
    ]
    for copy in copies:
        copy.start()
    copies[0].wait()
    copies[1].wait()
    fill(sends, lambda turn, slot: state[requested(plan, turn, slot)])
    copies[2].wait()
    rounded[...] = adjoint[...].astype(LOW)


def build_kernel(rows, slots, weights, high, low, held, total, sems):
    parts = sems.shape[0]
    block_count, quarter, width = held.shape
    chunk = block_count // parts
    copies = [
        pltpu.make_async_copy(
            weights.at[0, pl.ds(part * chunk, chunk)],
            held.at[pl.ds(part * chunk, chunk)],
            sems.at[part],
        )
        for part in range(parts)
    ]
    for copy in copies:
        copy.start()
    total[...] = jnp.zeros_like(total)
    for part, copy in enumerate(copies):
        copy.wait()
        for block in range(part * chunk, (part + 1) * chunk):
            total[slots[0, block], rows[0, block]] += held[block].astype(FULL)
    for slot in range(total.shape[0]):
        for row in range(total.shape[1]):
            place = (pl.ds(slot * quarter, quarter), pl.ds(row * width, width))
            value = total[slot, row]
            rounded = value.astype(LOW)
            high[place] = rounded
            low[place] = (value - rounded.astype(FULL)).astype(LOW)


def far_first(pairs):
    return zip(range(len(pairs), 0, -1), pairs)


def pair_kernel(kept, got, *pairs):
    for turn, pair in far_first(pairs):
        pair[0] = kept[turn]
        pair[1] = got[turn]


def by_turn(parts):
    kept, got, *pairs = parts
    yield 0, kept.at[0]
    yield 1, got.at[0]
    for turn, pair in far_first(pairs):
        yield 2 * turn, pair.at[0]
        yield 2 * turn + 1, pair.at[1]


def forward_kernel(operators, *refs):
    dense = refs[:operators]
    parts = refs[operators : operators + 1 + refs[operators].shape[0]]
    *owns, away, source, product = refs[operators + len(parts) :]
    quarters, quarter, hidden = product.shape
    width = quarters * quarter
    for turn, part in by_turn(parts):
        source[partner("node", turn)] = part[...]
    vectors = source[...].reshape(-1, hidden)
    for row in range(away.shape[1]):
        summed = sum(
            lax.dot_general(
                vectors,
                part[:, row * width : (row + 1) * width],
                (((0,), (0,)), ((), ())),
                preferred_element_type=FULL,
            )
            for part in dense
        )
        product[...] = summed.T.reshape(product.shape)
        for turn, own in enumerate(owns):
            own[row] = product[partner("edge", 2 * turn)]
            away[turn, row] = product[partner("edge", 2 * turn + 1)].astype(LOW)


def half_sum_kernel(turn, own, got, send):
    send[...] = (own[...] + got[turn].astype(FULL)).astype(LOW)


def adjoint_kernel(operators, *refs):
    *arrived, kept, away, source, product = refs[operators:]
    for turn, part in enumerate(arrived):
        source[:, partner("edge", turn)] = part[...]
    vectors = source[...].reshape(-1, source.shape[-1])
    product[...] = sum(
        jnp.dot(part[...], vectors, preferred_element_type=FULL) for part in refs[:operators]
    ).reshape(product.shape)
    fill((kept, away), lambda turn, slot: product[partner("node", turn), slot])


def state_of(own, got, arrived, teleport):
    summed = own[...] + got[0].astype(FULL)
    for part in arrived:
        summed += part[...].astype(FULL)
    return 0.9 * summed + 0.1 * teleport[...]


def next_state_kernel(table, teleport, own, got, *refs):
    *arrived, kept, away, state = refs
    state[...] = state_of(own, got, arrived, teleport)
    fill((kept, away), lambda turn, slot: state[requested(table, turn, slot)])


def last_state_kernel(teleport, own, got, *refs):
    *arrived, state = refs
    state[...] = state_of(own, got, arrived, teleport)


def gather_adjoint(table, parts, summed):
    summed[...] = jnp.zeros_like(summed)
    for turn, part in by_turn(parts):
        for slot in range(CAP):
            summed[requested(table, turn, slot)] += part[slot].astype(FULL)


def next_adjoint_kernel(table, cotangent, *refs):
    *parts, gradient, rounded, summed = refs
    gather_adjoint(table, parts, summed)
    adjoint = 0.9 * summed[...]
    gradient[...] = 0.1 * cotangent[...] + 0.1 * adjoint
    rounded[...] = adjoint.astype(LOW)


def last_adjoint_kernel(table, gradient_in, *refs):
    *parts, gradient, summed = refs
    gather_adjoint(table, parts, summed)
    gradient[...] = gradient_in[...] + 0.9 * summed[...]


def per_device_dense(teleport, cotangent, fetch_table, block_row, block_slot, values):
    row_count, hidden = teleport.shape
    _, block_count, quarter, width = values.shape
    count = row_count // quarter
    quarters = lax.axis_size("edge")
    slot_total = fetch_table.shape[1]
    owners = lax.axis_size("node")
    shape = (count, quarter, hidden)
    half_shape = (owners // 2, CAP, quarter, hidden)
    pair_shape = (2, CAP, quarter, hidden)
    teleport = teleport.reshape(shape)
    cotangent = cotangent.reshape(shape)

    def call(kernel, operands, places, outs, scratch, mebibytes=8, cost=None):
        return pl.pallas_call(
            kernel,
            out_shape=[jax.ShapeDtypeStruct(*out) for out in outs],
            in_specs=places,
            out_specs=[VMEM] * len(outs),
            scratch_shapes=scratch,
            compiler_params=params(mebibytes),
            cost_estimate=cost,
        )(*operands)

    def after(arrays, others):
        return lax.optimization_barrier((tuple(arrays), tuple(others)))[0]

    def to_node(array, turn):
        return lax.ppermute(array, "node", [(place, place ^ turn) for place in range(owners)])

    def pair_up(kept, got):
        return call(
            pair_kernel,
            (kept, got),
            [VMEM] * 2,
            [(pair_shape, LOW)] * (owners // 2 - 1),
            [],
        )

    def second_hop(pairs):
        return [to_node(pair, 2 * turn) for turn, pair in far_first(pairs)]

    def to_edge(array, turn):
        return lax.ppermute(array, "edge", [(place, place ^ turn) for place in range(quarters)])

    def gather_edge(array, others):
        moved = [to_edge(array, turn) for turn in range(2, quarters, 2)]
        near = to_edge(array, 1)
        moved = after(moved, others)
        return [array, near] + [part for high in moved for part in (high, to_edge(high, 1))]

    def half_sums(owns, got):
        return [
            call(
                functools.partial(half_sum_kernel, turn),
                (own, got),
                [VMEM] * 2,
                [(shape, LOW)],
                [],
            )[0]
            for turn, own in enumerate(owns[1:], 1)
        ]

    kept, away, rounded = call(
        start_kernel,
        (fetch_table, teleport, cotangent),
        [HBM] * 3,
        [(half_shape, LOW)] * 2 + [(shape, LOW)],
        [
            pltpu.SMEM(fetch_table.shape, fetch_table.dtype),
            pltpu.VMEM(shape, FULL),
            pltpu.VMEM(shape, FULL),
            pltpu.SemaphoreType.DMA((3,)),
        ],
        START_MEBIBYTES,
    )
    dense_shape = (slot_total * quarter, count * width)
    parts = next(size for size in (12, 8, 4, 2, 1) if block_count % size == 0)
    high, low = call(
        build_kernel,
        (block_row, block_slot, values),
        [SMEM, SMEM, HBM],
        [(dense_shape, LOW)] * 2,
        [
            pltpu.VMEM((block_count, quarter, width), LOW),
            pltpu.VMEM((slot_total, count, quarter, width), FULL),
            pltpu.SemaphoreType.DMA((parts,)),
        ],
        BUILD_MEBIBYTES,
        pl.CostEstimate(flops=0, bytes_accessed=values.size * 2, transcendentals=0),
    )

    gradient = cotangent
    for step in range(STEPS):
        last = step + 1 == STEPS
        dense = (high,) if last else (high, low)
        cost = pl.CostEstimate(
            flops=4 * high.size * hidden,
            bytes_accessed=2 * high.size * 2,
            transcendentals=0,
        )
        got = to_node(away, 1)
        (got,) = after((got,), (rounded, high) if step else (high,))
        pairs = pair_up(kept, got)
        columns = (kept, got, *second_hop(pairs))
        arrived = gather_edge(rounded, pairs if step else (high,))
        kept_sums, away_sums = call(
            functools.partial(adjoint_kernel, len(dense)),
            (*dense, *arrived),
            [VMEM] * (quarters + len(dense)),
            [(half_shape, LOW)] * 2,
            [
                pltpu.VMEM((count, quarters, quarter, hidden), LOW),
                pltpu.VMEM((owners, CAP, quarter, hidden), FULL),
            ],
            cost=cost,
        )
        got_sums = to_node(away_sums, 1)
        columns = after(columns, (away_sums,))
        *owns, away_rows = call(
            functools.partial(forward_kernel, len(dense)),
            (*dense, *columns),
            [VMEM] * (len(columns) + len(dense)),
            [(shape, FULL)] * (quarters // 2) + [((quarters // 2, *shape), LOW)],
            [
                pltpu.VMEM((owners, CAP, quarter, hidden), LOW),
                pltpu.VMEM((quarters, quarter, hidden), FULL),
            ],
            cost=cost,
        )
        (waiting_rows,) = after((away_rows,), (got_sums,))
        (got_sums,) = after((got_sums,), (away_rows,))
        got_rows = to_edge(waiting_rows, 1)
        *far, near = pair_up(kept_sums, got_sums)
        halves = half_sums(after(owns, (far[0],)), got_rows)
        moved_rows = [to_edge(half, 2 * turn) for turn, half in enumerate(halves, 1)]
        pairs = (*far, *after((near,), halves))
        transposed = (kept_sums, got_sums, *second_hop(pairs))
        partials = (owns[0], got_rows, *moved_rows)
        total = [pltpu.VMEM(shape, FULL)]
        if not last:
            kept, away = call(
                next_state_kernel,
                (fetch_table, teleport, *partials),
                [SMEM] + [VMEM] * (1 + len(partials)),
                [(half_shape, LOW)] * 2,
                total,
            )
            transposed = after(transposed, (away,))
            gradient, rounded = call(
                next_adjoint_kernel,
                (fetch_table, gradient, *transposed),
                [SMEM] + [VMEM] * (1 + len(transposed)),
                [(shape, FULL), (shape, LOW)],
                total,
            )
        else:
            (state,) = call(
                last_state_kernel,
                (teleport, *partials),
                [VMEM] * (1 + len(partials)),
                [(shape, FULL)],
                [],
            )
            transposed = after(transposed, (state,))
            (gradient,) = call(
                last_adjoint_kernel,
                (fetch_table, gradient, *transposed),
                [SMEM] + [VMEM] * (1 + len(transposed)),
                [(shape, FULL)],
                total,
            )
    return state.reshape(row_count, hidden), gradient.reshape(row_count, hidden)


def per_device_blocks(teleport, cotangent, fetch_table, block_row, block_slot, values):
    row_count, hidden = teleport.shape
    quarter = values.shape[2]
    block_count = values.shape[1]
    blocks_dev = row_count // quarter
    slot_total = fetch_table.shape[1]
    owner_count = lax.axis_size("node")
    group_size = 16
    turn_count = block_count // group_size
    owner_index = lax.axis_index("node")
    local_weights = values[0]
    row_ids = block_row[0]
    slot_ids = block_slot[0]
    own_plan = lax.dynamic_index_in_dim(fetch_table, owner_index, 0, keepdims=False)
    local_ids = jnp.take(own_plan, slot_ids, axis=0)
    global_ids = slot_ids // CAP * blocks_dev + local_ids
    requests = lax.dynamic_slice_in_dim(fetch_table, owner_index * CAP, CAP, 1).reshape(slot_total)
    block_range = jnp.arange(blocks_dev, dtype=jnp.int32)
    request_hot = requests[:, None] == block_range[None, :]
    request_float = request_hot.astype(jnp.float32)
    weight_groups = local_weights.reshape(turn_count, group_size, quarter, local_weights.shape[2])
    row_groups = row_ids.reshape(turn_count, group_size)
    slot_groups = slot_ids.reshape(turn_count, group_size)
    current = teleport
    for step_index in range(STEPS):
        propagate_rounded = current.astype(jnp.bfloat16)
        everything = lax.all_gather(propagate_rounded, "node", axis=0, tiled=True)
        feature_table = everything.reshape(owner_count * blocks_dev, quarter, hidden)
        columns = jnp.take(feature_table, global_ids, axis=0)
        column_groups = columns.reshape(turn_count, group_size, quarter, hidden)

        def partial_rows(amount):
            quarters_used = amount // row_count

            def partial_advance(running, inputs):
                weights, sources, targets = inputs
                product = jnp.einsum(
                    "bcr,bch->brh", weights, sources, preferred_element_type=jnp.float32
                )
                product = product.reshape(group_size, quarters_used, quarter, hidden)
                return (running.at[targets].add(product), None)

            start_sum = jnp.zeros((blocks_dev, quarters_used, quarter, hidden), jnp.float32)
            running, _ = lax.scan(
                partial_advance, start_sum, (weight_groups, column_groups, row_groups)
            )
            return running.transpose(1, 0, 2, 3).reshape(amount, hidden)

        current = (
            0.9
            * lax.psum_scatter(
                partial_rows(lax.axis_size("edge") * row_count),
                "edge",
                scatter_dimension=0,
                tiled=True,
            )
            + 0.1 * teleport
        )
    adjoint = cotangent
    gradient = 0.1 * cotangent
    for step_index in range(STEPS):
        rounded = adjoint.astype(jnp.bfloat16).reshape(blocks_dev, quarter, hidden)

        def fold_rows(running, arrived_rows):

            def fold_advance(carried, inputs):
                weights, targets, slot_targets = inputs
                sources = jnp.take(arrived_rows, targets, axis=0)
                product = jnp.einsum(
                    "bcr,brh->bch", weights, sources, preferred_element_type=jnp.float32
                )
                return (carried.at[slot_targets].add(product), None)

            carried, _ = lax.scan(fold_advance, running, (weight_groups, row_groups, slot_groups))
            return carried

        transpose_start_sum = jnp.zeros((slot_total, quarter, hidden), jnp.float32)
        partial_value = fold_rows(
            transpose_start_sum, lax.all_gather(rounded, "edge", axis=1, tiled=True)
        )
        summed = jnp.einsum(
            "sj,sch->jch",
            request_float,
            lax.all_to_all(partial_value, "node", split_axis=0, concat_axis=0, tiled=True),
            precision=lax.Precision.HIGHEST,
        )
        adjoint = 0.9 * summed.reshape(row_count, hidden)
        factor = 0.1 if step_index + 1 < STEPS else 1.0
        gradient = gradient + factor * adjoint
    return (current, gradient)


def per_device(teleport, cotangent, fetch_table, block_row, block_slot, values):
    arguments = (teleport, cotangent, fetch_table, block_row, block_slot, values)
    row_count = teleport.shape[0]
    dense_bytes = fetch_table.shape[1] * row_count * values.shape[3] * 2
    if dense_bytes <= DENSE_BYTES:
        return per_device_dense(*arguments)
    return per_device_blocks(*arguments)


def solution(mesh):
    placed = (
        P(("node", "edge"), None),
        P(("node", "edge"), None),
        P(),
        P("node", None),
        P("node", None),
        P("node", None, "edge", None),
    )
    return jax.shard_map(
        per_device,
        mesh=mesh,
        in_specs=placed,
        out_specs=(P(("node", "edge"), None), P(("node", "edge"), None)),
        check_vma=False,
    )
```

```python
import functools

import jax
import jax.numpy as jnp
from jax import lax
from jax.experimental import pallas as pl
from jax.experimental.pallas import tpu as pltpu
from jax.sharding import PartitionSpec as P

CAP = 2
STEPS = 2
DENSE_BYTES = 8 * 2**20
START_MEBIBYTES = 60
BUILD_MEBIBYTES = 40
IDS_ROOM = 24576
LOW = jnp.bfloat16
FULL = jnp.float32

VMEM = pl.BlockSpec(memory_space=pltpu.VMEM)
SMEM = pl.BlockSpec(memory_space=pltpu.SMEM)
HBM = pl.BlockSpec(memory_space=pltpu.HBM)


def params(mebibytes):
    return pltpu.CompilerParams(vmem_limit_bytes=mebibytes * 2**20)


def partner(axis, turn):
    return lax.axis_index(axis) ^ turn


def requested(table, turn, slot):
    column = lax.axis_index("node") * CAP + slot
    return jnp.maximum(table[partner("node", turn), column], 0)


def fill(sends, block):
    for low, send in enumerate(sends):
        for turn in range(send.shape[0]):
            for slot in range(CAP):
                send[turn, slot] = block(2 * turn + low, slot).astype(send.dtype)


def start_kernel(table, teleport, cotangent, rows, slots, *refs):
    *sends, rounded, ids, plan, state, adjoint, sems = refs
    copies = [
        pltpu.make_async_copy(source, target, sems.at[index])
        for index, (source, target) in enumerate(
            (
                (table, plan),
                (teleport, state),
                (cotangent, adjoint),
                (rows, ids.at[0]),
                (slots, ids.at[1]),
            )
        )
    ]
    for copy in copies:
        copy.start()
    copies[0].wait()
    copies[1].wait()
    fill(sends, lambda turn, slot: state[requested(plan, turn, slot)])
    copies[2].wait()
    rounded[...] = adjoint[...].astype(LOW)
    copies[3].wait()
    copies[4].wait()


def build_kernel(ids, weights, high, low, held, total, own_ids, sems):
    parts = sems.shape[0] - 1
    block_count, quarter, width = held.shape
    chunk = block_count // parts
    copies = [
        pltpu.make_async_copy(
            weights.at[0, pl.ds(part * chunk, chunk)],
            held.at[pl.ds(part * chunk, chunk)],
            sems.at[part],
        )
        for part in range(parts)
    ]
    ids_copy = pltpu.make_async_copy(ids.at[pl.ds(0, 2)], own_ids, sems.at[parts])
    ids_copy.start()
    for copy in copies:
        copy.start()
    total[...] = jnp.zeros_like(total)
    ids_copy.wait()
    for part, copy in enumerate(copies):
        copy.wait()
        for block in range(part * chunk, (part + 1) * chunk):
            total[own_ids[1, 0, block], own_ids[0, 0, block]] += held[block].astype(FULL)
    for slot in range(total.shape[0]):
        for row in range(total.shape[1]):
            place = (pl.ds(slot * quarter, quarter), pl.ds(row * width, width))
            value = total[slot, row]
            rounded = value.astype(LOW)
            high[place] = rounded
            low[place] = (value - rounded.astype(FULL)).astype(LOW)


def far_first(pairs):
    return zip(range(len(pairs), 0, -1), pairs)


def pair_kernel(kept, got, *pairs):
    for turn, pair in far_first(pairs):
        pair[0] = kept[turn]
        pair[1] = got[turn]


def by_turn(parts):
    kept, got, *pairs = parts
    yield 0, kept.at[0]
    yield 1, got.at[0]
    for turn, pair in far_first(pairs):
        yield 2 * turn, pair.at[0]
        yield 2 * turn + 1, pair.at[1]


def forward_kernel(operators, *refs):
    dense = refs[:operators]
    parts = refs[operators : operators + 1 + refs[operators].shape[0]]
    *partials, source, product = refs[operators + len(parts) :]
    quarters, quarter, hidden = product.shape
    width = quarters * quarter
    for turn, part in by_turn(parts):
        source[partner("node", turn)] = part[...]
    vectors = source[...].reshape(-1, hidden)
    for row in range(partials[0].shape[0]):
        summed = sum(
            lax.dot_general(
                vectors,
                part[:, row * width : (row + 1) * width],
                (((0,), (0,)), ((), ())),
                preferred_element_type=FULL,
            )
            for part in dense
        )
        product[...] = summed.T.reshape(product.shape)
        for turn, partial in zip((0, 1, *range(quarters - 1, 1, -1)), partials):
            partial[row] = product[partner("edge", turn)].astype(partial.dtype)


def adjoint_kernel(operators, *refs):
    *arrived, kept, away, source, product = refs[operators:]
    for turn, part in enumerate(arrived):
        source[:, partner("edge", turn)] = part[...]
    vectors = source[...].reshape(-1, source.shape[-1])
    product[...] = sum(
        jnp.dot(part[...], vectors, preferred_element_type=FULL) for part in refs[:operators]
    ).reshape(product.shape)
    fill((kept, away), lambda turn, slot: product[partner("node", turn), slot])


def state_of(arrived, teleport):
    summed = arrived[0][...]
    for part in arrived[1:]:
        summed += part[...].astype(FULL)
    return 0.9 * summed + 0.1 * teleport[...]


def next_state_kernel(table, teleport, *refs):
    *arrived, kept, away, state = refs
    state[...] = state_of(arrived, teleport)
    fill((kept, away), lambda turn, slot: state[requested(table, turn, slot)])


def last_state_kernel(teleport, *refs):
    *arrived, state = refs
    state[...] = state_of(arrived, teleport)


def gather_adjoint(table, parts, summed):
    summed[...] = jnp.zeros_like(summed)
    for turn, part in by_turn(parts):
        for slot in range(CAP):
            summed[requested(table, turn, slot)] += part[slot].astype(FULL)


def next_adjoint_kernel(table, cotangent, *refs):
    *parts, gradient, rounded, summed = refs
    gather_adjoint(table, parts, summed)
    adjoint = 0.9 * summed[...]
    gradient[...] = 0.1 * cotangent[...] + 0.1 * adjoint
    rounded[...] = adjoint.astype(LOW)


def last_adjoint_kernel(table, gradient_in, *refs):
    *parts, gradient, summed = refs
    gather_adjoint(table, parts, summed)
    gradient[...] = gradient_in[...] + 0.9 * summed[...]


def per_device_dense(teleport, cotangent, fetch_table, block_row, block_slot, values):
    row_count, hidden = teleport.shape
    _, block_count, quarter, width = values.shape
    count = row_count // quarter
    quarters = lax.axis_size("edge")
    slot_total = fetch_table.shape[1]
    owners = lax.axis_size("node")
    shape = (count, quarter, hidden)
    half_shape = (owners // 2, CAP, quarter, hidden)
    pair_shape = (2, CAP, quarter, hidden)
    teleport = teleport.reshape(shape)
    cotangent = cotangent.reshape(shape)

    def call(kernel, operands, places, outs, scratch, mebibytes=8, cost=None, places_out=None):
        return pl.pallas_call(
            kernel,
            out_shape=[jax.ShapeDtypeStruct(*out) for out in outs],
            in_specs=places,
            out_specs=places_out or [VMEM] * len(outs),
            scratch_shapes=scratch,
            compiler_params=params(mebibytes),
            cost_estimate=cost,
        )(*operands)

    def after(arrays, others):
        return lax.optimization_barrier((tuple(arrays), tuple(others)))[0]

    def to_node(array, turn):
        return lax.ppermute(array, "node", [(place, place ^ turn) for place in range(owners)])

    def over_node(kept, got):
        pairs = call(
            pair_kernel,
            (kept, got),
            [VMEM] * 2,
            [(pair_shape, LOW)] * (owners // 2 - 1),
            [],
        )
        return (kept, got, *(to_node(pair, 2 * turn) for turn, pair in far_first(pairs)))

    def over_edge(arrays, turns):
        return [arrays[0]] + [
            lax.ppermute(array, "edge", [(place, place ^ turn) for place in range(quarters)])
            for turn, array in zip(turns, arrays[1:])
        ]

    kept, away, rounded, ids = call(
        start_kernel,
        (fetch_table, teleport, cotangent, block_row, block_slot),
        [HBM] * 5,
        [(half_shape, LOW)] * 2
        + [(shape, LOW), ((IDS_ROOM, *block_row.shape), block_row.dtype)],
        [
            pltpu.SMEM(fetch_table.shape, fetch_table.dtype),
            pltpu.VMEM(shape, FULL),
            pltpu.VMEM(shape, FULL),
            pltpu.SemaphoreType.DMA((5,)),
        ],
        START_MEBIBYTES,
        places_out=[VMEM] * 3 + [HBM],
    )
    dense_shape = (slot_total * quarter, count * width)
    parts = next(size for size in (12, 8, 4, 2, 1) if block_count % size == 0)
    high, low = call(
        build_kernel,
        (ids, values),
        [HBM] * 2,
        [(dense_shape, LOW)] * 2,
        [
            pltpu.VMEM((block_count, quarter, width), LOW),
            pltpu.VMEM((slot_total, count, quarter, width), FULL),
            pltpu.SMEM((2, *block_row.shape), block_row.dtype),
            pltpu.SemaphoreType.DMA((parts + 1,)),
        ],
        BUILD_MEBIBYTES,
        pl.CostEstimate(flops=0, bytes_accessed=values.size * 2, transcendentals=0),
    )

    gradient = cotangent
    for step in range(STEPS):
        last = step + 1 == STEPS
        dense = (high,) if last else (high, low)
        cost = pl.CostEstimate(
            flops=2 * len(dense) * high.size * hidden,
            bytes_accessed=len(dense) * high.size * 2,
            transcendentals=0,
        )
        arrived = over_edge([rounded] * quarters, range(1, quarters))
        got = to_node(away, 1)
        (got,) = after((got,), (rounded, high) if step else (high,))
        columns = over_node(kept, got)
        kept_sums, away_sums = call(
            functools.partial(adjoint_kernel, len(dense)),
            (*dense, *arrived),
            [VMEM] * (quarters + len(dense)),
            [(half_shape, LOW)] * 2,
            [
                pltpu.VMEM((count, quarters, quarter, hidden), LOW),
                pltpu.VMEM((owners, CAP, quarter, hidden), FULL),
            ],
            cost=cost,
        )
        got_sums = to_node(away_sums, 1)
        columns = after(columns, (away_sums,))
        partials = call(
            functools.partial(forward_kernel, len(dense)),
            (*dense, *columns),
            [VMEM] * (len(columns) + len(dense)),
            [(shape, FULL)] + [(shape, LOW)] * (quarters - 1),
            [
                pltpu.VMEM((owners, CAP, quarter, hidden), LOW),
                pltpu.VMEM((quarters, quarter, hidden), FULL),
            ],
            cost=cost,
        )
        (got_sums,) = after((got_sums,), partials[1:])
        transposed = over_node(kept_sums, got_sums)
        partials = over_edge(partials, (1, *range(quarters - 1, 1, -1)))
        total = [pltpu.VMEM(shape, FULL)]
        if not last:
            kept, away = call(
                next_state_kernel,
                (fetch_table, teleport, *partials),
                [SMEM] + [VMEM] * (1 + quarters),
                [(half_shape, LOW)] * 2,
                total,
            )
            transposed = after(transposed, (away,))
            gradient, rounded = call(
                next_adjoint_kernel,
                (fetch_table, gradient, *transposed),
                [SMEM] + [VMEM] * (1 + len(transposed)),
                [(shape, FULL), (shape, LOW)],
                total,
            )
        else:
            (state,) = call(
                last_state_kernel,
                (teleport, *partials),
                [VMEM] * (1 + quarters),
                [(shape, FULL)],
                [],
            )
            transposed = after(transposed, (state,))
            (gradient,) = call(
                last_adjoint_kernel,
                (fetch_table, gradient, *transposed),
                [SMEM] + [VMEM] * (1 + len(transposed)),
                [(shape, FULL)],
                total,
            )
    return state.reshape(row_count, hidden), gradient.reshape(row_count, hidden)


def per_device_blocks(teleport, cotangent, fetch_table, block_row, block_slot, values):
    row_count, hidden = teleport.shape
    quarter = values.shape[2]
    block_count = values.shape[1]
    blocks_dev = row_count // quarter
    slot_total = fetch_table.shape[1]
    owner_count = lax.axis_size("node")
    group_size = 16
    turn_count = block_count // group_size
    owner_index = lax.axis_index("node")
    local_weights = values[0]
    row_ids = block_row[0]
    slot_ids = block_slot[0]
    own_plan = lax.dynamic_index_in_dim(fetch_table, owner_index, 0, keepdims=False)
    local_ids = jnp.take(own_plan, slot_ids, axis=0)
    global_ids = slot_ids // CAP * blocks_dev + local_ids
    requests = lax.dynamic_slice_in_dim(fetch_table, owner_index * CAP, CAP, 1).reshape(slot_total)
    block_range = jnp.arange(blocks_dev, dtype=jnp.int32)
    request_hot = requests[:, None] == block_range[None, :]
    request_float = request_hot.astype(jnp.float32)
    weight_groups = local_weights.reshape(turn_count, group_size, quarter, local_weights.shape[2])
    row_groups = row_ids.reshape(turn_count, group_size)
    slot_groups = slot_ids.reshape(turn_count, group_size)
    current = teleport
    for step_index in range(STEPS):
        propagate_rounded = current.astype(jnp.bfloat16)
        everything = lax.all_gather(propagate_rounded, "node", axis=0, tiled=True)
        feature_table = everything.reshape(owner_count * blocks_dev, quarter, hidden)
        columns = jnp.take(feature_table, global_ids, axis=0)
        column_groups = columns.reshape(turn_count, group_size, quarter, hidden)

        def partial_rows(amount):
            quarters_used = amount // row_count

            def partial_advance(running, inputs):
                weights, sources, targets = inputs
                product = jnp.einsum(
                    "bcr,bch->brh", weights, sources, preferred_element_type=jnp.float32
                )
                product = product.reshape(group_size, quarters_used, quarter, hidden)
                return (running.at[targets].add(product), None)

            start_sum = jnp.zeros((blocks_dev, quarters_used, quarter, hidden), jnp.float32)
            running, _ = lax.scan(
                partial_advance, start_sum, (weight_groups, column_groups, row_groups)
            )
            return running.transpose(1, 0, 2, 3).reshape(amount, hidden)

        current = (
            0.9
            * lax.psum_scatter(
                partial_rows(lax.axis_size("edge") * row_count),
                "edge",
                scatter_dimension=0,
                tiled=True,
            )
            + 0.1 * teleport
        )
    adjoint = cotangent
    gradient = 0.1 * cotangent
    for step_index in range(STEPS):
        rounded = adjoint.astype(jnp.bfloat16).reshape(blocks_dev, quarter, hidden)

        def fold_rows(running, arrived_rows):

            def fold_advance(carried, inputs):
                weights, targets, slot_targets = inputs
                sources = jnp.take(arrived_rows, targets, axis=0)
                product = jnp.einsum(
                    "bcr,brh->bch", weights, sources, preferred_element_type=jnp.float32
                )
                return (carried.at[slot_targets].add(product), None)

            carried, _ = lax.scan(fold_advance, running, (weight_groups, row_groups, slot_groups))
            return carried

        transpose_start_sum = jnp.zeros((slot_total, quarter, hidden), jnp.float32)
        partial_value = fold_rows(
            transpose_start_sum, lax.all_gather(rounded, "edge", axis=1, tiled=True)
        )
        summed = jnp.einsum(
            "sj,sch->jch",
            request_float,
            lax.all_to_all(partial_value, "node", split_axis=0, concat_axis=0, tiled=True),
            precision=lax.Precision.HIGHEST,
        )
        adjoint = 0.9 * summed.reshape(row_count, hidden)
        factor = 0.1 if step_index + 1 < STEPS else 1.0
        gradient = gradient + factor * adjoint
    return (current, gradient)


def per_device(teleport, cotangent, fetch_table, block_row, block_slot, values):
    arguments = (teleport, cotangent, fetch_table, block_row, block_slot, values)
    row_count = teleport.shape[0]
    dense_bytes = fetch_table.shape[1] * row_count * values.shape[3] * 2
    if dense_bytes <= DENSE_BYTES:
        return per_device_dense(*arguments)
    return per_device_blocks(*arguments)


def solution(mesh):
    placed = (
        P(("node", "edge"), None),
        P(("node", "edge"), None),
        P(),
        P("node", None),
        P("node", None),
        P("node", None, "edge", None),
    )
    return jax.shard_map(
        per_device,
        mesh=mesh,
        in_specs=placed,
        out_specs=(P(("node", "edge"), None), P(("node", "edge"), None)),
        check_vma=False,
    )
```

```python
import functools

import jax
import jax.numpy as jnp
from jax import lax
from jax.experimental import pallas as pl
from jax.experimental.pallas import tpu as pltpu
from jax.sharding import PartitionSpec as P

CAP = 2
STEPS = 2
DENSE_BYTES = 8 * 2**20
START_MEBIBYTES = 60
BUILD_MEBIBYTES = 40
IDS_ROOM = 24576
LOW = jnp.bfloat16
FULL = jnp.float32

VMEM = pl.BlockSpec(memory_space=pltpu.VMEM)
SMEM = pl.BlockSpec(memory_space=pltpu.SMEM)
HBM = pl.BlockSpec(memory_space=pltpu.HBM)


def params(mebibytes):
    return pltpu.CompilerParams(vmem_limit_bytes=mebibytes * 2**20)


def partner(axis, turn):
    return lax.axis_index(axis) ^ turn


def requested(table, turn, slot):
    column = lax.axis_index("node") * CAP + slot
    return jnp.maximum(table[partner("node", turn), column], 0)


def fill(sends, block):
    for low, send in enumerate(sends):
        for turn in range(send.shape[0]):
            for slot in range(CAP):
                send[turn, slot] = block(2 * turn + low, slot).astype(send.dtype)


def start_kernel(table, teleport, cotangent, rows, slots, *refs):
    *sends, rounded, ids, plan, state, adjoint, sems = refs
    copies = [
        pltpu.make_async_copy(source, target, sems.at[index])
        for index, (source, target) in enumerate(
            (
                (table, plan),
                (teleport, state),
                (cotangent, adjoint),
                (rows, ids.at[0]),
                (slots, ids.at[1]),
            )
        )
    ]
    for copy in copies:
        copy.start()
    copies[0].wait()
    copies[1].wait()
    fill(sends, lambda turn, slot: state[requested(plan, turn, slot)])
    copies[2].wait()
    rounded[...] = adjoint[...].astype(LOW)
    copies[3].wait()
    copies[4].wait()


def build_kernel(ids, weights, high, low, held, total, own_ids, sems):
    parts = sems.shape[0] - 1
    block_count, quarter, width = held.shape
    chunk = block_count // parts
    copies = [
        pltpu.make_async_copy(
            weights.at[0, pl.ds(part * chunk, chunk)],
            held.at[pl.ds(part * chunk, chunk)],
            sems.at[part],
        )
        for part in range(parts)
    ]
    ids_copy = pltpu.make_async_copy(ids.at[pl.ds(0, 2)], own_ids, sems.at[parts])
    ids_copy.start()
    for copy in copies:
        copy.start()
    total[...] = jnp.zeros_like(total)
    ids_copy.wait()
    for part, copy in enumerate(copies):
        copy.wait()
        for block in range(part * chunk, (part + 1) * chunk):
            total[own_ids[1, 0, block], own_ids[0, 0, block]] += held[block].astype(FULL)
    for slot in range(total.shape[0]):
        for row in range(total.shape[1]):
            place = (pl.ds(slot * quarter, quarter), pl.ds(row * width, width))
            value = total[slot, row]
            rounded = value.astype(LOW)
            high[place] = rounded
            low[place] = (value - rounded.astype(FULL)).astype(LOW)


def far_first(pairs):
    return zip(range(len(pairs), 0, -1), pairs)


def pair_kernel(kept, got, *pairs):
    for turn, pair in far_first(pairs):
        pair[0] = kept[turn]
        pair[1] = got[turn]


def by_turn(parts):
    kept, got, *pairs = parts
    yield 0, kept.at[0]
    yield 1, got.at[0]
    for turn, pair in far_first(pairs):
        yield 2 * turn, pair.at[0]
        yield 2 * turn + 1, pair.at[1]


def forward_kernel(operators, *refs):
    dense = refs[:operators]
    parts = refs[operators : operators + 1 + refs[operators].shape[0]]
    *partials, source, product = refs[operators + len(parts) :]
    quarters, quarter, hidden = product.shape
    width = quarters * quarter
    for turn, part in by_turn(parts):
        source[partner("node", turn)] = part[...]
    vectors = source[...].reshape(-1, hidden)
    for row in range(partials[0].shape[0]):
        summed = sum(
            lax.dot_general(
                vectors,
                part[:, row * width : (row + 1) * width],
                (((0,), (0,)), ((), ())),
                preferred_element_type=FULL,
            )
            for part in dense
        )
        product[...] = summed.T.reshape(product.shape)
        for turn, partial in zip((0, 1, *range(quarters - 1, 1, -1)), partials):
            partial[row] = product[partner("edge", turn)].astype(partial.dtype)


def adjoint_kernel(operators, *refs):
    *arrived, kept, away, source, product = refs[operators:]
    for turn, part in enumerate(arrived):
        source[:, partner("edge", turn)] = part[...]
    vectors = source[...].reshape(-1, source.shape[-1]).T
    summed = sum(
        lax.dot_general(vectors, part[...], (((1,), (1,)), ((), ())), preferred_element_type=FULL)
        for part in refs[:operators]
    )
    product[...] = summed.T.reshape(product.shape)
    fill((kept, away), lambda turn, slot: product[partner("node", turn), slot])


def state_of(arrived, teleport):
    summed = arrived[0][...]
    for part in arrived[1:]:
        summed += part[...].astype(FULL)
    return 0.9 * summed + 0.1 * teleport[...]


def next_state_kernel(table, teleport, *refs):
    *arrived, kept, away, state = refs
    state[...] = state_of(arrived, teleport)
    fill((kept, away), lambda turn, slot: state[requested(table, turn, slot)])


def last_state_kernel(teleport, *refs):
    *arrived, state = refs
    state[...] = state_of(arrived, teleport)


def gather_adjoint(table, parts, summed):
    summed[...] = jnp.zeros_like(summed)
    for turn, part in by_turn(parts):
        for slot in range(CAP):
            summed[requested(table, turn, slot)] += part[slot].astype(FULL)


def next_adjoint_kernel(table, cotangent, *refs):
    *parts, gradient, rounded, summed = refs
    gather_adjoint(table, parts, summed)
    adjoint = 0.9 * summed[...]
    gradient[...] = 0.1 * cotangent[...] + 0.1 * adjoint
    rounded[...] = adjoint.astype(LOW)


def last_adjoint_kernel(table, gradient_in, *refs):
    *parts, gradient, summed = refs
    gather_adjoint(table, parts, summed)
    gradient[...] = gradient_in[...] + 0.9 * summed[...]


def per_device_dense(teleport, cotangent, fetch_table, block_row, block_slot, values):
    row_count, hidden = teleport.shape
    _, block_count, quarter, width = values.shape
    count = row_count // quarter
    quarters = lax.axis_size("edge")
    slot_total = fetch_table.shape[1]
    owners = lax.axis_size("node")
    shape = (count, quarter, hidden)
    half_shape = (owners // 2, CAP, quarter, hidden)
    pair_shape = (2, CAP, quarter, hidden)
    teleport = teleport.reshape(shape)
    cotangent = cotangent.reshape(shape)

    def call(kernel, operands, places, outs, scratch, mebibytes=8, cost=None, places_out=None):
        return pl.pallas_call(
            kernel,
            out_shape=[jax.ShapeDtypeStruct(*out) for out in outs],
            in_specs=places,
            out_specs=places_out or [VMEM] * len(outs),
            scratch_shapes=scratch,
            compiler_params=params(mebibytes),
            cost_estimate=cost,
        )(*operands)

    def after(arrays, others):
        return lax.optimization_barrier((tuple(arrays), tuple(others)))[0]

    def to_node(array, turn):
        return lax.ppermute(array, "node", [(place, place ^ turn) for place in range(owners)])

    def over_node(kept, got):
        pairs = call(
            pair_kernel,
            (kept, got),
            [VMEM] * 2,
            [(pair_shape, LOW)] * (owners // 2 - 1),
            [],
        )
        return (kept, got, *(to_node(pair, 2 * turn) for turn, pair in far_first(pairs)))

    def over_edge(arrays, turns):
        return [arrays[0]] + [
            lax.ppermute(array, "edge", [(place, place ^ turn) for place in range(quarters)])
            for turn, array in zip(turns, arrays[1:])
        ]

    kept, away, rounded, ids = call(
        start_kernel,
        (fetch_table, teleport, cotangent, block_row, block_slot),
        [HBM] * 5,
        [(half_shape, LOW)] * 2
        + [(shape, LOW), ((IDS_ROOM, *block_row.shape), block_row.dtype)],
        [
            pltpu.SMEM(fetch_table.shape, fetch_table.dtype),
            pltpu.VMEM(shape, FULL),
            pltpu.VMEM(shape, FULL),
            pltpu.SemaphoreType.DMA((5,)),
        ],
        START_MEBIBYTES,
        places_out=[VMEM] * 3 + [HBM],
    )
    dense_shape = (slot_total * quarter, count * width)
    parts = next(size for size in (12, 8, 4, 2, 1) if block_count % size == 0)
    high, low = call(
        build_kernel,
        (ids, values),
        [HBM] * 2,
        [(dense_shape, LOW)] * 2,
        [
            pltpu.VMEM((block_count, quarter, width), LOW),
            pltpu.VMEM((slot_total, count, quarter, width), FULL),
            pltpu.SMEM((2, *block_row.shape), block_row.dtype),
            pltpu.SemaphoreType.DMA((parts + 1,)),
        ],
        BUILD_MEBIBYTES,
        pl.CostEstimate(flops=0, bytes_accessed=values.size * 2, transcendentals=0),
    )

    gradient = cotangent
    for step in range(STEPS):
        last = step + 1 == STEPS
        dense = (high,) if last else (high, low)
        cost = pl.CostEstimate(
            flops=2 * len(dense) * high.size * hidden,
            bytes_accessed=len(dense) * high.size * 2,
            transcendentals=0,
        )
        arrived = over_edge([rounded] * quarters, range(1, quarters))
        got = to_node(away, 1)
        (got,) = after((got,), (rounded, high) if step else (high,))
        columns = over_node(kept, got)
        kept_sums, away_sums = call(
            functools.partial(adjoint_kernel, len(dense)),
            (*dense, *arrived),
            [VMEM] * (quarters + len(dense)),
            [(half_shape, LOW)] * 2,
            [
                pltpu.VMEM((count, quarters, quarter, hidden), LOW),
                pltpu.VMEM((owners, CAP, quarter, hidden), FULL),
            ],
            cost=cost,
        )
        got_sums = to_node(away_sums, 1)
        columns = after(columns, (away_sums,))
        partials = call(
            functools.partial(forward_kernel, len(dense)),
            (*dense, *columns),
            [VMEM] * (len(columns) + len(dense)),
            [(shape, FULL)] + [(shape, LOW)] * (quarters - 1),
            [
                pltpu.VMEM((owners, CAP, quarter, hidden), LOW),
                pltpu.VMEM((quarters, quarter, hidden), FULL),
            ],
            cost=cost,
        )
        (got_sums,) = after((got_sums,), partials[1:])
        transposed = over_node(kept_sums, got_sums)
        partials = over_edge(partials, (1, *range(quarters - 1, 1, -1)))
        total = [pltpu.VMEM(shape, FULL)]
        if not last:
            kept, away = call(
                next_state_kernel,
                (fetch_table, teleport, *partials),
                [SMEM] + [VMEM] * (1 + quarters),
                [(half_shape, LOW)] * 2,
                total,
            )
            transposed = after(transposed, (away,))
            gradient, rounded = call(
                next_adjoint_kernel,
                (fetch_table, gradient, *transposed),
                [SMEM] + [VMEM] * (1 + len(transposed)),
                [(shape, FULL), (shape, LOW)],
                total,
            )
        else:
            (state,) = call(
                last_state_kernel,
                (teleport, *partials),
                [VMEM] * (1 + quarters),
                [(shape, FULL)],
                [],
            )
            transposed = after(transposed, (state,))
            (gradient,) = call(
                last_adjoint_kernel,
                (fetch_table, gradient, *transposed),
                [SMEM] + [VMEM] * (1 + len(transposed)),
                [(shape, FULL)],
                total,
            )
    return state.reshape(row_count, hidden), gradient.reshape(row_count, hidden)


def per_device_blocks(teleport, cotangent, fetch_table, block_row, block_slot, values):
    row_count, hidden = teleport.shape
    quarter = values.shape[2]
    block_count = values.shape[1]
    blocks_dev = row_count // quarter
    slot_total = fetch_table.shape[1]
    owner_count = lax.axis_size("node")
    group_size = 16
    turn_count = block_count // group_size
    owner_index = lax.axis_index("node")
    local_weights = values[0]
    row_ids = block_row[0]
    slot_ids = block_slot[0]
    own_plan = lax.dynamic_index_in_dim(fetch_table, owner_index, 0, keepdims=False)
    local_ids = jnp.take(own_plan, slot_ids, axis=0)
    global_ids = slot_ids // CAP * blocks_dev + local_ids
    requests = lax.dynamic_slice_in_dim(fetch_table, owner_index * CAP, CAP, 1).reshape(slot_total)
    block_range = jnp.arange(blocks_dev, dtype=jnp.int32)
    request_hot = requests[:, None] == block_range[None, :]
    request_float = request_hot.astype(jnp.float32)
    weight_groups = local_weights.reshape(turn_count, group_size, quarter, local_weights.shape[2])
    row_groups = row_ids.reshape(turn_count, group_size)
    slot_groups = slot_ids.reshape(turn_count, group_size)
    current = teleport
    for step_index in range(STEPS):
        propagate_rounded = current.astype(jnp.bfloat16)
        everything = lax.all_gather(propagate_rounded, "node", axis=0, tiled=True)
        feature_table = everything.reshape(owner_count * blocks_dev, quarter, hidden)
        columns = jnp.take(feature_table, global_ids, axis=0)
        column_groups = columns.reshape(turn_count, group_size, quarter, hidden)

        def partial_rows(amount):
            quarters_used = amount // row_count

            def partial_advance(running, inputs):
                weights, sources, targets = inputs
                product = jnp.einsum(
                    "bcr,bch->brh", weights, sources, preferred_element_type=jnp.float32
                )
                product = product.reshape(group_size, quarters_used, quarter, hidden)
                return (running.at[targets].add(product), None)

            start_sum = jnp.zeros((blocks_dev, quarters_used, quarter, hidden), jnp.float32)
            running, _ = lax.scan(
                partial_advance, start_sum, (weight_groups, column_groups, row_groups)
            )
            return running.transpose(1, 0, 2, 3).reshape(amount, hidden)

        current = (
            0.9
            * lax.psum_scatter(
                partial_rows(lax.axis_size("edge") * row_count),
                "edge",
                scatter_dimension=0,
                tiled=True,
            )
            + 0.1 * teleport
        )
    adjoint = cotangent
    gradient = 0.1 * cotangent
    for step_index in range(STEPS):
        rounded = adjoint.astype(jnp.bfloat16).reshape(blocks_dev, quarter, hidden)

        def fold_rows(running, arrived_rows):

            def fold_advance(carried, inputs):
                weights, targets, slot_targets = inputs
                sources = jnp.take(arrived_rows, targets, axis=0)
                product = jnp.einsum(
                    "bcr,brh->bch", weights, sources, preferred_element_type=jnp.float32
                )
                return (carried.at[slot_targets].add(product), None)

            carried, _ = lax.scan(fold_advance, running, (weight_groups, row_groups, slot_groups))
            return carried

        transpose_start_sum = jnp.zeros((slot_total, quarter, hidden), jnp.float32)
        partial_value = fold_rows(
            transpose_start_sum, lax.all_gather(rounded, "edge", axis=1, tiled=True)
        )
        summed = jnp.einsum(
            "sj,sch->jch",
            request_float,
            lax.all_to_all(partial_value, "node", split_axis=0, concat_axis=0, tiled=True),
            precision=lax.Precision.HIGHEST,
        )
        adjoint = 0.9 * summed.reshape(row_count, hidden)
        factor = 0.1 if step_index + 1 < STEPS else 1.0
        gradient = gradient + factor * adjoint
    return (current, gradient)


def per_device(teleport, cotangent, fetch_table, block_row, block_slot, values):
    arguments = (teleport, cotangent, fetch_table, block_row, block_slot, values)
    row_count = teleport.shape[0]
    dense_bytes = fetch_table.shape[1] * row_count * values.shape[3] * 2
    if dense_bytes <= DENSE_BYTES:
        return per_device_dense(*arguments)
    return per_device_blocks(*arguments)


def solution(mesh):
    placed = (
        P(("node", "edge"), None),
        P(("node", "edge"), None),
        P(),
        P("node", None),
        P("node", None),
        P("node", None, "edge", None),
    )
    return jax.shard_map(
        per_device,
        mesh=mesh,
        in_specs=placed,
        out_specs=(P(("node", "edge"), None), P(("node", "edge"), None)),
        check_vma=False,
    )
```

```python
import functools

import jax
import jax.numpy as jnp
from jax import lax
from jax.experimental import pallas as pl
from jax.experimental.pallas import tpu as pltpu
from jax.sharding import PartitionSpec as P

CAP = 2
STEPS = 2
DENSE_BYTES = 8 * 2**20
START_MEBIBYTES = 60
BUILD_MEBIBYTES = 40
IDS_ROOM = 24576
LOW = jnp.bfloat16
FULL = jnp.float32

VMEM = pl.BlockSpec(memory_space=pltpu.VMEM)
SMEM = pl.BlockSpec(memory_space=pltpu.SMEM)
HBM = pl.BlockSpec(memory_space=pltpu.HBM)


def params(mebibytes):
    return pltpu.CompilerParams(vmem_limit_bytes=mebibytes * 2**20)


def partner(axis, turn):
    return lax.axis_index(axis) ^ turn


def requested(table, turn, slot):
    column = lax.axis_index("node") * CAP + slot
    return jnp.maximum(table[partner("node", turn), column], 0)


def fill(sends, block):
    for low, send in enumerate(sends):
        for turn in range(send.shape[0]):
            for slot in range(CAP):
                send[turn, slot] = block(2 * turn + low, slot).astype(send.dtype)


def start_kernel(table, teleport, cotangent, rows, slots, *refs):
    *sends, rounded, ids, plan, state, adjoint, sems = refs
    copies = [
        pltpu.make_async_copy(source, target, sems.at[index])
        for index, (source, target) in enumerate(
            (
                (table, plan),
                (teleport, state),
                (cotangent, adjoint),
                (rows, ids.at[0]),
                (slots, ids.at[1]),
            )
        )
    ]
    for copy in copies:
        copy.start()
    copies[0].wait()
    copies[1].wait()
    fill(sends, lambda turn, slot: state[requested(plan, turn, slot)])
    copies[2].wait()
    rounded[...] = adjoint[...].astype(LOW)
    copies[3].wait()
    copies[4].wait()


def place_of(turn, owners):
    return turn % 2 * (owners // 2) + turn // 2


def build_kernel(ids, weights, high, low, held, total, own_ids, sems):
    parts = sems.shape[0] - 1
    block_count, quarter, width = held.shape
    chunk = block_count // parts
    owners = total.shape[0] // CAP
    copies = [
        pltpu.make_async_copy(
            weights.at[0, pl.ds(part * chunk, chunk)],
            held.at[pl.ds(part * chunk, chunk)],
            sems.at[part],
        )
        for part in range(parts)
    ]
    ids_copy = pltpu.make_async_copy(ids.at[pl.ds(0, 2)], own_ids, sems.at[parts])
    ids_copy.start()
    for copy in copies:
        copy.start()
    total[...] = jnp.zeros_like(total)
    ids_copy.wait()
    for part, copy in enumerate(copies):
        copy.wait()
        for block in range(part * chunk, (part + 1) * chunk):
            slot = own_ids[1, 0, block]
            place = place_of(partner("node", slot // CAP), owners) * CAP + slot % CAP
            total[place, own_ids[0, 0, block]] += held[block].astype(FULL)
    for slot in range(total.shape[0]):
        for row in range(total.shape[1]):
            place = (pl.ds(slot * quarter, quarter), pl.ds(row * width, width))
            value = total[slot, row]
            rounded = value.astype(LOW)
            high[place] = rounded
            low[place] = (value - rounded.astype(FULL)).astype(LOW)


def far_first(pairs):
    return zip(range(len(pairs), 0, -1), pairs)


def pair_kernel(kept, got, *pairs):
    for turn, pair in far_first(pairs):
        pair[0] = kept[turn]
        pair[1] = got[turn]


def by_turn(parts):
    kept, got, *pairs = parts
    yield 0, kept.at[0]
    yield 1, got.at[0]
    for turn, pair in far_first(pairs):
        yield 2 * turn, pair.at[0]
        yield 2 * turn + 1, pair.at[1]


def forward_kernel(operators, *refs):
    dense = refs[:operators]
    parts = refs[operators : operators + 1 + refs[operators].shape[0]]
    *partials, source, product = refs[operators + len(parts) :]
    quarters, quarter, hidden = product.shape
    width = quarters * quarter
    for turn, part in by_turn(parts):
        source[place_of(turn, source.shape[0])] = part[...]
    vectors = source[...].reshape(-1, hidden)
    for row in range(partials[0].shape[0]):
        summed = sum(
            lax.dot_general(
                vectors,
                part[:, row * width : (row + 1) * width],
                (((0,), (0,)), ((), ())),
                preferred_element_type=FULL,
            )
            for part in dense
        )
        product[...] = summed.T.reshape(product.shape)
        for turn, partial in zip((0, 1, *range(quarters - 1, 1, -1)), partials):
            partial[row] = product[partner("edge", turn)].astype(partial.dtype)


def adjoint_kernel(operators, low, *refs):
    *arrived, send, source = refs[operators:]
    for turn, part in enumerate(arrived):
        source[:, partner("edge", turn)] = part[...]
    vectors = source[...].reshape(-1, source.shape[-1])
    half = refs[0].shape[0] // 2
    product = sum(
        jnp.dot(part[low * half : (low + 1) * half], vectors, preferred_element_type=FULL)
        for part in refs[:operators]
    )
    send[...] = product.reshape(send.shape).astype(LOW)


def state_of(arrived, teleport):
    summed = arrived[0][...]
    for part in arrived[1:]:
        summed += part[...].astype(FULL)
    return 0.9 * summed + 0.1 * teleport[...]


def next_state_kernel(table, teleport, *refs):
    *arrived, kept, away, state = refs
    state[...] = state_of(arrived, teleport)
    fill((kept, away), lambda turn, slot: state[requested(table, turn, slot)])


def last_state_kernel(teleport, *refs):
    *arrived, state = refs
    state[...] = state_of(arrived, teleport)


def gather_adjoint(table, parts, summed):
    summed[...] = jnp.zeros_like(summed)
    for turn, part in by_turn(parts):
        for slot in range(CAP):
            summed[requested(table, turn, slot)] += part[slot].astype(FULL)


def next_adjoint_kernel(table, cotangent, *refs):
    *parts, gradient, rounded, summed = refs
    gather_adjoint(table, parts, summed)
    adjoint = 0.9 * summed[...]
    gradient[...] = 0.1 * cotangent[...] + 0.1 * adjoint
    rounded[...] = adjoint.astype(LOW)


def last_adjoint_kernel(table, gradient_in, *refs):
    *parts, gradient, summed = refs
    gather_adjoint(table, parts, summed)
    gradient[...] = gradient_in[...] + 0.9 * summed[...]


def per_device_dense(teleport, cotangent, fetch_table, block_row, block_slot, values):
    row_count, hidden = teleport.shape
    _, block_count, quarter, width = values.shape
    count = row_count // quarter
    quarters = lax.axis_size("edge")
    slot_total = fetch_table.shape[1]
    owners = lax.axis_size("node")
    shape = (count, quarter, hidden)
    half_shape = (owners // 2, CAP, quarter, hidden)
    pair_shape = (2, CAP, quarter, hidden)
    teleport = teleport.reshape(shape)
    cotangent = cotangent.reshape(shape)

    def call(kernel, operands, places, outs, scratch, mebibytes=8, cost=None, places_out=None):
        return pl.pallas_call(
            kernel,
            out_shape=[jax.ShapeDtypeStruct(*out) for out in outs],
            in_specs=places,
            out_specs=places_out or [VMEM] * len(outs),
            scratch_shapes=scratch,
            compiler_params=params(mebibytes),
            cost_estimate=cost,
        )(*operands)

    def after(arrays, others):
        return lax.optimization_barrier((tuple(arrays), tuple(others)))[0]

    def to_node(array, turn):
        return lax.ppermute(array, "node", [(place, place ^ turn) for place in range(owners)])

    def over_node(kept, got):
        pairs = call(
            pair_kernel,
            (kept, got),
            [VMEM] * 2,
            [(pair_shape, LOW)] * (owners // 2 - 1),
            [],
        )
        return (kept, got, *(to_node(pair, 2 * turn) for turn, pair in far_first(pairs)))

    def over_edge(arrays, turns):
        return [arrays[0]] + [
            lax.ppermute(array, "edge", [(place, place ^ turn) for place in range(quarters)])
            for turn, array in zip(turns, arrays[1:])
        ]

    kept, away, rounded, ids = call(
        start_kernel,
        (fetch_table, teleport, cotangent, block_row, block_slot),
        [HBM] * 5,
        [(half_shape, LOW)] * 2
        + [(shape, LOW), ((IDS_ROOM, *block_row.shape), block_row.dtype)],
        [
            pltpu.SMEM(fetch_table.shape, fetch_table.dtype),
            pltpu.VMEM(shape, FULL),
            pltpu.VMEM(shape, FULL),
            pltpu.SemaphoreType.DMA((5,)),
        ],
        START_MEBIBYTES,
        places_out=[VMEM] * 3 + [HBM],
    )
    dense_shape = (slot_total * quarter, count * width)
    parts = next(size for size in (12, 8, 4, 2, 1) if block_count % size == 0)
    high, low = call(
        build_kernel,
        (ids, values),
        [HBM] * 2,
        [(dense_shape, LOW)] * 2,
        [
            pltpu.VMEM((block_count, quarter, width), LOW),
            pltpu.VMEM((slot_total, count, quarter, width), FULL),
            pltpu.SMEM((2, *block_row.shape), block_row.dtype),
            pltpu.SemaphoreType.DMA((parts + 1,)),
        ],
        BUILD_MEBIBYTES,
        pl.CostEstimate(flops=0, bytes_accessed=values.size * 2, transcendentals=0),
    )

    gradient = cotangent
    for step in range(STEPS):
        last = step + 1 == STEPS
        dense = (high,) if last else (high, low)
        cells = len(dense) * high.size
        half_cost, cost = (
            pl.CostEstimate(
                flops=2 * part * hidden, bytes_accessed=2 * part, transcendentals=0
            )
            for part in (cells // 2, cells)
        )
        arrived = over_edge([rounded] * quarters, range(1, quarters))
        got = to_node(away, 1)
        (got,) = after((got,), (rounded, high) if step else (high,))
        columns = over_node(kept, got)
        def adjoint_half(low, rows):
            return call(
                functools.partial(adjoint_kernel, len(dense), low),
                (*dense, *rows),
                [VMEM] * (quarters + len(dense)),
                [(half_shape, LOW)],
                [pltpu.VMEM((count, quarters, quarter, hidden), LOW)],
                cost=half_cost,
            )[0]

        away_sums = adjoint_half(1, arrived)
        kept_sums = adjoint_half(0, after(arrived, (away_sums,)))
        got_sums = to_node(away_sums, 1)
        columns = after(columns, (kept_sums,))
        partials = call(
            functools.partial(forward_kernel, len(dense)),
            (*dense, *columns),
            [VMEM] * (len(columns) + len(dense)),
            [(shape, FULL)] + [(shape, LOW)] * (quarters - 1),
            [
                pltpu.VMEM((owners, CAP, quarter, hidden), LOW),
                pltpu.VMEM((quarters, quarter, hidden), FULL),
            ],
            cost=cost,
        )
        (got_sums,) = after((got_sums,), partials[1:])
        transposed = over_node(kept_sums, got_sums)
        partials = over_edge(partials, (1, *range(quarters - 1, 1, -1)))
        total = [pltpu.VMEM(shape, FULL)]
        if not last:
            kept, away = call(
                next_state_kernel,
                (fetch_table, teleport, *partials),
                [SMEM] + [VMEM] * (1 + quarters),
                [(half_shape, LOW)] * 2,
                total,
            )
            transposed = after(transposed, (away,))
            gradient, rounded = call(
                next_adjoint_kernel,
                (fetch_table, gradient, *transposed),
                [SMEM] + [VMEM] * (1 + len(transposed)),
                [(shape, FULL), (shape, LOW)],
                total,
            )
        else:
            (state,) = call(
                last_state_kernel,
                (teleport, *partials),
                [VMEM] * (1 + quarters),
                [(shape, FULL)],
                [],
            )
            transposed = after(transposed, (state,))
            (gradient,) = call(
                last_adjoint_kernel,
                (fetch_table, gradient, *transposed),
                [SMEM] + [VMEM] * (1 + len(transposed)),
                [(shape, FULL)],
                total,
            )
    return state.reshape(row_count, hidden), gradient.reshape(row_count, hidden)


def per_device_blocks(teleport, cotangent, fetch_table, block_row, block_slot, values):
    row_count, hidden = teleport.shape
    quarter = values.shape[2]
    block_count = values.shape[1]
    blocks_dev = row_count // quarter
    slot_total = fetch_table.shape[1]
    owner_count = lax.axis_size("node")
    group_size = 16
    turn_count = block_count // group_size
    owner_index = lax.axis_index("node")
    local_weights = values[0]
    row_ids = block_row[0]
    slot_ids = block_slot[0]
    own_plan = lax.dynamic_index_in_dim(fetch_table, owner_index, 0, keepdims=False)
    local_ids = jnp.take(own_plan, slot_ids, axis=0)
    global_ids = slot_ids // CAP * blocks_dev + local_ids
    requests = lax.dynamic_slice_in_dim(fetch_table, owner_index * CAP, CAP, 1).reshape(slot_total)
    block_range = jnp.arange(blocks_dev, dtype=jnp.int32)
    request_hot = requests[:, None] == block_range[None, :]
    request_float = request_hot.astype(jnp.float32)
    weight_groups = local_weights.reshape(turn_count, group_size, quarter, local_weights.shape[2])
    row_groups = row_ids.reshape(turn_count, group_size)
    slot_groups = slot_ids.reshape(turn_count, group_size)
    current = teleport
    for step_index in range(STEPS):
        propagate_rounded = current.astype(jnp.bfloat16)
        everything = lax.all_gather(propagate_rounded, "node", axis=0, tiled=True)
        feature_table = everything.reshape(owner_count * blocks_dev, quarter, hidden)
        columns = jnp.take(feature_table, global_ids, axis=0)
        column_groups = columns.reshape(turn_count, group_size, quarter, hidden)

        def partial_rows(amount):
            quarters_used = amount // row_count

            def partial_advance(running, inputs):
                weights, sources, targets = inputs
                product = jnp.einsum(
                    "bcr,bch->brh", weights, sources, preferred_element_type=jnp.float32
                )
                product = product.reshape(group_size, quarters_used, quarter, hidden)
                return (running.at[targets].add(product), None)

            start_sum = jnp.zeros((blocks_dev, quarters_used, quarter, hidden), jnp.float32)
            running, _ = lax.scan(
                partial_advance, start_sum, (weight_groups, column_groups, row_groups)
            )
            return running.transpose(1, 0, 2, 3).reshape(amount, hidden)

        current = (
            0.9
            * lax.psum_scatter(
                partial_rows(lax.axis_size("edge") * row_count),
                "edge",
                scatter_dimension=0,
                tiled=True,
            )
            + 0.1 * teleport
        )
    adjoint = cotangent
    gradient = 0.1 * cotangent
    for step_index in range(STEPS):
        rounded = adjoint.astype(jnp.bfloat16).reshape(blocks_dev, quarter, hidden)

        def fold_rows(running, arrived_rows):

            def fold_advance(carried, inputs):
                weights, targets, slot_targets = inputs
                sources = jnp.take(arrived_rows, targets, axis=0)
                product = jnp.einsum(
                    "bcr,brh->bch", weights, sources, preferred_element_type=jnp.float32
                )
                return (carried.at[slot_targets].add(product), None)

            carried, _ = lax.scan(fold_advance, running, (weight_groups, row_groups, slot_groups))
            return carried

        transpose_start_sum = jnp.zeros((slot_total, quarter, hidden), jnp.float32)
        partial_value = fold_rows(
            transpose_start_sum, lax.all_gather(rounded, "edge", axis=1, tiled=True)
        )
        summed = jnp.einsum(
            "sj,sch->jch",
            request_float,
            lax.all_to_all(partial_value, "node", split_axis=0, concat_axis=0, tiled=True),
            precision=lax.Precision.HIGHEST,
        )
        adjoint = 0.9 * summed.reshape(row_count, hidden)
        factor = 0.1 if step_index + 1 < STEPS else 1.0
        gradient = gradient + factor * adjoint
    return (current, gradient)


def per_device(teleport, cotangent, fetch_table, block_row, block_slot, values):
    arguments = (teleport, cotangent, fetch_table, block_row, block_slot, values)
    row_count = teleport.shape[0]
    dense_bytes = fetch_table.shape[1] * row_count * values.shape[3] * 2
    if dense_bytes <= DENSE_BYTES:
        return per_device_dense(*arguments)
    return per_device_blocks(*arguments)


def solution(mesh):
    placed = (
        P(("node", "edge"), None),
        P(("node", "edge"), None),
        P(),
        P("node", None),
        P("node", None),
        P("node", None, "edge", None),
    )
    return jax.shard_map(
        per_device,
        mesh=mesh,
        in_specs=placed,
        out_specs=(P(("node", "edge"), None), P(("node", "edge"), None)),
        check_vma=False,
    )
```

```python
import functools

import jax
import jax.numpy as jnp
from jax import lax
from jax.experimental import pallas as pl
from jax.experimental.pallas import tpu as pltpu
from jax.sharding import PartitionSpec as P

CAP = 2
STEPS = 2
DENSE_BYTES = 8 * 2**20
START_MEBIBYTES = 60
BUILD_MEBIBYTES = 40
IDS_ROOM = 24576
LOW = jnp.bfloat16
FULL = jnp.float32

VMEM = pl.BlockSpec(memory_space=pltpu.VMEM)
SMEM = pl.BlockSpec(memory_space=pltpu.SMEM)
HBM = pl.BlockSpec(memory_space=pltpu.HBM)


def params(mebibytes):
    return pltpu.CompilerParams(vmem_limit_bytes=mebibytes * 2**20)


def partner(axis, turn):
    return lax.axis_index(axis) ^ turn


def requested(table, turn, slot):
    column = lax.axis_index("node") * CAP + slot
    return jnp.maximum(table[partner("node", turn), column], 0)


def fill(sends, block):
    for low, send in enumerate(sends):
        for turn in range(send.shape[0]):
            for slot in range(CAP):
                send[turn, slot] = block(2 * turn + low, slot).astype(send.dtype)


def start_kernel(table, teleport, cotangent, rows, slots, *refs):
    *sends, rounded, ids, plan, state, adjoint, sems = refs
    copies = [
        pltpu.make_async_copy(source, target, sems.at[index])
        for index, (source, target) in enumerate(
            (
                (table, plan),
                (teleport, state),
                (cotangent, adjoint),
                (rows, ids.at[0]),
                (slots, ids.at[1]),
            )
        )
    ]
    for copy in copies:
        copy.start()
    copies[0].wait()
    copies[1].wait()
    fill(sends, lambda turn, slot: state[requested(plan, turn, slot)])
    copies[2].wait()
    rounded[...] = adjoint[...].astype(LOW)
    copies[3].wait()
    copies[4].wait()


def place_of(turn, owners):
    return (turn & 1) * (owners // 2) + (turn >> 1)


def build_kernel(ids, weights, high, low, held, total, own_ids, places, sems):
    parts = sems.shape[0] - 1
    block_count, quarter, width = held.shape
    chunk = block_count // parts
    owners = total.shape[0] // CAP
    copies = [
        pltpu.make_async_copy(
            weights.at[0, pl.ds(part * chunk, chunk)],
            held.at[pl.ds(part * chunk, chunk)],
            sems.at[part],
        )
        for part in range(parts)
    ]
    ids_copy = pltpu.make_async_copy(ids.at[pl.ds(0, 2)], own_ids, sems.at[parts])
    ids_copy.start()
    for copy in copies:
        copy.start()
    for slot in range(total.shape[0]):
        places[slot] = place_of(partner("node", slot // CAP), owners) * CAP + slot % CAP
    total[...] = jnp.zeros_like(total)
    ids_copy.wait()
    for part, copy in enumerate(copies):
        copy.wait()
        for block in range(part * chunk, (part + 1) * chunk):
            total[places[own_ids[1, 0, block]], own_ids[0, 0, block]] += held[block].astype(FULL)
    for slot in range(total.shape[0]):
        for row in range(total.shape[1]):
            place = (pl.ds(slot * quarter, quarter), pl.ds(row * width, width))
            value = total[slot, row]
            rounded = value.astype(LOW)
            high[place] = rounded
            low[place] = (value - rounded.astype(FULL)).astype(LOW)


def far_first(pairs):
    return zip(range(len(pairs), 0, -1), pairs)


def pair_kernel(kept, got, *pairs):
    for turn, pair in far_first(pairs):
        pair[0] = kept[turn]
        pair[1] = got[turn]


def by_turn(parts):
    kept, got, *pairs = parts
    yield 0, kept.at[0]
    yield 1, got.at[0]
    for turn, pair in far_first(pairs):
        yield 2 * turn, pair.at[0]
        yield 2 * turn + 1, pair.at[1]


def forward_kernel(operators, *refs):
    dense = refs[:operators]
    parts = refs[operators : operators + 1 + refs[operators].shape[0]]
    *partials, source, product = refs[operators + len(parts) :]
    quarters, quarter, hidden = product.shape
    width = quarters * quarter
    for turn, part in by_turn(parts):
        source[place_of(turn, source.shape[0])] = part[...]
    vectors = source[...].reshape(-1, hidden)
    for row in range(partials[0].shape[0]):
        summed = sum(
            lax.dot_general(
                vectors,
                part[:, row * width : (row + 1) * width],
                (((0,), (0,)), ((), ())),
                preferred_element_type=FULL,
            )
            for part in dense
        )
        product[...] = summed.T.reshape(product.shape)
        for turn, partial in zip((0, 1, *range(quarters - 1, 1, -1)), partials):
            partial[row] = product[partner("edge", turn)].astype(partial.dtype)


def adjoint_kernel(operators, low, *refs):
    *arrived, send, source = refs[operators:]
    for turn, part in enumerate(arrived):
        source[:, partner("edge", turn)] = part[...]
    vectors = source[...].reshape(-1, source.shape[-1])
    half = refs[0].shape[0] // 2
    product = sum(
        jnp.dot(part[low * half : (low + 1) * half], vectors, preferred_element_type=FULL)
        for part in refs[:operators]
    )
    send[...] = product.reshape(send.shape).astype(LOW)


def state_of(arrived, teleport):
    summed = arrived[0][...]
    for part in arrived[1:]:
        summed += part[...].astype(FULL)
    return 0.9 * summed + 0.1 * teleport[...]


def next_state_kernel(table, teleport, *refs):
    *arrived, kept, away, state = refs
    state[...] = state_of(arrived, teleport)
    fill((kept, away), lambda turn, slot: state[requested(table, turn, slot)])


def last_state_kernel(teleport, *refs):
    *arrived, state = refs
    state[...] = state_of(arrived, teleport)


def gather_adjoint(table, parts, summed):
    summed[...] = jnp.zeros_like(summed)
    for turn, part in by_turn(parts):
        for slot in range(CAP):
            summed[requested(table, turn, slot)] += part[slot].astype(FULL)


def next_adjoint_kernel(table, cotangent, *refs):
    *parts, gradient, rounded, summed = refs
    gather_adjoint(table, parts, summed)
    adjoint = 0.9 * summed[...]
    gradient[...] = 0.1 * cotangent[...] + 0.1 * adjoint
    rounded[...] = adjoint.astype(LOW)


def last_adjoint_kernel(table, gradient_in, *refs):
    *parts, gradient, summed = refs
    gather_adjoint(table, parts, summed)
    gradient[...] = gradient_in[...] + 0.9 * summed[...]


def per_device_dense(teleport, cotangent, fetch_table, block_row, block_slot, values):
    row_count, hidden = teleport.shape
    _, block_count, quarter, width = values.shape
    count = row_count // quarter
    quarters = lax.axis_size("edge")
    slot_total = fetch_table.shape[1]
    owners = lax.axis_size("node")
    shape = (count, quarter, hidden)
    half_shape = (owners // 2, CAP, quarter, hidden)
    pair_shape = (2, CAP, quarter, hidden)
    teleport = teleport.reshape(shape)
    cotangent = cotangent.reshape(shape)

    def call(kernel, operands, places, outs, scratch, mebibytes=8, cost=None, places_out=None):
        return pl.pallas_call(
            kernel,
            out_shape=[jax.ShapeDtypeStruct(*out) for out in outs],
            in_specs=places,
            out_specs=places_out or [VMEM] * len(outs),
            scratch_shapes=scratch,
            compiler_params=params(mebibytes),
            cost_estimate=cost,
        )(*operands)

    def after(arrays, others):
        return lax.optimization_barrier((tuple(arrays), tuple(others)))[0]

    def to_node(array, turn):
        return lax.ppermute(array, "node", [(place, place ^ turn) for place in range(owners)])

    def over_node(kept, got):
        pairs = call(
            pair_kernel,
            (kept, got),
            [VMEM] * 2,
            [(pair_shape, LOW)] * (owners // 2 - 1),
            [],
        )
        return (kept, got, *(to_node(pair, 2 * turn) for turn, pair in far_first(pairs)))

    def over_edge(arrays, turns):
        return [arrays[0]] + [
            lax.ppermute(array, "edge", [(place, place ^ turn) for place in range(quarters)])
            for turn, array in zip(turns, arrays[1:])
        ]

    kept, away, rounded, ids = call(
        start_kernel,
        (fetch_table, teleport, cotangent, block_row, block_slot),
        [HBM] * 5,
        [(half_shape, LOW)] * 2
        + [(shape, LOW), ((IDS_ROOM, *block_row.shape), block_row.dtype)],
        [
            pltpu.SMEM(fetch_table.shape, fetch_table.dtype),
            pltpu.VMEM(shape, FULL),
            pltpu.VMEM(shape, FULL),
            pltpu.SemaphoreType.DMA((5,)),
        ],
        START_MEBIBYTES,
        places_out=[VMEM] * 3 + [HBM],
    )
    dense_shape = (slot_total * quarter, count * width)
    parts = next(size for size in (12, 8, 4, 2, 1) if block_count % size == 0)
    high, low = call(
        build_kernel,
        (ids, values),
        [HBM] * 2,
        [(dense_shape, LOW)] * 2,
        [
            pltpu.VMEM((block_count, quarter, width), LOW),
            pltpu.VMEM((slot_total, count, quarter, width), FULL),
            pltpu.SMEM((2, *block_row.shape), block_row.dtype),
            pltpu.SMEM((slot_total,), block_row.dtype),
            pltpu.SemaphoreType.DMA((parts + 1,)),
        ],
        BUILD_MEBIBYTES,
        pl.CostEstimate(flops=0, bytes_accessed=values.size * 2, transcendentals=0),
    )

    gradient = cotangent
    for step in range(STEPS):
        last = step + 1 == STEPS
        dense = (high,) if last else (high, low)
        cells = len(dense) * high.size
        half_cost, cost = (
            pl.CostEstimate(
                flops=2 * part * hidden, bytes_accessed=2 * part, transcendentals=0
            )
            for part in (cells // 2, cells)
        )
        arrived = over_edge([rounded] * quarters, range(1, quarters))
        got = to_node(away, 1)
        (got,) = after((got,), (rounded, high) if step else (high,))
        columns = over_node(kept, got)
        def adjoint_half(low, rows):
            return call(
                functools.partial(adjoint_kernel, len(dense), low),
                (*dense, *rows),
                [VMEM] * (quarters + len(dense)),
                [(half_shape, LOW)],
                [pltpu.VMEM((count, quarters, quarter, hidden), LOW)],
                cost=half_cost,
            )[0]

        away_sums = adjoint_half(1, arrived)
        kept_sums = adjoint_half(0, after(arrived, (away_sums,)))
        got_sums = to_node(away_sums, 1)
        columns = after(columns, (kept_sums,))
        partials = call(
            functools.partial(forward_kernel, len(dense)),
            (*dense, *columns),
            [VMEM] * (len(columns) + len(dense)),
            [(shape, FULL)] + [(shape, LOW)] * (quarters - 1),
            [
                pltpu.VMEM((owners, CAP, quarter, hidden), LOW),
                pltpu.VMEM((quarters, quarter, hidden), FULL),
            ],
            cost=cost,
        )
        (got_sums,) = after((got_sums,), partials[1:])
        transposed = over_node(kept_sums, got_sums)
        partials = over_edge(partials, (1, *range(quarters - 1, 1, -1)))
        total = [pltpu.VMEM(shape, FULL)]
        if not last:
            kept, away = call(
                next_state_kernel,
                (fetch_table, teleport, *partials),
                [SMEM] + [VMEM] * (1 + quarters),
                [(half_shape, LOW)] * 2,
                total,
            )
            transposed = after(transposed, (away,))
            gradient, rounded = call(
                next_adjoint_kernel,
                (fetch_table, gradient, *transposed),
                [SMEM] + [VMEM] * (1 + len(transposed)),
                [(shape, FULL), (shape, LOW)],
                total,
            )
        else:
            (state,) = call(
                last_state_kernel,
                (teleport, *partials),
                [VMEM] * (1 + quarters),
                [(shape, FULL)],
                [],
            )
            transposed = after(transposed, (state,))
            (gradient,) = call(
                last_adjoint_kernel,
                (fetch_table, gradient, *transposed),
                [SMEM] + [VMEM] * (1 + len(transposed)),
                [(shape, FULL)],
                total,
            )
    return state.reshape(row_count, hidden), gradient.reshape(row_count, hidden)


def per_device_blocks(teleport, cotangent, fetch_table, block_row, block_slot, values):
    row_count, hidden = teleport.shape
    quarter = values.shape[2]
    block_count = values.shape[1]
    blocks_dev = row_count // quarter
    slot_total = fetch_table.shape[1]
    owner_count = lax.axis_size("node")
    group_size = 16
    turn_count = block_count // group_size
    owner_index = lax.axis_index("node")
    local_weights = values[0]
    row_ids = block_row[0]
    slot_ids = block_slot[0]
    own_plan = lax.dynamic_index_in_dim(fetch_table, owner_index, 0, keepdims=False)
    local_ids = jnp.take(own_plan, slot_ids, axis=0)
    global_ids = slot_ids // CAP * blocks_dev + local_ids
    requests = lax.dynamic_slice_in_dim(fetch_table, owner_index * CAP, CAP, 1).reshape(slot_total)
    block_range = jnp.arange(blocks_dev, dtype=jnp.int32)
    request_hot = requests[:, None] == block_range[None, :]
    request_float = request_hot.astype(jnp.float32)
    weight_groups = local_weights.reshape(turn_count, group_size, quarter, local_weights.shape[2])
    row_groups = row_ids.reshape(turn_count, group_size)
    slot_groups = slot_ids.reshape(turn_count, group_size)
    current = teleport
    for step_index in range(STEPS):
        propagate_rounded = current.astype(jnp.bfloat16)
        everything = lax.all_gather(propagate_rounded, "node", axis=0, tiled=True)
        feature_table = everything.reshape(owner_count * blocks_dev, quarter, hidden)
        columns = jnp.take(feature_table, global_ids, axis=0)
        column_groups = columns.reshape(turn_count, group_size, quarter, hidden)

        def partial_rows(amount):
            quarters_used = amount // row_count

            def partial_advance(running, inputs):
                weights, sources, targets = inputs
                product = jnp.einsum(
                    "bcr,bch->brh", weights, sources, preferred_element_type=jnp.float32
                )
                product = product.reshape(group_size, quarters_used, quarter, hidden)
                return (running.at[targets].add(product), None)

            start_sum = jnp.zeros((blocks_dev, quarters_used, quarter, hidden), jnp.float32)
            running, _ = lax.scan(
                partial_advance, start_sum, (weight_groups, column_groups, row_groups)
            )
            return running.transpose(1, 0, 2, 3).reshape(amount, hidden)

        current = (
            0.9
            * lax.psum_scatter(
                partial_rows(lax.axis_size("edge") * row_count),
                "edge",
                scatter_dimension=0,
                tiled=True,
            )
            + 0.1 * teleport
        )
    adjoint = cotangent
    gradient = 0.1 * cotangent
    for step_index in range(STEPS):
        rounded = adjoint.astype(jnp.bfloat16).reshape(blocks_dev, quarter, hidden)

        def fold_rows(running, arrived_rows):

            def fold_advance(carried, inputs):
                weights, targets, slot_targets = inputs
                sources = jnp.take(arrived_rows, targets, axis=0)
                product = jnp.einsum(
                    "bcr,brh->bch", weights, sources, preferred_element_type=jnp.float32
                )
                return (carried.at[slot_targets].add(product), None)

            carried, _ = lax.scan(fold_advance, running, (weight_groups, row_groups, slot_groups))
            return carried

        transpose_start_sum = jnp.zeros((slot_total, quarter, hidden), jnp.float32)
        partial_value = fold_rows(
            transpose_start_sum, lax.all_gather(rounded, "edge", axis=1, tiled=True)
        )
        summed = jnp.einsum(
            "sj,sch->jch",
            request_float,
            lax.all_to_all(partial_value, "node", split_axis=0, concat_axis=0, tiled=True),
            precision=lax.Precision.HIGHEST,
        )
        adjoint = 0.9 * summed.reshape(row_count, hidden)
        factor = 0.1 if step_index + 1 < STEPS else 1.0
        gradient = gradient + factor * adjoint
    return (current, gradient)


def per_device(teleport, cotangent, fetch_table, block_row, block_slot, values):
    arguments = (teleport, cotangent, fetch_table, block_row, block_slot, values)
    row_count = teleport.shape[0]
    dense_bytes = fetch_table.shape[1] * row_count * values.shape[3] * 2
    if dense_bytes <= DENSE_BYTES:
        return per_device_dense(*arguments)
    return per_device_blocks(*arguments)


def solution(mesh):
    placed = (
        P(("node", "edge"), None),
        P(("node", "edge"), None),
        P(),
        P("node", None),
        P("node", None),
        P("node", None, "edge", None),
    )
    return jax.shard_map(
        per_device,
        mesh=mesh,
        in_specs=placed,
        out_specs=(P(("node", "edge"), None), P(("node", "edge"), None)),
        check_vma=False,
    )
```

```python
import functools

import jax
import jax.numpy as jnp
from jax import lax
from jax.experimental import pallas as pl
from jax.experimental.pallas import tpu as pltpu
from jax.sharding import PartitionSpec as P

CAP = 2
STEPS = 2
DENSE_BYTES = 8 * 2**20
START_MEBIBYTES = 60
BUILD_MEBIBYTES = 40
IDS_ROOM = 24576
LOW = jnp.bfloat16
FULL = jnp.float32

VMEM = pl.BlockSpec(memory_space=pltpu.VMEM)
SMEM = pl.BlockSpec(memory_space=pltpu.SMEM)
HBM = pl.BlockSpec(memory_space=pltpu.HBM)


def params(mebibytes):
    return pltpu.CompilerParams(vmem_limit_bytes=mebibytes * 2**20)


def partner(axis, turn):
    return lax.axis_index(axis) ^ turn


def requested(table, turn, slot):
    column = lax.axis_index("node") * CAP + slot
    return jnp.maximum(table[partner("node", turn), column], 0)


def fill(sends, block):
    for low, send in enumerate(sends):
        for turn in range(send.shape[0]):
            for slot in range(CAP):
                send[turn, slot] = block(2 * turn + low, slot).astype(send.dtype)


def start_kernel(table, teleport, cotangent, rows, slots, *refs):
    *sends, rounded, ids, plan, state, adjoint, sems = refs
    copies = [
        pltpu.make_async_copy(source, target, sems.at[index])
        for index, (source, target) in enumerate(
            (
                (table, plan),
                (teleport, state),
                (cotangent, adjoint),
                (rows, ids.at[0]),
                (slots, ids.at[1]),
            )
        )
    ]
    for copy in copies:
        copy.start()
    copies[0].wait()
    copies[1].wait()
    fill(sends, lambda turn, slot: state[requested(plan, turn, slot)])
    copies[2].wait()
    rounded[...] = adjoint[...].astype(LOW)
    copies[3].wait()
    copies[4].wait()


def place_of(turn, owners):
    return (turn & 1) * (owners // 2) + (turn >> 1)


def build_kernel(ids, weights, high, low, held, total, own_ids, places, sems):
    parts = sems.shape[0] - 1
    block_count, quarter, width = held.shape
    chunk = block_count // parts
    owners = total.shape[0] // CAP
    copies = [
        pltpu.make_async_copy(
            weights.at[0, pl.ds(part * chunk, chunk)],
            held.at[pl.ds(part * chunk, chunk)],
            sems.at[part],
        )
        for part in range(parts)
    ]
    ids_copy = pltpu.make_async_copy(ids.at[pl.ds(0, 2)], own_ids, sems.at[parts])
    ids_copy.start()
    for copy in copies:
        copy.start()
    for slot in range(total.shape[0]):
        places[slot] = place_of(partner("node", slot // CAP), owners) * CAP + slot % CAP
    total[...] = jnp.zeros_like(total)
    ids_copy.wait()
    for part, copy in enumerate(copies):
        copy.wait()
        for block in range(part * chunk, (part + 1) * chunk):
            total[places[own_ids[1, 0, block]], own_ids[0, 0, block]] += held[block].astype(FULL)
    for slot in range(total.shape[0]):
        for row in range(total.shape[1]):
            place = (pl.ds(slot * quarter, quarter), pl.ds(row * width, width))
            value = total[slot, row]
            rounded = value.astype(LOW)
            high[place] = rounded
            low[place] = (value - rounded.astype(FULL)).astype(LOW)


def far_first(pairs):
    return zip(range(len(pairs), 0, -1), pairs)


def pair_kernel(kept, got, *pairs):
    for turn, pair in far_first(pairs):
        pair[0] = kept[turn]
        pair[1] = got[turn]


def by_turn(parts):
    kept, got, *pairs = parts
    yield 0, kept.at[0]
    yield 1, got.at[0]
    for turn, pair in far_first(pairs):
        yield 2 * turn, pair.at[0]
        yield 2 * turn + 1, pair.at[1]


def forward_kernel(operators, *refs):
    dense = refs[:operators]
    parts = refs[operators : operators + 1 + refs[operators].shape[0]]
    *partials, source, product = refs[operators + len(parts) :]
    quarters, quarter, hidden = product.shape
    width = quarters * quarter
    for turn, part in by_turn(parts):
        source[place_of(turn, source.shape[0])] = part[...]
    vectors = source[...].reshape(-1, hidden)
    for row in range(partials[0].shape[0]):
        summed = sum(
            lax.dot_general(
                vectors,
                part[:, row * width : (row + 1) * width],
                (((0,), (0,)), ((), ())),
                preferred_element_type=FULL,
            )
            for part in dense
        )
        product[...] = summed.T.reshape(product.shape)
        for turn, partial in zip((0, 1, *range(quarters - 1, 1, -1)), partials):
            partial[row] = product[partner("edge", turn)].astype(partial.dtype)


def adjoint_kernel(operators, low, *refs):
    *arrived, send, source = refs[operators:]
    for turn, part in enumerate(arrived):
        source[:, partner("edge", turn)] = part[...]
    vectors = source[...].reshape(-1, source.shape[-1])
    half = refs[0].shape[0] // 2
    product = sum(
        jnp.dot(part[low * half : (low + 1) * half], vectors, preferred_element_type=FULL)
        for part in refs[:operators]
    )
    send[...] = product.reshape(send.shape).astype(LOW)


def state_of(arrived, teleport):
    summed = arrived[0][...]
    for part in arrived[1:]:
        summed += part[...].astype(FULL)
    return 0.9 * summed + 0.1 * teleport[...]


def next_state_kernel(table, teleport, *refs):
    *arrived, kept, away, state = refs
    state[...] = state_of(arrived, teleport)
    fill((kept, away), lambda turn, slot: state[requested(table, turn, slot)])


def last_state_kernel(teleport, *refs):
    *arrived, state = refs
    state[...] = state_of(arrived, teleport)


def gather_adjoint(table, parts, summed):
    summed[...] = jnp.zeros_like(summed)
    for turn, part in by_turn(parts):
        for slot in range(CAP):
            summed[requested(table, turn, slot)] += part[slot].astype(FULL)


def next_adjoint_kernel(table, cotangent, *refs):
    *parts, gradient, rounded, summed = refs
    gather_adjoint(table, parts, summed)
    adjoint = 0.9 * summed[...]
    gradient[...] = 0.1 * cotangent[...] + 0.1 * adjoint
    rounded[...] = adjoint.astype(LOW)


def last_adjoint_kernel(table, gradient_in, *refs):
    *parts, gradient, summed = refs
    gather_adjoint(table, parts, summed)
    gradient[...] = gradient_in[...] + 0.9 * summed[...]


def per_device_dense(teleport, cotangent, fetch_table, block_row, block_slot, values):
    row_count, hidden = teleport.shape
    _, block_count, quarter, width = values.shape
    count = row_count // quarter
    quarters = lax.axis_size("edge")
    slot_total = fetch_table.shape[1]
    owners = lax.axis_size("node")
    shape = (count, quarter, hidden)
    half_shape = (owners // 2, CAP, quarter, hidden)
    pair_shape = (2, CAP, quarter, hidden)
    teleport = teleport.reshape(shape)
    cotangent = cotangent.reshape(shape)

    def call(kernel, operands, places, outs, scratch, mebibytes=8, cost=None, places_out=None):
        return pl.pallas_call(
            kernel,
            out_shape=[jax.ShapeDtypeStruct(*out) for out in outs],
            in_specs=places,
            out_specs=places_out or [VMEM] * len(outs),
            scratch_shapes=scratch,
            compiler_params=params(mebibytes),
            cost_estimate=cost,
        )(*operands)

    def after(arrays, others):
        return lax.optimization_barrier((tuple(arrays), tuple(others)))[0]

    def to_node(array, turn):
        return lax.ppermute(array, "node", [(place, place ^ turn) for place in range(owners)])

    def over_node(kept, got):
        pairs = call(
            pair_kernel,
            (kept, got),
            [VMEM] * 2,
            [(pair_shape, LOW)] * (owners // 2 - 1),
            [],
        )
        return (kept, got, *(to_node(pair, 2 * turn) for turn, pair in far_first(pairs)))

    def over_edge(arrays, turns):
        return [arrays[0]] + [
            lax.ppermute(array, "edge", [(place, place ^ turn) for place in range(quarters)])
            for turn, array in zip(turns, arrays[1:])
        ]

    kept, away, rounded, ids = call(
        start_kernel,
        (fetch_table, teleport, cotangent, block_row, block_slot),
        [HBM] * 5,
        [(half_shape, LOW)] * 2
        + [(shape, LOW), ((IDS_ROOM, *block_row.shape), block_row.dtype)],
        [
            pltpu.SMEM(fetch_table.shape, fetch_table.dtype),
            pltpu.VMEM(shape, FULL),
            pltpu.VMEM(shape, FULL),
            pltpu.SemaphoreType.DMA((5,)),
        ],
        START_MEBIBYTES,
        places_out=[VMEM] * 3 + [HBM],
    )
    dense_shape = (slot_total * quarter, count * width)
    parts = next(size for size in (6, 4, 2, 1) if block_count % size == 0)
    high, low = call(
        build_kernel,
        (ids, values),
        [HBM] * 2,
        [(dense_shape, LOW)] * 2,
        [
            pltpu.VMEM((block_count, quarter, width), LOW),
            pltpu.VMEM((slot_total, count, quarter, width), FULL),
            pltpu.SMEM((2, *block_row.shape), block_row.dtype),
            pltpu.SMEM((slot_total,), block_row.dtype),
            pltpu.SemaphoreType.DMA((parts + 1,)),
        ],
        BUILD_MEBIBYTES,
        pl.CostEstimate(flops=0, bytes_accessed=values.size * 2, transcendentals=0),
    )

    gradient = cotangent
    for step in range(STEPS):
        last = step + 1 == STEPS
        dense = (high,) if last else (high, low)
        cells = len(dense) * high.size
        half_cost, cost = (
            pl.CostEstimate(
                flops=2 * part * hidden, bytes_accessed=2 * part, transcendentals=0
            )
            for part in (cells // 2, cells)
        )
        arrived = over_edge([rounded] * quarters, range(1, quarters))
        got = to_node(away, 1)
        (got,) = after((got,), (rounded, high) if step else (high,))
        columns = over_node(kept, got)
        def adjoint_half(low, rows):
            return call(
                functools.partial(adjoint_kernel, len(dense), low),
                (*dense, *rows),
                [VMEM] * (quarters + len(dense)),
                [(half_shape, LOW)],
                [pltpu.VMEM((count, quarters, quarter, hidden), LOW)],
                cost=half_cost,
            )[0]

        away_sums = adjoint_half(1, arrived)
        kept_sums = adjoint_half(0, after(arrived, (away_sums,)))
        got_sums = to_node(away_sums, 1)
        columns = after(columns, (kept_sums,))
        partials = call(
            functools.partial(forward_kernel, len(dense)),
            (*dense, *columns),
            [VMEM] * (len(columns) + len(dense)),
            [(shape, FULL)] + [(shape, LOW)] * (quarters - 1),
            [
                pltpu.VMEM((owners, CAP, quarter, hidden), LOW),
                pltpu.VMEM((quarters, quarter, hidden), FULL),
            ],
            cost=cost,
        )
        (got_sums,) = after((got_sums,), partials[1:])
        transposed = over_node(kept_sums, got_sums)
        partials = over_edge(partials, (1, *range(quarters - 1, 1, -1)))
        total = [pltpu.VMEM(shape, FULL)]
        if not last:
            kept, away = call(
                next_state_kernel,
                (fetch_table, teleport, *partials),
                [SMEM] + [VMEM] * (1 + quarters),
                [(half_shape, LOW)] * 2,
                total,
            )
            transposed = after(transposed, (away,))
            gradient, rounded = call(
                next_adjoint_kernel,
                (fetch_table, gradient, *transposed),
                [SMEM] + [VMEM] * (1 + len(transposed)),
                [(shape, FULL), (shape, LOW)],
                total,
            )
        else:
            (state,) = call(
                last_state_kernel,
                (teleport, *partials),
                [VMEM] * (1 + quarters),
                [(shape, FULL)],
                [],
            )
            transposed = after(transposed, (state,))
            (gradient,) = call(
                last_adjoint_kernel,
                (fetch_table, gradient, *transposed),
                [SMEM] + [VMEM] * (1 + len(transposed)),
                [(shape, FULL)],
                total,
            )
    return state.reshape(row_count, hidden), gradient.reshape(row_count, hidden)


def per_device_blocks(teleport, cotangent, fetch_table, block_row, block_slot, values):
    row_count, hidden = teleport.shape
    quarter = values.shape[2]
    block_count = values.shape[1]
    blocks_dev = row_count // quarter
    slot_total = fetch_table.shape[1]
    owner_count = lax.axis_size("node")
    group_size = 16
    turn_count = block_count // group_size
    owner_index = lax.axis_index("node")
    local_weights = values[0]
    row_ids = block_row[0]
    slot_ids = block_slot[0]
    own_plan = lax.dynamic_index_in_dim(fetch_table, owner_index, 0, keepdims=False)
    local_ids = jnp.take(own_plan, slot_ids, axis=0)
    global_ids = slot_ids // CAP * blocks_dev + local_ids
    requests = lax.dynamic_slice_in_dim(fetch_table, owner_index * CAP, CAP, 1).reshape(slot_total)
    block_range = jnp.arange(blocks_dev, dtype=jnp.int32)
    request_hot = requests[:, None] == block_range[None, :]
    request_float = request_hot.astype(jnp.float32)
    weight_groups = local_weights.reshape(turn_count, group_size, quarter, local_weights.shape[2])
    row_groups = row_ids.reshape(turn_count, group_size)
    slot_groups = slot_ids.reshape(turn_count, group_size)
    current = teleport
    for step_index in range(STEPS):
        propagate_rounded = current.astype(jnp.bfloat16)
        everything = lax.all_gather(propagate_rounded, "node", axis=0, tiled=True)
        feature_table = everything.reshape(owner_count * blocks_dev, quarter, hidden)
        columns = jnp.take(feature_table, global_ids, axis=0)
        column_groups = columns.reshape(turn_count, group_size, quarter, hidden)

        def partial_rows(amount):
            quarters_used = amount // row_count

            def partial_advance(running, inputs):
                weights, sources, targets = inputs
                product = jnp.einsum(
                    "bcr,bch->brh", weights, sources, preferred_element_type=jnp.float32
                )
                product = product.reshape(group_size, quarters_used, quarter, hidden)
                return (running.at[targets].add(product), None)

            start_sum = jnp.zeros((blocks_dev, quarters_used, quarter, hidden), jnp.float32)
            running, _ = lax.scan(
                partial_advance, start_sum, (weight_groups, column_groups, row_groups)
            )
            return running.transpose(1, 0, 2, 3).reshape(amount, hidden)

        current = (
            0.9
            * lax.psum_scatter(
                partial_rows(lax.axis_size("edge") * row_count),
                "edge",
                scatter_dimension=0,
                tiled=True,
            )
            + 0.1 * teleport
        )
    adjoint = cotangent
    gradient = 0.1 * cotangent
    for step_index in range(STEPS):
        rounded = adjoint.astype(jnp.bfloat16).reshape(blocks_dev, quarter, hidden)

        def fold_rows(running, arrived_rows):

            def fold_advance(carried, inputs):
                weights, targets, slot_targets = inputs
                sources = jnp.take(arrived_rows, targets, axis=0)
                product = jnp.einsum(
                    "bcr,brh->bch", weights, sources, preferred_element_type=jnp.float32
                )
                return (carried.at[slot_targets].add(product), None)

            carried, _ = lax.scan(fold_advance, running, (weight_groups, row_groups, slot_groups))
            return carried

        transpose_start_sum = jnp.zeros((slot_total, quarter, hidden), jnp.float32)
        partial_value = fold_rows(
            transpose_start_sum, lax.all_gather(rounded, "edge", axis=1, tiled=True)
        )
        summed = jnp.einsum(
            "sj,sch->jch",
            request_float,
            lax.all_to_all(partial_value, "node", split_axis=0, concat_axis=0, tiled=True),
            precision=lax.Precision.HIGHEST,
        )
        adjoint = 0.9 * summed.reshape(row_count, hidden)
        factor = 0.1 if step_index + 1 < STEPS else 1.0
        gradient = gradient + factor * adjoint
    return (current, gradient)


def per_device(teleport, cotangent, fetch_table, block_row, block_slot, values):
    arguments = (teleport, cotangent, fetch_table, block_row, block_slot, values)
    row_count = teleport.shape[0]
    dense_bytes = fetch_table.shape[1] * row_count * values.shape[3] * 2
    if dense_bytes <= DENSE_BYTES:
        return per_device_dense(*arguments)
    return per_device_blocks(*arguments)


def solution(mesh):
    placed = (
        P(("node", "edge"), None),
        P(("node", "edge"), None),
        P(),
        P("node", None),
        P("node", None),
        P("node", None, "edge", None),
    )
    return jax.shard_map(
        per_device,
        mesh=mesh,
        in_specs=placed,
        out_specs=(P(("node", "edge"), None), P(("node", "edge"), None)),
        check_vma=False,
    )
```
